32 devices in a mesh: dp: 16 (over z, y, x), seq: 2 (over core).
Axes of the slice: x: 2, y: 2, z: 4, core: 2. Of those that a mesh axis runs over, the one named last changes fastest.
Arguments:
- tokens: bfloat16 [16, 2048, 768], P('dp', 'seq'), may hold values from -6 to 6
- lengths: int32 [16, 16], P('dp'), may hold values from 1 to 512, as said below
- partners: int32 [256], replicated, may hold values from 0 to 255, as said below
- query_proj: bfloat16 [768, 768], replicated, may hold values from -0.21875 to 0.21875
- query_bias: float32 [768], replicated, may hold values from -1.25 to 1.25
- key_proj: bfloat16 [768, 768], replicated, may hold values from -0.21875 to 0.21875
- value_proj: bfloat16 [768, 768], replicated, may hold values from -0.21875 to 0.21875
- value_bias: float32 [768], replicated, may hold values from -1.25 to 1.25
- output_proj: bfloat16 [768, 768], replicated, may hold values from -0.875 to 0.875
- output_bias: float32 [768], replicated, may hold values from -1.25 to 1.25
- first_gain: float32 [768], replicated, may hold values from 0.5 to 1.5
- first_shift: float32 [768], replicated, may hold values from -0.3125 to 0.3125
- expand_proj: bfloat16 [768, 3072], replicated, may hold values from -0.21875 to 0.21875
- expand_bias: float32 [3072], replicated, may hold values from -1.25 to 1.25
- shrink_proj: bfloat16 [3072, 768], replicated, may hold values from -0.21875 to 0.21875
- shrink_bias: float32 [768], replicated, may hold values from -1.25 to 1.25
- second_gain: float32 [768], replicated, may hold values from 0.5 to 1.5
- second_shift: float32 [768], replicated, may hold values from -0.3125 to 0.3125
Outputs:
- passage_loss: float32 [256], P('dp')
- tokens_grad: float32 [16, 2048, 768], P('dp', 'seq')
- query_proj_grad: float32 [768, 768], replicated
- query_bias_grad: float32 [768], replicated
- key_proj_grad: float32 [768, 768], replicated
- value_projection_gradient: float32 [768, 768], replicated
- value_bias_gradient: float32 [768], replicated
- output_proj_grad: float32 [768, 768], replicated
- output_bias_grad: float32 [768], replicated
- first_gain_grad: float32 [768], replicated
- first_shift_grad: float32 [768], replicated
- expand_proj_grad: float32 [768, 3072], replicated
- expand_bias_grad: float32 [3072], replicated
- shrink_proj_grad: float32 [3072, 768], replicated
- shrink_bias_grad: float32 [768], replicated
- second_gain_grad: float32 [768], replicated
- second_shift_grad: float32 [768], replicated
The draws below stay inside these ranges and needn't reach their ends.
Inputs may be any that keep to these rules, and one draw needn't show every extreme that they name: `lengths`: in every row exactly one passage has 512 positions and it holds positions 1023 and 1024 of the row; the passages of a row together take at most 2048 positions. `partners`: never the passage itself.
All inputs are finite; a program needn't handle non-finite values.
Results may differ from the reference program's by a relative error of at most 0.015.
Values may be sent and summed in bfloat16 or wider, within the bound.
No kernel may reach another device: no remote copies, remote signals or barrier semaphores. Data moves between devices by JAX's collectives and lax.ppermute only.
A program may use at most 192 MiB of HBM per device.

```python
import jax
import jax.numpy as jnp
from jax import lax

MODEL_WIDTH = 768
HEADS = 12
FF = 3072
TOK_DEV = 1024
PASS = 16
ROW_POSITIONS = 2048
PACKED_ROWS = 16
PASSAGES = 256


def draw_lengths(key, part):
    key = jax.random.fold_in(key, 11)
    others = PASS - 1
    longest_length = TOK_DEV // 2
    budget = TOK_DEV + TOK_DEV // 2 - PASS + 1
    expon = jax.random.randint(key, (PACKED_ROWS, others), 0, 3)
    weights_int = jnp.left_shift(jnp.ones((PACKED_ROWS, others), jnp.int32), expon.astype(jnp.int32))
    weight_total = jnp.sum(weights_int, 1, keepdims=True)
    pieces = 1 + budget * weights_int // weight_total
    pieces = jnp.minimum(pieces, longest_length - 1).astype(jnp.int32)
    ends = jnp.cumsum(pieces, 1).astype(jnp.int32)
    place = jnp.sum((ends <= TOK_DEV - 1).astype(jnp.int32), 1, keepdims=True)
    index = jnp.arange(PASS, dtype=jnp.int32)[None, :] + jnp.zeros((PACKED_ROWS, 1), jnp.int32)
    before = jnp.take_along_axis(pieces, jnp.clip(index, 0, others - 1), 1)
    after = jnp.take_along_axis(pieces, jnp.clip(index - 1, 0, others - 1), 1)
    result = jnp.where(index < place, before, jnp.where(index == place, longest_length, after))
    return result.astype(jnp.int32)


def draw_partners(key, part):
    key = jax.random.fold_in(key, 23)
    offsets = jax.random.randint(key, (PASSAGES,), 1, PASSAGES)
    return ((jnp.arange(PASSAGES, dtype=jnp.int32) + offsets) % PASSAGES).astype(jnp.int32)


def block_levels(key, dims, cuts, smallest, top_value):
    factor_of, own = 1.0, jax.random.fold_in(key, 6)
    for position, shards_of in cuts:
        heights = jnp.exp(jax.random.uniform(jax.random.fold_in(own, position), (shards_of,), jnp.float32, smallest / len(cuts), top_value / len(cuts)))
        factor_of = factor_of * jnp.repeat(heights, dims[position] // shards_of).reshape([-1 if axis == position else 1 for axis in range(len(dims))])
    return factor_of


def normal_values(rng, shape, width, limit, cuts=(), held_as=jnp.bfloat16):
    values = width * jax.random.normal(rng, shape, jnp.float32)
    if cuts:
        values = values * block_levels(rng, shape, cuts, -0.22, 0.18)
    return jnp.clip(values, -limit, limit).astype(held_as)


def setup_inputs(seed: int = 0) -> dict:
    seeds = jax.random.split(jax.random.key(seed), 19)
    return {
        "tokens": normal_values(seeds[0], (PACKED_ROWS, ROW_POSITIONS, MODEL_WIDTH), 1.0, 6.0, ((0, 16), (1, 2))),
        "lengths": draw_lengths(jax.random.fold_in(seeds[18], 71), 0),
        "partners": draw_partners(jax.random.fold_in(seeds[18], 71), 0),
        "query_proj": normal_values(seeds[3], (MODEL_WIDTH, MODEL_WIDTH), MODEL_WIDTH ** -0.5, 0.21875),
        "query_bias": normal_values(seeds[4], (MODEL_WIDTH,), 0.2, 1.25, (), jnp.float32),
        "key_proj": normal_values(seeds[5], (MODEL_WIDTH, MODEL_WIDTH), MODEL_WIDTH ** -0.5, 0.21875),
        "value_proj": normal_values(seeds[6], (MODEL_WIDTH, MODEL_WIDTH), MODEL_WIDTH ** -0.5, 0.21875),
        "value_bias": normal_values(seeds[7], (MODEL_WIDTH,), 0.2, 1.25, (), jnp.float32),
        "output_proj": normal_values(seeds[8], (MODEL_WIDTH, MODEL_WIDTH), (MODEL_WIDTH // 16) ** -0.5, 0.875),
        "output_bias": normal_values(seeds[9], (MODEL_WIDTH,), 0.2, 1.25, (), jnp.float32),
        "first_gain": jnp.clip(1.0 + 0.1 * jax.random.normal(seeds[10], (MODEL_WIDTH,), jnp.float32), 0.5, 1.5),
        "first_shift": normal_values(seeds[11], (MODEL_WIDTH,), 0.05, 0.3125, (), jnp.float32),
        "expand_proj": normal_values(seeds[12], (MODEL_WIDTH, FF), MODEL_WIDTH ** -0.5, 0.21875),
        "expand_bias": normal_values(seeds[13], (FF,), 0.2, 1.25, (), jnp.float32),
        "shrink_proj": normal_values(seeds[14], (FF, MODEL_WIDTH), (FF // 4) ** -0.5, 0.21875),
        "shrink_bias": normal_values(seeds[15], (MODEL_WIDTH,), 0.2, 1.25, (), jnp.float32),
        "second_gain": jnp.clip(1.0 + 0.1 * jax.random.normal(seeds[16], (MODEL_WIDTH,), jnp.float32), 0.5, 1.5),
        "second_shift": normal_values(seeds[17], (MODEL_WIDTH,), 0.05, 0.3125, (), jnp.float32),
    }


@jax.custom_vjp
def low(v):
    return lax.optimization_barrier(v.astype(jnp.bfloat16)).astype(jnp.float32)

@jax.custom_vjp
def low_back(v):
    return v

def low_keep(v):
    return (low(v), None)

def low_pass(kept, grad):
    return (grad,)

def back_keep(v):
    return (v, None)

def back_low(kept, grad):
    return (low(grad),)
low.defvjp(low_keep, low_pass)
low_back.defvjp(back_keep, back_low)
EPS_NORM = 1e-12
BIG_NEG = -1000000000.0
HIGH = lax.Precision.HIGHEST

def rounded(value):
    return low(low_back(value))

def matmul_high(left, right):
    return jnp.dot(left, right, precision=HIGH)

def layer_norm(resid, gain, shift):
    center = resid - lax.optimization_barrier(jnp.mean(resid, -1, keepdims=True))
    spread = lax.optimization_barrier(jnp.mean(center * center, -1, keepdims=True))
    return center * lax.rsqrt(spread + EPS_NORM) * gain + shift

def normalize_rows(pooled):
    return pooled * lax.rsqrt(lax.optimization_barrier(jnp.sum(pooled * pooled, -1, keepdims=True)) + 1e-06)

def segment_ids(counts, length):
    ends = jnp.cumsum(counts).astype(jnp.int32)
    positions = jnp.arange(length, dtype=jnp.int32)
    return lax.optimization_barrier(jnp.sum((positions[:, None] >= ends[None, :]).astype(jnp.int32), -1)).astype(jnp.int32)

def block_row(weights, row_data, counts):
    query_proj, query_bias, key_proj, value_proj, value_bias, output_proj, output_bias, first_gain, first_shift, expand_proj, expand_bias, shrink_proj, shrink_bias, second_gain, second_shift = weights
    length, features = row_data.shape
    head_size = features // HEADS
    segment = segment_ids(counts, length)
    queries = rounded(matmul_high(row_data, query_proj) + query_bias).reshape(length, HEADS, head_size)
    key_rows = rounded(matmul_high(row_data, key_proj)).reshape(length, HEADS, head_size)
    value_rows = rounded(matmul_high(row_data, value_proj) + value_bias).reshape(length, HEADS, head_size)
    scores = low_back(jnp.einsum('qhe,khe->hqk', queries, key_rows, precision=HIGH) * 0.125)
    same = segment[:, None] == segment[None, :]
    scores = jnp.where(same[None, :, :], scores, BIG_NEG)
    probs = low(jax.nn.softmax(scores, -1))
    context = rounded(jnp.einsum('hqk,khe->qhe', probs, value_rows, precision=HIGH)).reshape(length, features)
    attended = low_back(matmul_high(context, output_proj) + output_bias)
    hidden = layer_norm(row_data + attended, first_gain, first_shift)
    expanded = low_back(matmul_high(low(hidden), expand_proj) + expand_bias)
    active = low(jax.nn.gelu(expanded, approximate=False))
    shrunk = low_back(matmul_high(active, shrink_proj) + shrink_bias)
    outputs = layer_norm(hidden + shrunk, second_gain, second_shift)
    members = (jnp.arange(PASS, dtype=jnp.int32)[:, None] == segment[None, :]).astype(jnp.float32)
    return matmul_high(members, outputs) / counts[:, None].astype(jnp.float32)

def reference(tokens, lengths, partners, query_proj, query_bias, key_proj, value_proj, value_bias, output_proj, output_bias, first_gain, first_shift, expand_proj, expand_bias, shrink_proj, shrink_bias, second_gain, second_shift):
    weights = (query_proj.astype(jnp.float32), query_bias.astype(jnp.float32), key_proj.astype(jnp.float32), value_proj.astype(jnp.float32), value_bias.astype(jnp.float32), output_proj.astype(jnp.float32), output_bias.astype(jnp.float32), first_gain.astype(jnp.float32), first_shift.astype(jnp.float32), expand_proj.astype(jnp.float32), expand_bias.astype(jnp.float32), shrink_proj.astype(jnp.float32), shrink_bias.astype(jnp.float32), second_gain.astype(jnp.float32), second_shift.astype(jnp.float32))
    row_data = tokens.astype(jnp.float32)

    def forward(row_data, weights):
        row_fn = jax.checkpoint(lambda packed: block_row(weights, packed[0], packed[1]))
        pooled = lax.map(row_fn, (row_data, lengths)).reshape(PASSAGES, row_data.shape[-1])
        unit_vec = low(normalize_rows(pooled))
        scores = matmul_high(unit_vec, unit_vec.T) * 100.0
        row_index = jnp.arange(PASSAGES, dtype=jnp.int32)
        scores = jnp.where(row_index[:, None] == row_index[None, :], BIG_NEG, scores)
        picked = lax.optimization_barrier(jnp.sum(jnp.where(row_index[None, :] == partners[:, None], scores, 0.0), -1))
        return jax.scipy.special.logsumexp(scores, -1) - picked
    passage_loss, pullback = jax.vjp(forward, row_data, weights)
    grad_rows, grads = pullback(jnp.ones_like(passage_loss))
    return (passage_loss, grad_rows, grads[0], grads[1], grads[2], grads[3], grads[4], grads[5], grads[6], grads[7], grads[8], grads[9], grads[10], grads[11], grads[12], grads[13], grads[14])
```

```python
import functools
import math

import jax
import jax.numpy as jnp
from jax import lax
from jax.experimental import pallas as pl
from jax.experimental.pallas import tpu as pltpu
from jax.sharding import PartitionSpec as P

HEADS = 12
EPS_NORM = 1e-12
BIG_NEG = -1000000000.0
HIGH = lax.Precision.HIGHEST
BF = jnp.bfloat16
F32 = jnp.float32
TILE = 128
MASKED = -float(2**30)
VMEM_MIB = 1 << 20


def dot(left, right, over=((1,), (0,))):
    return lax.dot_general(left, right, (over, ((), ())), preferred_element_type=F32)


def split3(value):
    high = value.astype(BF)
    rest = value - high.astype(F32)
    middle = rest.astype(BF)
    low = (rest - middle.astype(F32)).astype(BF)
    return high, middle, low


def lane_masks():
    lane = lax.broadcasted_iota(jnp.int32, (1, 2 * TILE), 1) % TILE
    even = jnp.where(lane < TILE // 2, 1.0, 0.0).astype(BF)
    odd = jnp.where(lane < TILE // 2, 0.0, 1.0).astype(BF)
    return even, odd


def stack_heads(pair, even, odd):
    return jnp.concatenate([pair * even, pair * odd], 0)


def row_scalar_lanes(value):
    lane = lax.broadcasted_iota(jnp.int32, (1, TILE), 1) % (TILE // 2)
    high = value.astype(BF).astype(F32)
    rest = value - high
    middle = rest.astype(BF).astype(F32)
    low = rest - middle
    return jnp.where(
        lane == 32, high, jnp.where(lane == 33, middle, jnp.where(lane == 34, low, 0.0))
    ).astype(BF)


def attend_kernel(
    lo_ref, hi_ref, q_ref, one_ref, k_ref, v_ref, aux_ref, c_ref, cb_ref, qaux_ref, s_scr, m_scr, o_scr
):
    lo, hi = lo_ref[pl.program_id(0)], hi_ref[pl.program_id(0)]
    pairs = q_ref.shape[1] // TILE
    even, odd = lane_masks()
    m_scr[...] = jnp.full(m_scr.shape, 2.0 * MASKED, F32)
    o_scr[...] = jnp.zeros(o_scr.shape, F32)
    ones_even = jnp.broadcast_to(even[:, :TILE], (TILE, TILE))
    ones_odd = jnp.broadcast_to(odd[:, :TILE], (TILE, TILE))

    def scores(t, carry):
        rows = pl.ds(pl.multiple_of(t * TILE, TILE), TILE)
        aux = aux_ref[rows, :]
        for j in range(pairs):
            cols = slice(j * TILE, (j + 1) * TILE)
            keys = stack_heads(jnp.concatenate([k_ref[rows, cols], aux], 1), even, odd)
            queries = jnp.concatenate([q_ref[:, cols], one_ref[...]], 1)
            s = dot(queries, keys, ((1,), (1,)))
            s_scr[t - lo, j] = s
            m_scr[j] = jnp.maximum(m_scr[j], s)
        return carry

    lax.fori_loop(lo, hi, scores, 0)
    for j in range(pairs):
        m = m_scr[j]
        top_even = jnp.max(m[:, :TILE], 1, keepdims=True)
        top_odd = jnp.max(m[:, TILE:], 1, keepdims=True)
        m_scr[j] = jnp.concatenate(
            [jnp.broadcast_to(top_even, (TILE, TILE)), jnp.broadcast_to(top_odd, (TILE, TILE))], 1
        )

    def weigh(t, carry):
        rows = pl.ds(pl.multiple_of(t * TILE, TILE), TILE)
        for j in range(pairs):
            cols = slice(j * TILE, (j + 1) * TILE)
            p = jnp.exp(s_scr[t - lo, j] - m_scr[j]).astype(BF)
            v = v_ref[rows, cols]
            values = jnp.concatenate(
                [
                    jnp.concatenate([v * even[:, :TILE], ones_even], 1),
                    jnp.concatenate([v * odd[:, :TILE], ones_odd], 1),
                ],
                0,
            )
            o_scr[j] += dot(p, values)
        return carry

    lax.fori_loop(lo, hi, weigh, 0)
    first = lax.broadcasted_iota(jnp.int32, (1, TILE), 1) < TILE // 2
    for j in range(pairs):
        cols = slice(j * TILE, (j + 1) * TILE)
        total = o_scr[j][:, TILE:]
        c = o_scr[j][:, :TILE] / total
        c_ref[:, cols] = c
        cb_ref[:, cols] = c.astype(BF)
        top = jnp.where(first, m_scr[j][:, :TILE], m_scr[j][:, TILE:])
        qaux_ref[:, cols] = row_scalar_lanes(top + jnp.log(total)) + one_ref[...]


def attend(queries, one_hot, keys, values, aux, lo, hi):
    length, features = queries.shape
    window = keys.shape[0]
    pairs = features // TILE
    row = lambda i, *_: (i, 0)
    whole = lambda i, *_: (0, 0)
    return pl.pallas_call(
        attend_kernel,
        grid_spec=pltpu.PrefetchScalarGridSpec(
            num_scalar_prefetch=2,
            grid=(length // TILE,),
            in_specs=[
                pl.BlockSpec((TILE, features), row),
                pl.BlockSpec((TILE, TILE), row),
                pl.BlockSpec((window, features), whole),
                pl.BlockSpec((window, features), whole),
                pl.BlockSpec((window, TILE), whole),
            ],
            out_specs=[pl.BlockSpec((TILE, features), row)] * 3,
            scratch_shapes=[
                pltpu.VMEM((window // TILE, pairs, TILE, 2 * TILE), F32),
                pltpu.VMEM((pairs, TILE, 2 * TILE), F32),
                pltpu.VMEM((pairs, TILE, 2 * TILE), F32),
            ],
        ),
        out_shape=[
            jax.ShapeDtypeStruct((length, features), F32),
            jax.ShapeDtypeStruct((length, features), BF),
            jax.ShapeDtypeStruct((length, features), BF),
        ],
        compiler_params=pltpu.CompilerParams(vmem_limit_bytes=40 * VMEM_MIB),
        name="attend",
    )(lo, hi, queries, one_hot, keys, values, aux)


def attend_back_kernel(
    lo_ref, hi_ref, q_ref, qaux_ref, dc_ref, c_ref, k_ref, v_ref, aux_ref,
    dq_ref, dk_ref, dv_ref, dqt_scr, daux_scr, dk_scr, dv_scr,
):
    step = pl.program_id(0)
    pairs = q_ref.shape[1] // TILE
    tiles = q_ref.shape[0] // TILE
    even, odd = lane_masks()

    @pl.when(step == 0)
    def _():
        dqt_scr[...] = jnp.zeros(dqt_scr.shape, F32)
        lane = lax.broadcasted_iota(jnp.int32, (TILE, TILE), 0) // (TILE // 2)
        other = lax.broadcasted_iota(jnp.int32, (TILE, TILE), 1) // (TILE // 2)
        same_head = jnp.where(lane == other, 1.0, 0.0).astype(BF)

        def deltas(i, carry):
            rows = pl.ds(pl.multiple_of(i * TILE, TILE), TILE)
            for j in range(pairs):
                cols = slice(j * TILE, (j + 1) * TILE)
                product = dc_ref[rows, cols].astype(F32) * c_ref[rows, cols]
                high, middle, low = split3(product)
                delta = dot(high, same_head) + dot(middle, same_head) + dot(low, same_head)
                daux_scr[rows, cols] = row_scalar_lanes(delta)
            return carry

        lax.fori_loop(0, tiles, deltas, 0)

    dk_scr[...] = jnp.zeros(dk_scr.shape, F32)
    dv_scr[...] = jnp.zeros(dv_scr.shape, F32)

    def tile(i, carry):
        rows = pl.ds(pl.multiple_of(i * TILE, TILE), TILE)
        for j in range(pairs):
            cols = slice(j * TILE, (j + 1) * TILE)
            k = k_ref[:, cols]
            keys = jnp.concatenate([k, aux_ref[...]], 1)
            values = jnp.concatenate([v_ref[:, cols], aux_ref[...]], 1)
            queries = stack_heads(jnp.concatenate([q_ref[rows, cols], qaux_ref[rows, cols]], 1), even, odd)
            grads = stack_heads(jnp.concatenate([dc_ref[rows, cols], daux_scr[rows, cols]], 1), even, odd)
            p = jnp.exp(dot(keys, queries, ((1,), (1,))))
            ds = (p * dot(values, grads, ((1,), (1,)))).astype(BF)
            dv_scr[j] += dot(p.astype(BF), grads[:, :TILE])
            dk_scr[j] += dot(ds, queries[:, :TILE])
            keys_t = jnp.concatenate([(k * even[:, :TILE]).T, (k * odd[:, :TILE]).T], 1)
            dqt_scr[j, :, rows] += dot(keys_t, jnp.concatenate([ds[:, :TILE], ds[:, TILE:]], 0))
        return carry

    lax.fori_loop(lo_ref[step], hi_ref[step], tile, 0)
    for j in range(pairs):
        cols = slice(j * TILE, (j + 1) * TILE)
        dk_ref[:, cols] = dk_scr[j].astype(BF)
        dv_ref[:, cols] = dv_scr[j].astype(BF)

    @pl.when(step == pl.num_programs(0) - 1)
    def _():
        for i in range(tiles):
            for j in range(pairs):
                block = dqt_scr[j, :, i * TILE : (i + 1) * TILE] * 0.125
                dq_ref[i * TILE : (i + 1) * TILE, j * TILE : (j + 1) * TILE] = block.T.astype(BF)


def attend_back(queries, qaux, grad_context, context, keys, values, aux, lo, hi):
    length, features = queries.shape
    window = keys.shape[0]
    pairs = features // TILE
    row = lambda i, *_: (i, 0)
    whole = lambda i, *_: (0, 0)
    return pl.pallas_call(
        attend_back_kernel,
        grid_spec=pltpu.PrefetchScalarGridSpec(
            num_scalar_prefetch=2,
            grid=(window // TILE,),
            in_specs=[pl.BlockSpec((length, features), whole)] * 4
            + [
                pl.BlockSpec((TILE, features), row),
                pl.BlockSpec((TILE, features), row),
                pl.BlockSpec((TILE, TILE), row),
            ],
            out_specs=[
                pl.BlockSpec((length, features), whole),
                pl.BlockSpec((TILE, features), row),
                pl.BlockSpec((TILE, features), row),
            ],
            scratch_shapes=[
                pltpu.VMEM((pairs, TILE, length), F32),
                pltpu.VMEM((length, features), BF),
                pltpu.VMEM((pairs, TILE, TILE), F32),
                pltpu.VMEM((pairs, TILE, TILE), F32),
            ],
        ),
        out_shape=[
            jax.ShapeDtypeStruct((length, features), BF),
            jax.ShapeDtypeStruct((window, features), BF),
            jax.ShapeDtypeStruct((window, features), BF),
        ],
        compiler_params=pltpu.CompilerParams(vmem_limit_bytes=40 * VMEM_MIB),
        name="attend_back",
    )(lo, hi, queries, qaux, grad_context, context, keys, values, aux)


def gelu_parts(u):
    size = jnp.abs(u)
    base = 1.0 + (0.3275911 * math.sqrt(0.5)) * size
    t = pl.reciprocal(base, approx=True)
    t = t * (2.0 - base * t)
    bell = jnp.exp(-0.5 * (u * u))
    poly = t * (0.127414796 + t * (-0.142248368 + t * (0.7107068705 + t * (-0.7265760135 + t * 0.5307027145))))
    tail = poly * bell
    below = jnp.where(u < 0.0, tail, 1.0 - tail)
    return u * below, below + u * bell * (1.0 / math.sqrt(2.0 * math.pi))


def normalized(resid):
    center = resid - jnp.mean(resid, -1, keepdims=True)
    scale = lax.rsqrt(jnp.mean(center * center, -1, keepdims=True) + EPS_NORM)
    return center * scale, scale


def feed_kernel(
    cb_ref, x_ref, member_ref, wo_ref, bo_ref, g1_ref, b1_ref, w1_ref, be_ref, w2_ref, bs_ref, g2_ref, b2_ref,
    n1_ref, r1_ref, h_ref, f_ref, gp_ref, n2_ref, r2_ref, pool_ref,
):
    attended = dot(cb_ref[...], wo_ref[...]) + bo_ref[...]
    unit, scale = normalized(x_ref[...].astype(F32) + attended)
    n1_ref[...] = unit.astype(BF)
    r1_ref[...] = scale
    hidden = unit * g1_ref[...] + b1_ref[...]
    low = hidden.astype(BF)
    h_ref[...] = low
    resid = hidden + bs_ref[...]
    chunk = 512
    for start in range(0, w1_ref.shape[1], chunk):
        cols = slice(start, start + chunk)
        u = dot(low, w1_ref[:, cols]) + be_ref[:, cols]
        active, slope = gelu_parts(u)
        active = active.astype(BF)
        f_ref[:, cols] = active
        gp_ref[:, cols] = slope.astype(BF)
        resid = resid + dot(active, w2_ref[cols, :])
    unit, scale = normalized(resid)
    n2_ref[...] = unit.astype(BF)
    r2_ref[...] = scale
    out = unit * g2_ref[...] + b2_ref[...]
    high, middle, _ = split3(out)
    part = dot(member_ref[...], high) + dot(member_ref[...], middle)

    @pl.when(pl.program_id(0) == 0)
    def _():
        pool_ref[...] = part

    @pl.when(pl.program_id(0) > 0)
    def _():
        pool_ref[...] += part


def feed(cb, x, member, wo, bo, g1, b1, w1, be, w2, bs, g2, b2):
    length, features = x.shape
    hidden = w1.shape[1]
    pass_count = member.shape[0]
    rows = 256
    row = lambda i: (i, 0)
    whole = lambda i: (0, 0)
    once = pl.Buffered(1)

    def full(array):
        return pl.BlockSpec(array.shape, whole, pipeline_mode=once)

    return pl.pallas_call(
        feed_kernel,
        grid=(length // rows,),
        in_specs=[
            pl.BlockSpec((rows, features), row),
            pl.BlockSpec((rows, features), row),
            pl.BlockSpec((pass_count, rows), lambda i: (0, i)),
        ]
        + [full(a) for a in (wo, bo, g1, b1, w1, be, w2, bs, g2, b2)],
        out_specs=[
            pl.BlockSpec((rows, features), row),
            pl.BlockSpec((rows, 1), row),
            pl.BlockSpec((rows, features), row),
            pl.BlockSpec((rows, hidden), row),
            pl.BlockSpec((rows, hidden), row),
            pl.BlockSpec((rows, features), row),
            pl.BlockSpec((rows, 1), row),
            pl.BlockSpec((pass_count, features), whole),
        ],
        out_shape=[
            jax.ShapeDtypeStruct((length, features), BF),
            jax.ShapeDtypeStruct((length, 1), F32),
            jax.ShapeDtypeStruct((length, features), BF),
            jax.ShapeDtypeStruct((length, hidden), BF),
            jax.ShapeDtypeStruct((length, hidden), BF),
            jax.ShapeDtypeStruct((length, features), BF),
            jax.ShapeDtypeStruct((length, 1), F32),
            jax.ShapeDtypeStruct((pass_count, features), F32),
        ],
        compiler_params=pltpu.CompilerParams(vmem_limit_bytes=48 * VMEM_MIB),
        name="feed",
    )(cb, x, member, wo, bo, g1, b1, w1, be, w2, bs, g2, b2)


def norm_back(grad, unit, scale, gain):
    wide = grad * gain
    return scale * (
        wide - jnp.mean(wide, -1, keepdims=True) - unit * jnp.mean(wide * unit, -1, keepdims=True)
    )


def add_rows(ref, row, value):
    ref[row : row + 1, :] += jnp.sum(value, 0, keepdims=True)


def start_back_kernel(spread_ref, pooled_ref, n2_ref, r2_ref, g2_ref, dr_ref, dy_ref, sums_ref):
    @pl.when(pl.program_id(0) == 0)
    def _():
        sums_ref[...] = jnp.zeros(sums_ref.shape, F32)

    grad = dot(spread_ref[...], pooled_ref[...])
    unit = n2_ref[...].astype(F32)
    add_rows(sums_ref, 0, grad * unit)
    add_rows(sums_ref, 1, grad)
    dr = norm_back(grad, unit, r2_ref[...], g2_ref[...])
    dr_ref[...] = dr
    dy = dr.astype(BF)
    dy_ref[...] = dy
    add_rows(sums_ref, 2, dy.astype(F32))


def start_back(spread, pooled_parts, n2, r2, g2):
    length, features = n2.shape
    rows = 256
    row = lambda i: (i, 0)
    whole = lambda i: (0, 0)
    return pl.pallas_call(
        start_back_kernel,
        grid=(length // rows,),
        in_specs=[
            pl.BlockSpec((rows, spread.shape[1]), row),
            pl.BlockSpec(pooled_parts.shape, whole),
            pl.BlockSpec((rows, features), row),
            pl.BlockSpec((rows, 1), row),
            pl.BlockSpec((1, features), whole),
        ],
        out_specs=[
            pl.BlockSpec((rows, features), row),
            pl.BlockSpec((rows, features), row),
            pl.BlockSpec((8, features), whole),
        ],
        out_shape=[
            jax.ShapeDtypeStruct((length, features), F32),
            jax.ShapeDtypeStruct((length, features), BF),
            jax.ShapeDtypeStruct((8, features), F32),
        ],
        name="start_back",
    )(spread, pooled_parts, n2, r2, g2)


def feed_back_kernel(
    dr2_ref, dy_ref, gp_ref, n1_ref, r1_ref, w2_ref, w1_ref, wo_ref, g1_ref,
    du_ref, dr1_ref, da_ref, dc_ref, sums_ref, wide_sums_ref,
):
    @pl.when(pl.program_id(0) == 0)
    def _():
        sums_ref[...] = jnp.zeros(sums_ref.shape, F32)
        wide_sums_ref[...] = jnp.zeros(wide_sums_ref.shape, F32)

    dy = dy_ref[...]
    dh = dr2_ref[...]
    chunk = 512
    for start in range(0, w1_ref.shape[1], chunk):
        cols = slice(start, start + chunk)
        slope = gp_ref[:, cols].astype(F32)
        du = (slope * dot(dy, w2_ref[cols, :], ((1,), (1,)))).astype(BF)
        du_ref[:, cols] = du
        wide_sums_ref[0:1, cols] += jnp.sum(du.astype(F32), 0, keepdims=True)
        dh = dh + dot(du, w1_ref[:, cols], ((1,), (1,)))
    unit = n1_ref[...].astype(F32)
    add_rows(sums_ref, 0, dh * unit)
    add_rows(sums_ref, 1, dh)
    dr = norm_back(dh, unit, r1_ref[...], g1_ref[...])
    dr1_ref[...] = dr
    da = dr.astype(BF)
    da_ref[...] = da
    add_rows(sums_ref, 2, da.astype(F32))
    dc_ref[...] = dot(da, wo_ref[...], ((1,), (1,))).astype(BF)


def feed_back(dr2, dy, gp, n1, r1, w2, w1, wo, g1):
    length, features = dy.shape
    hidden = gp.shape[1]
    rows = 256
    row = lambda i: (i, 0)
    whole = lambda i: (0, 0)
    once = pl.Buffered(1)

    def full(array):
        return pl.BlockSpec(array.shape, whole, pipeline_mode=once)

    return pl.pallas_call(
        feed_back_kernel,
        grid=(length // rows,),
        in_specs=[
            pl.BlockSpec((rows, features), row),
            pl.BlockSpec((rows, features), row),
            pl.BlockSpec((rows, hidden), row),
            pl.BlockSpec((rows, features), row),
            pl.BlockSpec((rows, 1), row),
            full(w2),
            full(w1),
            full(wo),
            full(g1),
        ],
        out_specs=[
            pl.BlockSpec((rows, hidden), row),
            pl.BlockSpec((rows, features), row),
            pl.BlockSpec((rows, features), row),
            pl.BlockSpec((rows, features), row),
            pl.BlockSpec((8, features), whole),
            pl.BlockSpec((8, hidden), whole),
        ],
        out_shape=[
            jax.ShapeDtypeStruct((length, hidden), BF),
            jax.ShapeDtypeStruct((length, features), F32),
            jax.ShapeDtypeStruct((length, features), BF),
            jax.ShapeDtypeStruct((length, features), BF),
            jax.ShapeDtypeStruct((8, features), F32),
            jax.ShapeDtypeStruct((8, hidden), F32),
        ],
        compiler_params=pltpu.CompilerParams(vmem_limit_bytes=48 * VMEM_MIB),
        name="feed_back",
    )(dr2, dy, gp, n1, r1, w2, w1, wo, g1)


def swap_seq(array):
    return lax.ppermute(array, "seq", [(0, 1), (1, 0)])


def swap_dp(array, bit):
    count = lax.axis_size("dp")
    return lax.ppermute(array, "dp", [(i, i ^ (1 << bit)) for i in range(count)])


def pick_half(array, axis, which):
    half = array.shape[axis] // 2
    return lax.dynamic_slice_in_dim(array, which * half, half, axis)


def join(mine, other, axis, place):
    return jnp.where(
        place == 0, jnp.concatenate([mine, other], axis), jnp.concatenate([other, mine], axis)
    )


def halving_axis(shape):
    rows, cols = shape
    if rows % 32 == 0:
        return 0
    if cols % 256 == 0:
        return 1
    return 0


def reduce_block(block, order):
    index = lax.axis_index("dp")
    axes = []
    for bit in order:
        place = (index >> bit) & 1
        axis = halving_axis(block.shape)
        axes.append(axis)
        other = swap_dp(pick_half(block, axis, 1 - place), bit)
        block = (pick_half(block, axis, place).astype(F32) + other.astype(F32)).astype(BF)
    for bit, axis in zip(reversed(order), reversed(axes)):
        place = (index >> bit) & 1
        block = join(block, swap_dp(block, bit), axis, place)
    return block


def reduce_all(partial, groups, axis, turn):
    seq = lax.axis_index("seq")
    bits = int(math.log2(lax.axis_size("dp")))
    orders = [list(range(bits)), [1, 0] + list(range(2, bits)), list(range(2, bits)) + [0, 1]]
    other = swap_seq(pick_half(partial, 0, 1 - seq))
    half = (pick_half(partial, 0, seq).astype(F32) + other.astype(F32)).astype(BF)
    pieces = jnp.split(half, groups, axis) if groups > 1 else [half]
    done = [reduce_block(piece, orders[(turn + i) % 3]) for i, piece in enumerate(pieces)]
    half = jnp.concatenate(done, axis) if groups > 1 else done[0]
    return join(half, swap_seq(half), 0, seq).astype(F32)


def sum_small(array):
    array = array + swap_seq(array)
    for bit in range(int(math.log2(lax.axis_size("dp")))):
        array = array + swap_dp(array, bit)
    return array


def body(
    tokens, lengths, partners, query_proj, query_bias, key_proj, value_proj, value_bias, output_proj, output_bias,
    first_gain, first_shift, expand_proj, expand_bias, shrink_proj, shrink_bias, second_gain, second_shift,
):
    _, length, features = tokens.shape
    pass_count = lengths.shape[1]
    seq = lax.axis_index("seq")
    dp = lax.axis_index("dp")
    far = length // 2
    window = length + far
    x = tokens[0]

    x_far = swap_seq(lax.dynamic_slice_in_dim(x, (1 - seq) * far, far, 0))
    x_window = join(x, x_far, 0, seq)

    ends = jnp.cumsum(lengths[0])
    bounds = jnp.concatenate([jnp.zeros(1, jnp.int32), ends, jnp.full(1, 2 * length, jnp.int32)])
    window_start = seq * far
    own_start = seq * length
    positions = window_start + jnp.arange(window, dtype=jnp.int32)
    segment = jnp.sum((positions[:, None] >= ends[None, :]).astype(jnp.int32), -1)
    own_segment = lax.dynamic_slice_in_dim(segment, seq * far, length, 0)
    lane = jnp.arange(TILE, dtype=jnp.int32)
    in_head = lane % (TILE // 2)
    matches = segment[:, None] == in_head[None, :]
    aux = jnp.where(
        in_head[None, :] <= pass_count,
        jnp.where(matches, 0.0, MASKED),
        jnp.where((in_head >= 32) & (in_head < 35), -1.0, 0.0)[None, :],
    ).astype(BF)
    one_hot = (own_segment[:, None] == in_head[None, :]).astype(BF)
    spread = (
        (own_segment[:, None] == lane[None, :] % 32) & (lane < 96)[None, :] & (own_segment < pass_count)[:, None]
    ).astype(BF)
    member = (own_segment[None, :] == jnp.arange(pass_count, dtype=jnp.int32)[:, None]).astype(BF)

    def tile_range(segments, tiles, low, high):
        grouped = segments.reshape(tiles, TILE)
        begin = jnp.clip(bounds[grouped[:, 0]], low, high) - low
        end = jnp.clip(bounds[grouped[:, -1] + 1], low, high) - low
        return begin // TILE, (end + TILE - 1) // TILE

    key_lo, key_hi = tile_range(own_segment, length // TILE, window_start, window_start + window)
    query_lo, query_hi = tile_range(segment, window // TILE, own_start, own_start + length)

    queries = (dot(x, query_proj) + query_bias).astype(BF) * jnp.asarray(0.125, BF)
    keys = dot(x_window, key_proj).astype(BF)
    values = (dot(x_window, value_proj) + value_bias).astype(BF)
    context, context_low, qaux = attend(queries, one_hot, keys, values, aux, key_lo, key_hi)

    wide = lambda vector: vector.reshape(1, -1)
    unit1, scale1, hidden_low, active, slope, unit2, scale2, pooled_part = feed(
        context_low, x, member, output_proj, wide(output_bias), wide(first_gain), wide(first_shift),
        expand_proj, wide(expand_bias), shrink_proj, wide(shrink_bias), wide(second_gain), wide(second_shift),
    )

    lengths_wide = lengths.reshape(pass_count, 1).astype(F32)
    pooled = (pooled_part + swap_seq(pooled_part)) / lengths_wide
    inverse = lax.rsqrt(jnp.sum(pooled * pooled, -1, keepdims=True) + 1e-06)
    every = (pooled * inverse).astype(BF)
    for bit in range(int(math.log2(lax.axis_size("dp")))):
        every = join(every, swap_dp(every, bit), 0, (dp >> bit) & 1)
    count = every.shape[0]
    columns = jnp.arange(count, dtype=jnp.int32)
    scores = dot(every, every, ((1,), (1,))) * 100.0
    scores = jnp.where(columns[:, None] == columns[None, :], BIG_NEG, scores)
    log_sums = jax.scipy.special.logsumexp(scores, -1)
    target = columns[None, :] == partners[:, None]
    picked = jnp.sum(jnp.where(target, scores, 0.0), -1)
    own_first = dp * pass_count
    passage_loss = lax.dynamic_slice_in_dim(log_sums - picked, own_first, pass_count, 0)
    weights = jnp.exp(scores - log_sums[:, None]) - target.astype(F32)
    both = lax.dynamic_slice_in_dim(weights, own_first, pass_count, 0) + lax.dynamic_slice_in_dim(
        weights, own_first, pass_count, 1
    ).T
    grad_unit = 100.0 * jnp.dot(both, every.astype(F32), precision=HIGH)
    grad_pooled = (
        inverse * grad_unit - pooled * (inverse**3 * jnp.sum(pooled * grad_unit, -1, keepdims=True))
    ) / lengths_wide
    gap = jnp.zeros((32 - pass_count, features), BF)
    high, middle, low = split3(grad_pooled)
    pooled_parts = jnp.concatenate([high, gap, middle, gap, low, gap, gap, jnp.zeros((pass_count, features), BF)], 0)

    grad_second, grad_shrunk, sums2 = start_back(spread, pooled_parts, unit2, scale2, wide(second_gain))
    grad_shrink = dot(active, grad_shrunk, ((0,), (0,))).astype(BF)
    grad_expanded, grad_first, grad_attended, grad_context, sums1, wide_sums = feed_back(
        grad_second, grad_shrunk, slope, unit1, scale1, shrink_proj, expand_proj, output_proj, wide(first_gain)
    )
    grad_expand = dot(hidden_low, grad_expanded, ((0,), (0,))).astype(BF)
    grad_output = dot(context_low, grad_attended, ((0,), (0,))).astype(BF)
    grad_query, grad_keys, grad_values = attend_back(
        queries, qaux, grad_context, context, keys, values, aux, query_lo, query_hi
    )

    def gather_far(window_grad):
        own = lax.dynamic_slice_in_dim(window_grad, seq * far, length, 0)
        other = swap_seq(lax.dynamic_slice_in_dim(window_grad, (1 - seq) * length, far, 0))
        nothing = jnp.zeros((far, features), BF)
        return (own.astype(F32) + join(other, nothing, 0, 1 - seq).astype(F32)).astype(BF)

    grad_keys = gather_far(grad_keys)
    grad_values = gather_far(grad_values)
    grad_query_proj = dot(x, grad_query, ((0,), (0,))).astype(BF)
    grad_key_proj = dot(x, grad_keys, ((0,), (0,))).astype(BF)
    grad_value_proj = dot(x, grad_values, ((0,), (0,))).astype(BF)
    tokens_grad = (
        grad_first
        + dot(grad_query, query_proj, ((1,), (1,)))
        + dot(grad_keys, key_proj, ((1,), (1,)))
        + dot(grad_values, value_proj, ((1,), (1,)))
    )[None]

    small = jnp.concatenate(
        [
            sums2[:3],
            sums1[:3],
            jnp.sum(grad_query.astype(F32), 0, keepdims=True),
            jnp.sum(grad_values.astype(F32), 0, keepdims=True),
            wide_sums[:1].reshape(-1, features),
        ],
        0,
    )
    small = sum_small(small)
    shrink_total = reduce_all(grad_shrink, 3, 0, 0)
    expand_total = reduce_all(grad_expand, 3, 1, 0)
    output_total = reduce_all(grad_output, 1, 0, 0)
    query_total = reduce_all(grad_query_proj, 1, 0, 0)
    key_total = reduce_all(grad_key_proj, 1, 0, 1)
    value_total = reduce_all(grad_value_proj, 1, 0, 2)
    return (
        passage_loss,
        tokens_grad,
        query_total,
        small[6],
        key_total,
        value_total,
        small[7],
        output_total,
        small[5],
        small[3],
        small[4],
        expand_total,
        small[8:].reshape(-1),
        shrink_total,
        small[2],
        small[0],
        small[1],
    )


def solution(mesh):
    placed = (P("dp", "seq", None), P("dp", None)) + (P(),) * 16
    return jax.shard_map(
        body,
        mesh=mesh,
        in_specs=placed,
        out_specs=(P("dp"), P("dp", "seq", None)) + (P(),) * 15,
        check_vma=False,
    )
```

```python
import functools
import math

import jax
import jax.numpy as jnp
from jax import lax
from jax.experimental import pallas as pl
from jax.experimental.pallas import tpu as pltpu
from jax.sharding import PartitionSpec as P

HEADS = 12
EPS_NORM = 1e-12
BIG_NEG = -1000000000.0
HIGH = lax.Precision.HIGHEST
BF = jnp.bfloat16
F32 = jnp.float32
TILE = 128
MASKED = -float(2**30)
BIAS_O, GAIN_1, SHIFT_1, BIAS_S, GAIN_2, SHIFT_2, BIAS_Q, BIAS_V, BIAS_E = range(9)
VMEM_MIB = 1 << 20


def dot(left, right, over=((1,), (0,))):
    return lax.dot_general(left, right, (over, ((), ())), preferred_element_type=F32)


def split3(value):
    high = value.astype(BF)
    rest = value - high.astype(F32)
    middle = rest.astype(BF)
    low = (rest - middle.astype(F32)).astype(BF)
    return high, middle, low


def split_lanes(pair):
    row = lax.broadcasted_iota(jnp.int32, (TILE, 1), 0)
    first = jnp.where(row < TILE // 2, 1.0, 0.0).astype(BF)
    second = jnp.where(row < TILE // 2, 0.0, 1.0).astype(BF)
    return jnp.concatenate([pair * first, pair * second], 1)


def split_rows(pair):
    lane = lax.broadcasted_iota(jnp.int32, (1, TILE), 1)
    first = jnp.where(lane < TILE // 2, 1.0, 0.0).astype(BF)
    second = jnp.where(lane < TILE // 2, 0.0, 1.0).astype(BF)
    return jnp.concatenate([pair * first, pair * second], 0)


def lanes_to_rows(both):
    return jnp.concatenate([both[:, :TILE], both[:, TILE:]], 0)


def attend_kernel(
    lo_ref, hi_ref, qt_ref, onet_ref, k_ref, vt_ref, aux_ref, c_ref, ct_ref, ctb_ref, lse_ref, s_scr, q_scr, m_scr, o_scr
):
    lo, hi = lo_ref[pl.program_id(0)], hi_ref[pl.program_id(0)]
    pairs = k_ref.shape[1] // TILE
    m_scr[...] = jnp.full(m_scr.shape, 2.0 * MASKED, F32)
    o_scr[...] = jnp.zeros(o_scr.shape, F32)
    one = onet_ref[...]
    for j in range(pairs):
        q_scr[j, :TILE, :] = split_lanes(qt_ref[j * TILE : (j + 1) * TILE, :])
        q_scr[j, TILE:, :] = jnp.concatenate([one, one], 1)
    extra = o_scr.shape[1] - TILE
    row = lax.broadcasted_iota(jnp.int32, (extra, 2 * TILE), 0)
    lane = lax.broadcasted_iota(jnp.int32, (extra, 2 * TILE), 1)
    ones = jnp.where(row == lane // TILE, 1.0, 0.0).astype(BF)

    count = (hi - lo + 1) // 2
    lo = jnp.minimum(lo, k_ref.shape[0] // TILE - 2 * count)

    def scores(step, carry):
        start = pl.multiple_of((lo + 2 * step) * TILE, TILE)
        for half in range(2):
            rows = pl.ds(pl.multiple_of(start + half * TILE, TILE), TILE)
            aux = aux_ref[rows, :]
            for j in range(pairs):
                keys = jnp.concatenate([k_ref[rows, j * TILE : (j + 1) * TILE], aux], 1)
                s = dot(keys, q_scr[j])
                s_scr[2 * step + half, j] = s
                m_scr[j] = jnp.maximum(m_scr[j], jnp.max(s.reshape(TILE // 8, 8, 2 * TILE), 0))
        return carry

    lax.fori_loop(0, count, scores, 0)
    for j in range(pairs):
        m_scr[j] = jnp.broadcast_to(jnp.max(m_scr[j], 0, keepdims=True), (8, 2 * TILE))

    def weigh(step, carry):
        start = pl.multiple_of((lo + 2 * step) * TILE, TILE)
        for j in range(pairs):
            values, weights = [], []
            for half in range(2):
                cols = pl.ds(pl.multiple_of(start + half * TILE, TILE), TILE)
                p = jnp.exp(s_scr[2 * step + half, j] - m_scr[j, 0:1, :]).astype(BF)
                values.append(
                    jnp.concatenate([split_lanes(vt_ref[j * TILE : (j + 1) * TILE, cols]), ones], 0)
                )
                weights.append(lanes_to_rows(p))
            o_scr[j] += dot(jnp.concatenate(values, 1), jnp.concatenate(weights, 0))
        return carry

    lax.fori_loop(0, count, weigh, 0)
    half = TILE // 2
    for j in range(pairs):
        cols = slice(j * TILE, (j + 1) * TILE)
        total = o_scr[j, TILE : TILE + 2, :]
        inverse = 1.0 / total
        ct = jnp.concatenate(
            [o_scr[j, :half, :] * inverse[0:1], o_scr[j, half:TILE, :] * inverse[1:2]], 0
        )
        ct_ref[cols, :] = ct
        ctb_ref[cols, :] = ct.astype(BF)
        c_ref[:, cols] = ct.T.astype(BF)
        top = jnp.concatenate([m_scr[j, 0:1, :TILE], m_scr[j, 0:1, TILE:]], 0)
        lse_ref[2 * j : 2 * j + 2, :] = top + jnp.log(total)


def attend(queries_t, one_t, keys, values_t, aux, lo, hi):
    features, length = queries_t.shape
    window = keys.shape[0]
    pairs = features // TILE
    row = lambda i, *_: (i, 0)
    col = lambda i, *_: (0, i)
    whole = lambda i, *_: (0, 0)
    return pl.pallas_call(
        attend_kernel,
        grid_spec=pltpu.PrefetchScalarGridSpec(
            num_scalar_prefetch=2,
            grid=(length // TILE,),
            in_specs=[
                pl.BlockSpec((features, TILE), col),
                pl.BlockSpec((TILE, TILE), col),
                pl.BlockSpec((window, features), whole),
                pl.BlockSpec((features, window), whole),
                pl.BlockSpec((window, TILE), whole),
            ],
            out_specs=[
                pl.BlockSpec((TILE, features), row),
                pl.BlockSpec((features, TILE), col),
                pl.BlockSpec((features, TILE), col),
                pl.BlockSpec((2 * pairs, TILE), col),
            ],
            scratch_shapes=[
                pltpu.VMEM((window // TILE, pairs, TILE, 2 * TILE), F32),
                pltpu.VMEM((pairs, 2 * TILE, 2 * TILE), BF),
                pltpu.VMEM((pairs, 8, 2 * TILE), F32),
                pltpu.VMEM((pairs, TILE + 16, TILE), F32),
            ],
        ),
        out_shape=[
            jax.ShapeDtypeStruct((length, features), BF),
            jax.ShapeDtypeStruct((features, length), F32),
            jax.ShapeDtypeStruct((features, length), BF),
            jax.ShapeDtypeStruct((2 * pairs, length), F32),
        ],
        compiler_params=pltpu.CompilerParams(vmem_limit_bytes=60 * VMEM_MIB),
        name="attend",
    )(lo, hi, queries_t, one_t, keys, values_t, aux)


def attend_back_kernel(
    kt_ref, qt_list_ref, count_ref, q_ref, qt_ref, dc_ref, dct_ref, onet_ref, lse_ref, delta_ref, k_ref, keys_t_ref,
    v_ref, aux_ref, dq_ref, dk_ref, dv_ref, dqt_scr, dk_scr, dv_scr,
):
    pairs = q_ref.shape[1] // TILE
    dqt_scr[...] = jnp.zeros(dqt_scr.shape, F32)
    dk_scr[...] = jnp.zeros(dk_scr.shape, F32)
    dv_scr[...] = jnp.zeros(dv_scr.shape, F32)

    def tile(n):
        krows = pl.ds(pl.multiple_of(kt_ref[n] * TILE, TILE), TILE)
        rows = pl.ds(pl.multiple_of(qt_list_ref[n] * TILE, TILE), TILE)
        one = onet_ref[:, rows]
        ones = jnp.concatenate([one, one], 1)
        aux = aux_ref[krows, :]
        for j in range(pairs):
            cols = slice(j * TILE, (j + 1) * TILE)
            keys = jnp.concatenate([k_ref[krows, cols], aux], 1)
            queries_t = jnp.concatenate([split_lanes(qt_ref[cols, rows]), ones], 0)
            lse = jnp.concatenate([lse_ref[2 * j : 2 * j + 1, rows], lse_ref[2 * j + 1 : 2 * j + 2, rows]], 1)
            p = jnp.exp(dot(keys, queries_t) - lse)
            delta = jnp.concatenate([delta_ref[2 * j : 2 * j + 1, rows], delta_ref[2 * j + 1 : 2 * j + 2, rows]], 1)
            ds = (p * (dot(v_ref[krows, cols], split_lanes(dct_ref[cols, rows])) - delta)).astype(BF)
            dv_scr[krows, cols] += dot(p.astype(BF), split_rows(dc_ref[rows, cols]))
            dk_scr[krows, cols] += dot(ds, split_rows(q_ref[rows, cols]))
            dqt_scr[cols, rows] += dot(split_lanes(keys_t_ref[cols, krows]), lanes_to_rows(ds))

    count = count_ref[0]

    def two(step, carry):
        tile(2 * step)
        tile(2 * step + 1)
        return carry

    lax.fori_loop(0, count // 2, two, 0)

    @pl.when(count % 2 == 1)
    def _():
        tile(count - 1)

    dk_ref[...] = dk_scr[...].astype(BF)
    dv_ref[...] = dv_scr[...].astype(BF)
    for i in range(q_ref.shape[0] // TILE):
        for j in range(pairs):
            block = dqt_scr[j * TILE : (j + 1) * TILE, i * TILE : (i + 1) * TILE] * 0.125
            dq_ref[i * TILE : (i + 1) * TILE, j * TILE : (j + 1) * TILE] = block.T.astype(BF)


def attend_back(part, parts, pair_list, queries, queries_t, grads, grads_t, one_t, lse, delta, keys, keys_t, values, aux):
    length, features = queries.shape
    window = keys.shape[0]
    own = features // parts
    heads = lse.shape[0] // parts
    tall = pl.BlockSpec((length, own), lambda i, *_: (0, part))
    flat = pl.BlockSpec((own, length), lambda i, *_: (part, 0))
    tall_window = pl.BlockSpec((window, own), lambda i, *_: (0, part))
    rows = pl.BlockSpec((None, heads, length), lambda i, *_: (part, 0, 0))
    first = lambda i, *_: (0, 0)
    return pl.pallas_call(
        attend_back_kernel,
        grid_spec=pltpu.PrefetchScalarGridSpec(
            num_scalar_prefetch=3,
            grid=(1,),
            in_specs=[
                tall,
                flat,
                tall,
                flat,
                pl.BlockSpec((TILE, length), first),
                rows,
                rows,
                tall_window,
                pl.BlockSpec((own, window), lambda i, *_: (part, 0)),
                tall_window,
                pl.BlockSpec((window, TILE), first),
            ],
            out_specs=[
                pl.BlockSpec((length, own), first),
                pl.BlockSpec((window, own), first),
                pl.BlockSpec((window, own), first),
            ],
            scratch_shapes=[
                pltpu.VMEM((own, length), F32),
                pltpu.VMEM((window, own), F32),
                pltpu.VMEM((window, own), F32),
            ],
        ),
        out_shape=[
            jax.ShapeDtypeStruct((length, own), BF),
            jax.ShapeDtypeStruct((window, own), BF),
            jax.ShapeDtypeStruct((window, own), BF),
        ],
        compiler_params=pltpu.CompilerParams(vmem_limit_bytes=60 * VMEM_MIB),
        name="attend_back",
    )(
        *pair_list, queries, queries_t, grads, grads_t, one_t, lse.reshape(parts, heads, length),
        delta.reshape(parts, heads, length), keys, keys_t, values, aux,
    )


def setup_kernel(
    lengths_ref, seq_ref, aux_ref, onet_ref, spread_ref, lo_ref, hi_ref, kt_ref, qt_ref, count_ref
):
    window, length = aux_ref.shape[0], spread_ref.shape[0]
    far = window - length
    seq = seq_ref[0]
    passages = lengths_ref.shape[1]
    ends, total = [], jnp.int32(0)
    for p in range(passages):
        total = total + lengths_ref[0, p]
        ends.append(total)
    window_start, own_start = seq * far, seq * length

    def segments(positions):
        found = jnp.zeros(positions.shape, jnp.int32)
        for end in ends:
            found = found + jnp.where(positions >= end, 1, 0)
        return found

    lane = lax.broadcasted_iota(jnp.int32, (TILE, TILE), 1)
    row = lax.broadcasted_iota(jnp.int32, (TILE, TILE), 0)

    def window_tile(i, carry):
        rows = pl.ds(pl.multiple_of(i * TILE, TILE), TILE)
        found = segments(window_start + i * TILE + row)
        apart = jnp.where((found != lane) & (lane <= passages), MASKED, 0.0)
        aux_ref[rows, :] = apart.astype(BF)
        return carry

    lax.fori_loop(0, window // TILE, window_tile, 0)

    def own_tile(i, carry):
        rows = pl.ds(pl.multiple_of(i * TILE, TILE), TILE)
        found = segments(own_start + i * TILE + row)
        same = (found == lane % 32) & (lane < 96) & (found < passages)
        spread_ref[rows, :] = jnp.where(same, 1.0, 0.0).astype(BF)
        found = segments(own_start + i * TILE + lane[:8])
        one = jnp.where(jnp.broadcast_to(found[:1], (TILE, TILE)) == row, 1.0, 0.0)
        onet_ref[:, rows] = one.astype(BF)
        return carry

    lax.fori_loop(0, length // TILE, own_tile, 0)

    def reach(first, low, high):
        begin, end = jnp.int32(0), jnp.int32(2 * length)
        for stop in ends:
            begin = jnp.where(stop <= first, stop, begin)
        for stop in reversed(ends):
            end = jnp.where(stop > first + TILE - 1, stop, end)
        begin = jnp.clip(begin, low, high) - low
        end = jnp.clip(end, low, high) - low
        return begin // TILE, (end + TILE - 1) // TILE

    for i in range(length // TILE):
        lo_ref[i], hi_ref[i] = reach(own_start + i * TILE, window_start, window_start + window)
    count = jnp.int32(0)
    for t in range(window // TILE):
        low, high = reach(window_start + t * TILE, own_start, own_start + length)

        def put(i, count):
            kt_ref[count] = t
            qt_ref[count] = i
            return count + 1

        count = lax.fori_loop(low, high, put, count)
    count_ref[0] = count


def setup(lengths, seq, length, window):
    tiles, window_tiles = length // TILE, window // TILE
    smem = pl.BlockSpec(memory_space=pltpu.SMEM)
    vmem = pl.BlockSpec(memory_space=pltpu.VMEM)
    number = lambda n: jax.ShapeDtypeStruct((n,), jnp.int32)
    return pl.pallas_call(
        setup_kernel,
        in_specs=[smem, smem],
        out_specs=[vmem] * 3 + [smem] * 5,
        out_shape=[
            jax.ShapeDtypeStruct((window, TILE), BF),
            jax.ShapeDtypeStruct((TILE, length), BF),
            jax.ShapeDtypeStruct((length, TILE), BF),
            number(tiles),
            number(tiles),
            number(tiles * window_tiles),
            number(tiles * window_tiles),
            number(1),
        ],
        name="setup",
    )(lengths, seq.reshape(1).astype(jnp.int32))


def own_kernel(place_ref, x_ref, wq_ref, wk_ref, wv_ref, vec_ref, q_ref, qt_ref, k_ref, kt_ref, v_ref, vt_ref, xt_ref):
    x = x_ref[...]
    q = ((dot(x, wq_ref[...]) + vec_ref[BIAS_Q : BIAS_Q + 1, :]) .astype(BF).astype(F32) * 0.125).astype(BF)
    q_ref[...] = q
    qt_ref[...] = q.T
    k = dot(x, wk_ref[...]).astype(BF)
    k_ref[...] = k
    kt_ref[...] = k.T
    v = (dot(x, wv_ref[...]) + vec_ref[BIAS_V : BIAS_V + 1, :]).astype(BF)
    v_ref[...] = v
    vt_ref[...] = v.T
    xt_ref[...] = x.T


def far_kernel(place_ref, x_ref, wk_ref, wv_ref, vec_ref, k_in, kt_in, v_in, vt_in, k_ref, kt_ref, v_ref, vt_ref):
    x = x_ref[...]
    k = dot(x, wk_ref[...]).astype(BF)
    k_ref[...] = k
    kt_ref[...] = k.T
    v = (dot(x, wv_ref[...]) + vec_ref[BIAS_V : BIAS_V + 1, :]).astype(BF)
    v_ref[...] = v
    vt_ref[...] = v.T


def project(x, x_far, wq, wk, wv, vectors, seq):
    length, features = x.shape
    far = x_far.shape[0]
    window = length + far
    rows = 256
    place = jnp.stack([seq * (far // rows), (1 - seq) * (length // rows)]).astype(jnp.int32)
    row = lambda i, place: (i, 0)
    col = lambda i, place: (0, i)
    whole = lambda i, place: (0, 0)
    once = pl.Buffered(1)
    weight = pl.BlockSpec((features, features), whole, pipeline_mode=once)
    vector = pl.BlockSpec(vectors.shape, whole, pipeline_mode=once)
    tall = jax.ShapeDtypeStruct((length, features), BF)
    flat = jax.ShapeDtypeStruct((features, length), BF)
    tall_window = jax.ShapeDtypeStruct((window, features), BF)
    flat_window = jax.ShapeDtypeStruct((features, window), BF)

    def window_blocks(which):
        down = pl.BlockSpec((rows, features), lambda i, place: (place[which] + i, 0))
        across = pl.BlockSpec((features, rows), lambda i, place: (0, place[which] + i))
        return [down, across, down, across]

    limit = pltpu.CompilerParams(vmem_limit_bytes=32 * VMEM_MIB)
    q, qt, k, kt, v, vt, xt = pl.pallas_call(
        own_kernel,
        grid_spec=pltpu.PrefetchScalarGridSpec(
            num_scalar_prefetch=1,
            grid=(length // rows,),
            in_specs=[pl.BlockSpec((rows, features), row), weight, weight, weight, vector],
            out_specs=[pl.BlockSpec((rows, features), row), pl.BlockSpec((features, rows), col)]
            + window_blocks(0)
            + [pl.BlockSpec((features, rows), col)],
        ),
        out_shape=[tall, flat, tall_window, flat_window, tall_window, flat_window, flat],
        compiler_params=limit,
        name="project_own",
    )(place, x, wq, wk, wv, vectors)
    anywhere = pl.BlockSpec(memory_space=pl.ANY)
    k, kt, v, vt = pl.pallas_call(
        far_kernel,
        grid_spec=pltpu.PrefetchScalarGridSpec(
            num_scalar_prefetch=1,
            grid=(far // rows,),
            in_specs=[pl.BlockSpec((rows, features), row), weight, weight, vector] + [anywhere] * 4,
            out_specs=window_blocks(1),
        ),
        out_shape=[tall_window, flat_window, tall_window, flat_window],
        input_output_aliases={5: 0, 6: 1, 7: 2, 8: 3},
        compiler_params=limit,
        name="project_far",
    )(place, x_far, wk, wv, vectors, k, kt, v, vt)
    return q, qt, k, kt, v, vt, xt


def loss_kernel(partners_ref, lengths_ref, place_ref, every_ref, pooled_ref, loss_ref, parts_ref):
    every = every_ref[...]
    count, features = every.shape
    own, _ = pooled_ref.shape
    first = place_ref[0] * own
    scores = 100.0 * dot(every, every, ((1,), (1,)))
    row = lax.broadcasted_iota(jnp.int32, (count, count), 0)
    lane = lax.broadcasted_iota(jnp.int32, (count, count), 1)
    scores = jnp.where(row == lane, BIG_NEG, scores)
    top = jnp.max(scores, 0, keepdims=True)
    log_sums = top + jnp.log(jnp.sum(jnp.exp(scores - top), 0, keepdims=True))
    mine = every_ref[pl.ds(pl.multiple_of(first, own), own), :]
    near = 100.0 * dot(mine, every, ((1,), (1,)))
    own_row = lax.broadcasted_iota(jnp.int32, (own, count), 0)
    own_lane = lax.broadcasted_iota(jnp.int32, (own, count), 1)
    near = jnp.where(own_row + first == own_lane, BIG_NEG, near)
    top = jnp.max(near, 1, keepdims=True)
    own_sums = top + jnp.log(jnp.sum(jnp.exp(near - top), 1, keepdims=True))
    target = jnp.concatenate(
        [jnp.where(own_lane[:1] == partners_ref[first + i], 1.0, 0.0) for i in range(own)], 0
    )
    picked = jnp.sum(jnp.where(target > 0.0, near, 0.0), 1, keepdims=True)
    loss_ref[...] = jnp.broadcast_to(own_sums - picked, loss_ref.shape)
    lane_row = own_lane[:1]

    def aim(n, held):
        return jnp.where(lane_row == n, partners_ref[n], held)

    aims = lax.fori_loop(0, count, aim, jnp.full((1, count), -1, jnp.int32))
    targeted = jnp.where(aims == own_row + first, 1.0, 0.0)
    both = jnp.exp(near - own_sums) - target + (jnp.exp(near - log_sums) - targeted)
    high, middle, low = split3(both)
    grad = 100.0 * (dot(high, every) + dot(middle, every) + dot(low, every))
    pooled = pooled_ref[...]
    inverse = lax.rsqrt(jnp.sum(pooled * pooled, 1, keepdims=True) + 1e-06)
    grad = inverse * grad - pooled * (inverse * inverse * inverse * jnp.sum(pooled * grad, 1, keepdims=True))
    sizes = jnp.concatenate(
        [jnp.full((1, features), lengths_ref[0, i].astype(F32), F32) for i in range(own)], 0
    )
    high, middle, low = split3(grad / sizes)
    parts_ref[...] = jnp.zeros(parts_ref.shape, BF)
    parts_ref[0:own, :] = high
    parts_ref[32 : 32 + own, :] = middle
    parts_ref[64 : 64 + own, :] = low


def contrast(partners, lengths, place, every, pooled):
    own, features = pooled.shape
    smem = pl.BlockSpec(memory_space=pltpu.SMEM)
    vmem = pl.BlockSpec(memory_space=pltpu.VMEM)
    return pl.pallas_call(
        loss_kernel,
        in_specs=[smem, smem, smem, vmem, vmem],
        out_specs=[vmem, vmem],
        out_shape=[jax.ShapeDtypeStruct((own, TILE), F32), jax.ShapeDtypeStruct((TILE, features), BF)],
        compiler_params=pltpu.CompilerParams(vmem_limit_bytes=48 * VMEM_MIB),
        name="contrast",
    )(partners, lengths, place.reshape(1).astype(jnp.int32), every, pooled)


def gelu_parts(u):
    size = jnp.abs(u)
    base = 1.0 + (0.3275911 * math.sqrt(0.5)) * size
    t = pl.reciprocal(base, approx=True)
    t = t * (2.0 - base * t)
    bell = jnp.exp(-0.5 * (u * u))
    poly = t * (0.127414796 + t * (-0.142248368 + t * (0.7107068705 + t * (-0.7265760135 + t * 0.5307027145))))
    tail = poly * bell
    below = jnp.where(u < 0.0, tail, 1.0 - tail)
    return u * below, below + u * bell * (1.0 / math.sqrt(2.0 * math.pi))


def normalized(resid):
    center = resid - jnp.mean(resid, -1, keepdims=True)
    scale = lax.rsqrt(jnp.mean(center * center, -1, keepdims=True) + EPS_NORM)
    return center * scale, scale


def feed_kernel(
    cb_ref, x_ref, member_ref, wo_ref, w1_ref, w2_ref, vec_ref,
    n1_ref, r1_ref, h_ref, f_ref, gp_ref, n2_ref, r2_ref, pool_ref,
):
    vector = lambda which: vec_ref[which : which + 1, :]
    attended = dot(cb_ref[...], wo_ref[...]) + vector(BIAS_O)
    unit, scale = normalized(x_ref[...].astype(F32) + attended)
    n1_ref[...] = unit.astype(BF)
    r1_ref[...] = scale
    hidden = unit * vector(GAIN_1) + vector(SHIFT_1)
    low = hidden.astype(BF)
    h_ref[...] = low.T
    resid = hidden + vector(BIAS_S)
    chunk = vec_ref.shape[1]
    for part in range(w1_ref.shape[1] // chunk):
        cols = slice(part * chunk, (part + 1) * chunk)
        u = dot(low, w1_ref[:, cols]) + vector(BIAS_E + part)
        active, slope = gelu_parts(u)
        active = active.astype(BF)
        f_ref[cols, :] = active.T
        gp_ref[:, cols] = slope.astype(BF)
        resid = resid + dot(active, w2_ref[cols, :])
    unit, scale = normalized(resid)
    n2_ref[...] = unit.astype(BF)
    r2_ref[...] = scale
    out = unit * vector(GAIN_2) + vector(SHIFT_2)
    high, middle, _ = split3(out)
    part = dot(member_ref[...], high) + dot(member_ref[...], middle)

    @pl.when(pl.program_id(0) == 0)
    def _():
        pool_ref[...] = part

    @pl.when(pl.program_id(0) > 0)
    def _():
        pool_ref[...] += part


def feed(cb, x, one_t, pass_count, wo, w1, w2, vectors):
    length, features = x.shape
    hidden = w1.shape[1]
    rows = 256
    row = lambda i: (i, 0)
    whole = lambda i: (0, 0)
    once = pl.Buffered(1)

    def full(array):
        return pl.BlockSpec(array.shape, whole, pipeline_mode=once)

    return pl.pallas_call(
        feed_kernel,
        grid=(length // rows,),
        in_specs=[
            pl.BlockSpec((rows, features), row),
            pl.BlockSpec((rows, features), row),
            pl.BlockSpec((pass_count, rows), lambda i: (0, i)),
        ]
        + [full(a) for a in (wo, w1, w2, vectors)],
        out_specs=[
            pl.BlockSpec((rows, features), row),
            pl.BlockSpec((rows, 1), row),
            pl.BlockSpec((features, rows), lambda i: (0, i)),
            pl.BlockSpec((hidden, rows), lambda i: (0, i)),
            pl.BlockSpec((rows, hidden), row),
            pl.BlockSpec((rows, features), row),
            pl.BlockSpec((rows, 1), row),
            pl.BlockSpec((pass_count, features), whole),
        ],
        out_shape=[
            jax.ShapeDtypeStruct((length, features), BF),
            jax.ShapeDtypeStruct((length, 1), F32),
            jax.ShapeDtypeStruct((features, length), BF),
            jax.ShapeDtypeStruct((hidden, length), BF),
            jax.ShapeDtypeStruct((length, hidden), BF),
            jax.ShapeDtypeStruct((length, features), BF),
            jax.ShapeDtypeStruct((length, 1), F32),
            jax.ShapeDtypeStruct((pass_count, features), F32),
        ],
        compiler_params=pltpu.CompilerParams(vmem_limit_bytes=60 * VMEM_MIB),
        name="feed",
    )(cb, x, one_t, wo, w1, w2, vectors)


def norm_back(grad, unit, scale, gain):
    wide = grad * gain
    return scale * (
        wide - jnp.mean(wide, -1, keepdims=True) - unit * jnp.mean(wide * unit, -1, keepdims=True)
    )


def add_rows(ref, row, value):
    ref[row : row + 1, :] += jnp.sum(value, 0, keepdims=True)


def start_back_kernel(spread_ref, pooled_ref, n2_ref, r2_ref, g2_ref, dr_ref, dy_ref, sums_ref):
    @pl.when(pl.program_id(0) == 0)
    def _():
        sums_ref[...] = jnp.zeros(sums_ref.shape, F32)

    grad = dot(spread_ref[...], pooled_ref[...])
    unit = n2_ref[...].astype(F32)
    add_rows(sums_ref, 0, grad * unit)
    add_rows(sums_ref, 1, grad)
    dr = norm_back(grad, unit, r2_ref[...], g2_ref[GAIN_2 : GAIN_2 + 1, :])
    dr_ref[...] = dr
    dy = dr.astype(BF)
    dy_ref[...] = dy
    add_rows(sums_ref, 2, dy.astype(F32))


def start_back(spread, pooled_parts, n2, r2, g2):
    length, features = n2.shape
    rows = 256
    row = lambda i: (i, 0)
    whole = lambda i: (0, 0)
    return pl.pallas_call(
        start_back_kernel,
        grid=(length // rows,),
        in_specs=[
            pl.BlockSpec((rows, spread.shape[1]), row),
            pl.BlockSpec(pooled_parts.shape, whole),
            pl.BlockSpec((rows, features), row),
            pl.BlockSpec((rows, 1), row),
            pl.BlockSpec(g2.shape, whole),
        ],
        out_specs=[
            pl.BlockSpec((rows, features), row),
            pl.BlockSpec((rows, features), row),
            pl.BlockSpec((8, features), whole),
        ],
        out_shape=[
            jax.ShapeDtypeStruct((length, features), F32),
            jax.ShapeDtypeStruct((length, features), BF),
            jax.ShapeDtypeStruct((8, features), F32),
        ],
        name="start_back",
    )(spread, pooled_parts, n2, r2, g2)


def expand_back_kernel(dy_ref, gp_ref, w2_ref, du_ref, wide_sums_ref):
    @pl.when(pl.program_id(0) == 0)
    def _():
        wide_sums_ref[...] = jnp.zeros(wide_sums_ref.shape, F32)

    dy = dy_ref[...]
    chunk = 512
    for start in range(0, w2_ref.shape[0], chunk):
        cols = slice(start, start + chunk)
        slope = gp_ref[:, cols].astype(F32)
        du = (slope * dot(dy, w2_ref[cols, :], ((1,), (1,)))).astype(BF)
        du_ref[:, cols] = du
        wide_sums_ref[0:1, cols] += jnp.sum(du.astype(F32), 0, keepdims=True)


def expand_back(dy, gp, w2):
    length, features = dy.shape
    hidden = gp.shape[1]
    rows = 256
    row = lambda i: (i, 0)
    whole = lambda i: (0, 0)
    return pl.pallas_call(
        expand_back_kernel,
        grid=(length // rows,),
        in_specs=[
            pl.BlockSpec((rows, features), row),
            pl.BlockSpec((rows, hidden), row),
            pl.BlockSpec(w2.shape, whole, pipeline_mode=pl.Buffered(1)),
        ],
        out_specs=[pl.BlockSpec((rows, hidden), row), pl.BlockSpec((8, hidden), whole)],
        out_shape=[jax.ShapeDtypeStruct((length, hidden), BF), jax.ShapeDtypeStruct((8, hidden), F32)],
        compiler_params=pltpu.CompilerParams(vmem_limit_bytes=60 * VMEM_MIB),
        name="expand_back",
    )(dy, gp, w2)


def hidden_back_kernel(dr2_ref, du_ref, n1_ref, r1_ref, w1_ref, wo_ref, g1_ref, ct_ref, dr1_ref, da_ref, dc_ref, dct_ref, delta_ref, sums_ref):
    @pl.when(pl.program_id(0) == 0)
    def _():
        sums_ref[...] = jnp.zeros(sums_ref.shape, F32)

    dh = dr2_ref[...] + dot(du_ref[...], w1_ref[...], ((1,), (1,)))
    unit = n1_ref[...].astype(F32)
    add_rows(sums_ref, 0, dh * unit)
    add_rows(sums_ref, 1, dh)
    dr = norm_back(dh, unit, r1_ref[...], g1_ref[GAIN_1 : GAIN_1 + 1, :])
    dr1_ref[...] = dr
    da = dr.astype(BF)
    da_ref[...] = da
    add_rows(sums_ref, 2, da.astype(F32))
    dc_ref[...] = dot(da, wo_ref[...], ((1,), (1,))).astype(BF)
    dct = dot(wo_ref[...], da, ((1,), (1,))).astype(BF)
    dct_ref[...] = dct
    product = dct.astype(F32) * ct_ref[...]
    size = product.shape[0] // HEADS
    delta_ref[...] = jnp.concatenate(
        [jnp.sum(product[head * size : (head + 1) * size], 0, keepdims=True) for head in range(HEADS)], 0
    )


def hidden_back(dr2, du, n1, r1, w1, wo, g1, ct):
    length, features = dr2.shape
    hidden = du.shape[1]
    rows = 256
    row = lambda i: (i, 0)
    whole = lambda i: (0, 0)
    once = pl.Buffered(1)

    def full(array):
        return pl.BlockSpec(array.shape, whole, pipeline_mode=once)

    return pl.pallas_call(
        hidden_back_kernel,
        grid=(length // rows,),
        in_specs=[
            pl.BlockSpec((rows, features), row),
            pl.BlockSpec((rows, hidden), row),
            pl.BlockSpec((rows, features), row),
            pl.BlockSpec((rows, 1), row),
            full(w1),
            full(wo),
            full(g1),
            pl.BlockSpec((features, rows), lambda i: (0, i)),
        ],
        out_specs=[
            pl.BlockSpec((rows, features), row),
            pl.BlockSpec((rows, features), row),
            pl.BlockSpec((rows, features), row),
            pl.BlockSpec((features, rows), lambda i: (0, i)),
            pl.BlockSpec((HEADS, rows), lambda i: (0, i)),
            pl.BlockSpec((8, features), whole),
        ],
        out_shape=[
            jax.ShapeDtypeStruct((length, features), F32),
            jax.ShapeDtypeStruct((length, features), BF),
            jax.ShapeDtypeStruct((length, features), BF),
            jax.ShapeDtypeStruct((features, length), BF),
            jax.ShapeDtypeStruct((HEADS, length), F32),
            jax.ShapeDtypeStruct((8, features), F32),
        ],
        compiler_params=pltpu.CompilerParams(vmem_limit_bytes=60 * VMEM_MIB),
        name="hidden_back",
    )(dr2, du, n1, r1, w1, wo, g1, ct)


def swap_seq(array):
    return lax.ppermute(array, "seq", [(0, 1), (1, 0)])


def swap_dp(array, bit):
    count = lax.axis_size("dp")
    return lax.ppermute(array, "dp", [(i, i ^ (1 << bit)) for i in range(count)])


def swap_crossed(array, bits):
    count = lax.axis_size("dp")
    pairs = [(2 * i + s, 2 * (i ^ (1 << bits[s])) + s) for i in range(count) for s in range(2)]
    return lax.ppermute(array, ("dp", "seq"), pairs)


def pick_half(array, axis, which):
    half = array.shape[axis] // 2
    return lax.dynamic_slice_in_dim(array, which * half, half, axis)


def join(mine, other, axis, place):
    return jnp.where(
        place == 0, jnp.concatenate([mine, other], axis), jnp.concatenate([other, mine], axis)
    )


def halving_axis(shape):
    rows, cols = shape
    if rows % 32 == 0:
        return 0
    if cols % 256 == 0:
        return 1
    return 0


COLS = 384


def partial_kernel(counts, add, place_ref, *refs):
    sources = len(counts)
    lefts, rights = refs[:sources], refs[sources : 2 * sources]
    out_ref = refs[-1]
    block = place_ref[0] * (sum(counts) // 2) + pl.program_id(1)
    start = 0
    for left, right, count in zip(lefts, rights, counts):

        @pl.when((block >= start) & (block < start + count))
        def _(left=left, right=right):
            value = dot(left[...], right[...])
            if add:
                value = value + refs[2 * sources][...].astype(F32)
            out_ref[...] = value.astype(BF)

        start += count


def partial_grads(sources, half, part, parts, received=None):
    counts = [right.shape[1] // COLS for _, right in sources]
    total = sum(counts) // 2
    length = sources[0][0].shape[1]
    rows = sources[0][0].shape[0] // parts
    step = min(rows, 768)
    blocks = rows // step
    starts = [sum(counts[:i]) for i in range(len(counts))]
    in_specs = [
        pl.BlockSpec((step, length), lambda i, j, place: (place[1] * blocks + i, 0)) for _ in sources
    ]
    for start, count in zip(starts, counts):
        in_specs.append(
            pl.BlockSpec(
                (length, COLS),
                lambda i, j, place, start=start, count=count: (
                    0,
                    jnp.clip(place[0] * total + j - start, 0, count - 1),
                ),
            )
        )
    operands = [left for left, _ in sources] + [right for _, right in sources]
    if received is not None:
        in_specs.append(pl.BlockSpec((step, COLS), lambda i, j, place: (place[1] * blocks + i, j)))
        operands.append(received)
    return pl.pallas_call(
        functools.partial(partial_kernel, counts, received is not None),
        grid_spec=pltpu.PrefetchScalarGridSpec(
            num_scalar_prefetch=1,
            grid=(blocks, total),
            in_specs=in_specs,
            out_specs=pl.BlockSpec((step, COLS), lambda i, j, place: (i, j)),
        ),
        out_shape=jax.ShapeDtypeStruct((rows, total * COLS), BF),
        compiler_params=pltpu.CompilerParams(vmem_limit_bytes=60 * VMEM_MIB),
        name="partial_grads",
    )(jnp.stack([half, part]).astype(jnp.int32), *operands)


def fold_kernel(parts, place_ref, keep_ref, other_ref, *out_refs):
    total = (keep_ref[...].astype(F32) + other_ref[...].astype(F32)).astype(BF)
    for m in range(parts):

        @pl.when(pl.program_id(0) == m)
        def _(m=m):
            out_refs[m][...] = total


def fold(keep, other, place, parts):
    rows, cols = keep.shape[0] // parts, keep.shape[1]
    picked = pl.BlockSpec((rows, cols), lambda m, place: (place[0] ^ m, 0))
    return pl.pallas_call(
        functools.partial(fold_kernel, parts),
        grid_spec=pltpu.PrefetchScalarGridSpec(
            num_scalar_prefetch=1,
            grid=(parts,),
            in_specs=[picked, picked],
            out_specs=[pl.BlockSpec((rows, cols), lambda m, place: (0, 0))] * parts,
        ),
        out_shape=[jax.ShapeDtypeStruct((rows, cols), BF)] * parts,
        compiler_params=pltpu.CompilerParams(vmem_limit_bytes=60 * VMEM_MIB),
        name="fold",
    )(place.reshape(1).astype(jnp.int32), keep, other)


def assemble_kernel(counts, place_ref, own_ref, other_ref, *out_refs):
    block = pl.program_id(0)
    per_half = sum(counts) // 2
    mine = block // per_half == place_ref[0]
    shards, rows = own_ref.shape[0], own_ref.shape[1]

    def write(source, offset):
        start = 0
        for out_ref, count in zip(out_refs, counts):

            @pl.when((block >= start) & (block < start + count))
            def _(out_ref=out_ref):
                for shard in range(shards):
                    out_ref[shard * rows : (shard + 1) * rows, :] = source[shard ^ offset].astype(F32)

            start += count

    @pl.when(mine)
    def _():
        write(own_ref, place_ref[1])

    @pl.when(jnp.logical_not(mine))
    def _():
        write(other_ref, place_ref[2])


def assemble(own, other, places, counts):
    shards, rows, _ = own.shape
    per_half = sum(counts) // 2
    out_specs, start = [], 0
    for count in counts:
        out_specs.append(
            pl.BlockSpec(
                (shards * rows, COLS), lambda g, place, start=start, count=count: (0, jnp.clip(g - start, 0, count - 1))
            )
        )
        start += count

    def shard_block(flag):
        return pl.BlockSpec(
            (shards, rows, COLS),
            lambda g, place: (0, 0, jnp.where((g // per_half == place[0]) == flag, g % per_half, 0)),
        )

    return pl.pallas_call(
        functools.partial(assemble_kernel, counts),
        grid_spec=pltpu.PrefetchScalarGridSpec(
            num_scalar_prefetch=1,
            grid=(2 * per_half,),
            in_specs=[shard_block(True), shard_block(False)],
            out_specs=out_specs,
        ),
        out_shape=[jax.ShapeDtypeStruct((shards * rows, count * COLS), F32) for count in counts],
        compiler_params=pltpu.CompilerParams(vmem_limit_bytes=60 * VMEM_MIB),
        name="assemble",
    )(jnp.stack(places).astype(jnp.int32), own, other)


class GradTotal:
    steps = 8

    def __init__(self, sources):
        self.sources, self.step = sources, 0
        seq, dp = lax.axis_index("seq"), lax.axis_index("dp")
        self.seq, self.far = seq, (dp >> 2) & 3
        self.near = ((dp >> seq) & 1, (dp >> (1 - seq)) & 1)
        self.state = None

    def offset(self, seq):
        dp = lax.axis_index("dp")
        return ((dp >> seq) & 1) * 8 + ((dp >> (1 - seq)) & 1) * 4 + ((dp >> 2) & 3)

    def prepare(self):
        step = self.step
        if step == 0:
            self.out = [partial_grads(self.sources, 1 - self.seq, jnp.int32(0), 1)]
        elif step == 1:
            self.out = [partial_grads(self.sources, self.seq, 1 - self.near[0], 2, self.got[0])]
            self.swapped = self.got[0]
        elif step == 2:
            keep = partial_grads(self.sources, self.seq, self.near[0], 2, self.swapped)
            self.keep, send = fold(keep, self.got[0], self.near[1], 2)
            self.out = [send]
        elif step == 3:
            self.keep, *self.out = fold(self.keep, self.got[0], self.far, 4)
        elif step == 4:
            total = self.keep.astype(F32)
            for other in self.got:
                total = total + other.astype(F32)
            self.out = [total.astype(BF)]
        elif step == 5:
            self.out = [jnp.stack(self.out + self.got)]
        else:
            self.out = [jnp.concatenate(self.out + self.got)]

    def exchange(self):
        step, count = self.step, lax.axis_size("dp")
        if step in (0, 7):
            self.got = [swap_seq(self.out[0])]
        elif step in (1, 6):
            self.got = [swap_crossed(self.out[0], (0, 1))]
        elif step in (2, 5):
            self.got = [swap_crossed(self.out[0], (1, 0))]
        else:
            sends = self.out if step == 3 else self.out * 3
            self.got = [
                lax.ppermute(send, "dp", [(i, i ^ (m << 2)) for i in range(count)])
                for m, send in zip((1, 2, 3), sends)
            ]
        self.step += 1

    def done(self):
        return self.step == self.steps

    def whole(self, counts):
        places = [self.seq, self.offset(self.seq), self.offset(1 - self.seq)]
        return assemble(self.out[0], self.got[0], places, counts)


def plain_total(partial):
    seq, index = lax.axis_index("seq"), lax.axis_index("dp")
    block = (pick_half(partial, 0, seq).astype(F32) + swap_seq(pick_half(partial, 0, 1 - seq)).astype(F32)).astype(BF)
    steps = []
    for bit in range(int(math.log2(lax.axis_size("dp")))):
        place, axis = (index >> bit) & 1, halving_axis(block.shape)
        steps.append((bit, place, axis))
        other = swap_dp(pick_half(block, axis, 1 - place), bit)
        block = (pick_half(block, axis, place).astype(F32) + other.astype(F32)).astype(BF)
    for bit, place, axis in reversed(steps):
        block = join(block, swap_dp(block, bit), axis, place)
    return join(block, swap_seq(block), 0, seq).astype(F32)


class PlainTotal:
    def __init__(self, sources):
        self.sources = sources

    def done(self):
        return True

    def whole(self, counts):
        return [plain_total(dot(left, right).astype(BF)) for left, right in self.sources]


class Small:
    def __init__(self, partial):
        self.block, self.step = partial, 0
        self.steps = 1 + int(math.log2(lax.axis_size("dp")))

    def prepare(self):
        if self.step:
            self.block = self.block + self.got[0]
        self.out = [self.block]

    def exchange(self):
        block = self.out[0]
        self.block = block
        self.got = [swap_seq(block) if self.step == 0 else swap_dp(block, self.step - 1)]
        self.step += 1

    def done(self):
        return self.step == self.steps

    def whole(self):
        return self.block + self.got[0]


def fence(*values):
    return lax.optimization_barrier(values)


def beside(sums, work, *inputs):
    live = [total for total in sums if not total.done()]
    for total in live:
        total.prepare()
    inputs, sends = fence(inputs, [total.out for total in live])
    for total, send in zip(live, sends):
        total.out = send
        total.exchange()
    result, received = fence(work(*inputs), [total.got for total in live])
    for total, got in zip(live, received):
        total.got = got
    return result


def body(
    tokens, lengths, partners, query_proj, query_bias, key_proj, value_proj, value_bias, output_proj, output_bias,
    first_gain, first_shift, expand_proj, expand_bias, shrink_proj, shrink_bias, second_gain, second_shift,
):
    _, length, features = tokens.shape
    pass_count = lengths.shape[1]
    seq = lax.axis_index("seq")
    dp = lax.axis_index("dp")
    far = length // 2
    window = length + far
    x = tokens[0]

    x_far = swap_seq(lax.dynamic_slice_in_dim(x, (1 - seq) * far, far, 0))
    vectors = jnp.concatenate(
        [
            jnp.stack(
                [
                    output_bias, first_gain, first_shift, shrink_bias, second_gain, second_shift, query_bias, value_bias,
                ]
            ),
            expand_bias.reshape(-1, features),
        ]
    )
    aux, one_t, spread, key_lo, key_hi, *pair_list = setup(lengths, seq, length, window)
    queries, queries_t, keys, keys_t, values, values_t, x_t = project(
        x, x_far, query_proj, key_proj, value_proj, vectors, seq
    )
    context_low, context_t, context_low_t, lse = attend(queries_t, one_t, keys, values_t, aux, key_lo, key_hi)
    unit1, scale1, hidden_t, active_t, slope, unit2, scale2, pooled_part = feed(
        context_low, x, one_t, pass_count, output_proj, expand_proj, shrink_proj, vectors
    )

    lengths_wide = lengths.reshape(pass_count, 1).astype(F32)
    pooled = (pooled_part + swap_seq(pooled_part)) / lengths_wide
    inverse = lax.rsqrt(jnp.sum(pooled * pooled, -1, keepdims=True) + 1e-06)
    every = (pooled * inverse).astype(BF)
    for bit in range(int(math.log2(lax.axis_size("dp")))):
        every = join(every, swap_dp(every, bit), 0, (dp >> bit) & 1)
    passage_loss, pooled_parts = contrast(partners, lengths, dp, every, pooled)
    passage_loss = passage_loss[:, 0]

    grad_second, grad_shrunk, sums2 = start_back(spread, pooled_parts, unit2, scale2, vectors)
    Sum = GradTotal if lax.axis_size("dp") == 16 else PlainTotal
    shrink_sum = Sum([(active_t, grad_shrunk)])
    grad_expanded, wide_sums = beside([shrink_sum], expand_back, grad_shrunk, slope, shrink_proj)
    grad_first, grad_attended, grad_context, grad_context_t, delta, sums1 = beside(
        [shrink_sum],
        lambda second, expanded: hidden_back(
            second, expanded, unit1, scale1, expand_proj, output_proj, vectors, context_t
        ),
        grad_second,
        grad_expanded,
    )
    expand_sum = Sum([(hidden_t, grad_expanded), (context_low_t, grad_attended)])
    parts = 2
    pieces = []
    for part in range(parts):

        def attention_work(grad_context):
            return attend_back(
                part, parts, pair_list, queries, queries_t, grad_context, grad_context_t, one_t, lse, delta, keys,
                keys_t, values, aux,
            )

        pieces.append(beside([shrink_sum, expand_sum], attention_work, grad_context))
    grad_query, grad_keys, grad_values = (jnp.concatenate(piece, 1) for piece in zip(*pieces))

    def gather_far(window_grad):
        own = lax.dynamic_slice_in_dim(window_grad, seq * far, length, 0)
        other = swap_seq(lax.dynamic_slice_in_dim(window_grad, (1 - seq) * length, far, 0))
        nothing = jnp.zeros((far, features), BF)
        return (own.astype(F32) + join(other, nothing, 0, 1 - seq).astype(F32)).astype(BF)

    def last_work(grad_keys, grad_values):
        return gather_far(grad_keys), gather_far(grad_values)

    keys_grad, values_grad = beside([shrink_sum, expand_sum], last_work, grad_keys, grad_values)
    attention_sum = Sum([(x_t, grad_query), (x_t, keys_grad), (x_t, values_grad)])

    def tokens_work(grad_first, grad_query, keys_grad, values_grad):
        tokens_grad = (
            grad_first
            + dot(grad_query, query_proj, ((1,), (1,)))
            + dot(keys_grad, key_proj, ((1,), (1,)))
            + dot(values_grad, value_proj, ((1,), (1,)))
        )[None]
        small = jnp.concatenate(
            [
                sums2[:3],
                sums1[:3],
                jnp.sum(grad_query.astype(F32), 0, keepdims=True),
                jnp.sum(values_grad.astype(F32), 0, keepdims=True),
                wide_sums[:1].reshape(-1, features),
            ],
            0,
        )
        return tokens_grad, small

    tokens_grad, small = beside(
        [shrink_sum, expand_sum, attention_sum], tokens_work, grad_first, grad_query, keys_grad, values_grad
    )
    small_sum = Small(small)
    sums = [shrink_sum, expand_sum, attention_sum, small_sum]
    blocks = {shrink_sum: [features // COLS], expand_sum: [expand_proj.shape[1] // COLS, features // COLS]}
    wholes = {}
    while not all(total.done() for total in sums):
        ready = [total for total in (shrink_sum, expand_sum) if total.done() and total not in wholes][:1]
        results = beside(sums, lambda _: [total.whole(blocks[total]) for total in ready], small)
        wholes.update(zip(ready, results))
    for total in (shrink_sum, expand_sum):
        if total not in wholes:
            wholes[total] = total.whole(blocks[total])
    small = small_sum.whole()
    (shrink_total,) = wholes[shrink_sum]
    expand_total, output_total = wholes[expand_sum]
    query_total, key_total, value_total = attention_sum.whole([features // COLS] * 3)
    return (
        passage_loss,
        tokens_grad,
        query_total,
        small[6],
        key_total,
        value_total,
        small[7],
        output_total,
        small[5],
        small[3],
        small[4],
        expand_total,
        small[8:].reshape(-1),
        shrink_total,
        small[2],
        small[0],
        small[1],
    )


def solution(mesh):
    placed = (P("dp", "seq", None), P("dp", None)) + (P(),) * 16
    return jax.shard_map(
        body,
        mesh=mesh,
        in_specs=placed,
        out_specs=(P("dp"), P("dp", "seq", None)) + (P(),) * 15,
        check_vma=False,
    )
```

```python
import functools
import math

import jax
import jax.numpy as jnp
from jax import lax
from jax.experimental import pallas as pl
from jax.experimental.pallas import tpu as pltpu
from jax.sharding import PartitionSpec as P

HEADS = 12
EPS_NORM = 1e-12
BIG_NEG = -1000000000.0
HIGH = lax.Precision.HIGHEST
BF = jnp.bfloat16
F32 = jnp.float32
TILE = 128
MASKED = -float(2**30)
BIAS_O, GAIN_1, SHIFT_1, BIAS_S, GAIN_2, SHIFT_2, BIAS_Q, BIAS_V, BIAS_E = range(9)
VMEM_MIB = 1 << 20


def dot(left, right, over=((1,), (0,))):
    return lax.dot_general(left, right, (over, ((), ())), preferred_element_type=F32)


def split3(value):
    high = value.astype(BF)
    rest = value - high.astype(F32)
    middle = rest.astype(BF)
    low = (rest - middle.astype(F32)).astype(BF)
    return high, middle, low


def split_lanes(pair):
    row = lax.broadcasted_iota(jnp.int32, (TILE, 1), 0)
    first = jnp.where(row < TILE // 2, 1.0, 0.0).astype(BF)
    second = jnp.where(row < TILE // 2, 0.0, 1.0).astype(BF)
    return jnp.concatenate([pair * first, pair * second], 1)


def split_rows(pair):
    lane = lax.broadcasted_iota(jnp.int32, (1, TILE), 1)
    first = jnp.where(lane < TILE // 2, 1.0, 0.0).astype(BF)
    second = jnp.where(lane < TILE // 2, 0.0, 1.0).astype(BF)
    return jnp.concatenate([pair * first, pair * second], 0)


def lanes_to_rows(both):
    return jnp.concatenate([both[:, :TILE], both[:, TILE:]], 0)


def attend_kernel(
    lo_ref, hi_ref, qt_ref, onet_ref, k_ref, vt_ref, aux_ref, c_ref, ct_ref, ctb_ref, lse_ref, s_scr, q_scr, m_scr, o_scr
):
    lo, hi = lo_ref[pl.program_id(0)], hi_ref[pl.program_id(0)]
    pairs = k_ref.shape[1] // TILE
    m_scr[...] = jnp.full(m_scr.shape, 2.0 * MASKED, F32)
    o_scr[...] = jnp.zeros(o_scr.shape, F32)
    one = onet_ref[...]
    for j in range(pairs):
        q_scr[j, :TILE, :] = split_lanes(qt_ref[j * TILE : (j + 1) * TILE, :])
        q_scr[j, TILE:, :] = jnp.concatenate([one, one], 1)
    extra = o_scr.shape[1] - TILE
    row = lax.broadcasted_iota(jnp.int32, (extra, 2 * TILE), 0)
    lane = lax.broadcasted_iota(jnp.int32, (extra, 2 * TILE), 1)
    ones = jnp.where(row == lane // TILE, 1.0, 0.0).astype(BF)

    count = (hi - lo + 1) // 2
    lo = jnp.minimum(lo, k_ref.shape[0] // TILE - 2 * count)

    def scores(step, carry):
        start = pl.multiple_of((lo + 2 * step) * TILE, TILE)
        for half in range(2):
            rows = pl.ds(pl.multiple_of(start + half * TILE, TILE), TILE)
            aux = aux_ref[rows, :]
            for j in range(pairs):
                keys = jnp.concatenate([k_ref[rows, j * TILE : (j + 1) * TILE], aux], 1)
                s = dot(keys, q_scr[j])
                s_scr[2 * step + half, j] = s
                m_scr[j] = jnp.maximum(m_scr[j], jnp.max(s.reshape(TILE // 8, 8, 2 * TILE), 0))
        return carry

    lax.fori_loop(0, count, scores, 0)
    for j in range(pairs):
        m_scr[j] = jnp.broadcast_to(jnp.max(m_scr[j], 0, keepdims=True), (8, 2 * TILE))

    def weigh(step, carry):
        start = pl.multiple_of((lo + 2 * step) * TILE, TILE)
        for j in range(pairs):
            values, weights = [], []
            for half in range(2):
                cols = pl.ds(pl.multiple_of(start + half * TILE, TILE), TILE)
                p = jnp.exp(s_scr[2 * step + half, j] - m_scr[j, 0:1, :]).astype(BF)
                values.append(
                    jnp.concatenate([split_lanes(vt_ref[j * TILE : (j + 1) * TILE, cols]), ones], 0)
                )
                weights.append(lanes_to_rows(p))
            o_scr[j] += dot(jnp.concatenate(values, 1), jnp.concatenate(weights, 0))
        return carry

    lax.fori_loop(0, count, weigh, 0)
    half = TILE // 2
    for j in range(pairs):
        cols = slice(j * TILE, (j + 1) * TILE)
        total = o_scr[j, TILE : TILE + 2, :]
        inverse = 1.0 / total
        ct = jnp.concatenate(
            [o_scr[j, :half, :] * inverse[0:1], o_scr[j, half:TILE, :] * inverse[1:2]], 0
        )
        ct_ref[cols, :] = ct
        ctb_ref[cols, :] = ct.astype(BF)
        c_ref[:, cols] = ct.T.astype(BF)
        top = jnp.concatenate([m_scr[j, 0:1, :TILE], m_scr[j, 0:1, TILE:]], 0)
        lse_ref[2 * j : 2 * j + 2, :] = top + jnp.log(total)


def attend(queries_t, one_t, keys, values_t, aux, lo, hi):
    features, length = queries_t.shape
    window = keys.shape[0]
    pairs = features // TILE
    row = lambda i, *_: (i, 0)
    col = lambda i, *_: (0, i)
    whole = lambda i, *_: (0, 0)
    return pl.pallas_call(
        attend_kernel,
        grid_spec=pltpu.PrefetchScalarGridSpec(
            num_scalar_prefetch=2,
            grid=(length // TILE,),
            in_specs=[
                pl.BlockSpec((features, TILE), col),
                pl.BlockSpec((TILE, TILE), col),
                pl.BlockSpec((window, features), whole),
                pl.BlockSpec((features, window), whole),
                pl.BlockSpec((window, TILE), whole),
            ],
            out_specs=[
                pl.BlockSpec((TILE, features), row),
                pl.BlockSpec((features, TILE), col),
                pl.BlockSpec((features, TILE), col),
                pl.BlockSpec((2 * pairs, TILE), col),
            ],
            scratch_shapes=[
                pltpu.VMEM((window // TILE, pairs, TILE, 2 * TILE), F32),
                pltpu.VMEM((pairs, 2 * TILE, 2 * TILE), BF),
                pltpu.VMEM((pairs, 8, 2 * TILE), F32),
                pltpu.VMEM((pairs, TILE + 16, TILE), F32),
            ],
        ),
        out_shape=[
            jax.ShapeDtypeStruct((length, features), BF),
            jax.ShapeDtypeStruct((features, length), F32),
            jax.ShapeDtypeStruct((features, length), BF),
            jax.ShapeDtypeStruct((2 * pairs, length), F32),
        ],
        compiler_params=pltpu.CompilerParams(vmem_limit_bytes=60 * VMEM_MIB),
        name="attend",
    )(lo, hi, queries_t, one_t, keys, values_t, aux)


def attend_back_kernel(
    kt_ref, qt_list_ref, count_ref, place_ref, q_ref, qt_ref, dc_ref, dct_ref, onet_ref, lse_ref, delta_ref, k_ref, keys_t_ref,
    v_ref, aux_ref, grads_ref, far_ref, dqt_scr, dk_scr, dv_scr,
):
    pairs = q_ref.shape[1] // TILE
    dqt_scr[...] = jnp.zeros(dqt_scr.shape, F32)
    dk_scr[...] = jnp.zeros(dk_scr.shape, F32)
    dv_scr[...] = jnp.zeros(dv_scr.shape, F32)

    def tile(n):
        krows = pl.ds(pl.multiple_of(kt_ref[n] * TILE, TILE), TILE)
        rows = pl.ds(pl.multiple_of(qt_list_ref[n] * TILE, TILE), TILE)
        one = onet_ref[:, rows]
        ones = jnp.concatenate([one, one], 1)
        aux = aux_ref[krows, :]
        for j in range(pairs):
            cols = slice(j * TILE, (j + 1) * TILE)
            keys = jnp.concatenate([k_ref[krows, cols], aux], 1)
            queries_t = jnp.concatenate([split_lanes(qt_ref[cols, rows]), ones], 0)
            lse = jnp.concatenate([lse_ref[2 * j : 2 * j + 1, rows], lse_ref[2 * j + 1 : 2 * j + 2, rows]], 1)
            p = jnp.exp(dot(keys, queries_t) - lse)
            delta = jnp.concatenate([delta_ref[2 * j : 2 * j + 1, rows], delta_ref[2 * j + 1 : 2 * j + 2, rows]], 1)
            ds = (p * (dot(v_ref[krows, cols], split_lanes(dct_ref[cols, rows])) - delta)).astype(BF)
            dv_scr[krows, cols] += dot(p.astype(BF), split_rows(dc_ref[rows, cols]))
            dk_scr[krows, cols] += dot(ds, split_rows(q_ref[rows, cols]))
            dqt_scr[cols, rows] += dot(split_lanes(keys_t_ref[cols, krows]), lanes_to_rows(ds))

    count = count_ref[0]

    def two(step, carry):
        tile(2 * step)
        tile(2 * step + 1)
        return carry

    lax.fori_loop(0, count // 2, two, 0)

    @pl.when(count % 2 == 1)
    def _():
        tile(count - 1)

    length, own = q_ref.shape
    far = k_ref.shape[0] - length
    near_rows = pl.ds(pl.multiple_of(place_ref[0] * far, TILE), length)
    far_rows = pl.ds(pl.multiple_of((1 - place_ref[0]) * length, TILE), far)
    grads_ref[:, own : 2 * own] = dk_scr[near_rows, :].astype(BF)
    grads_ref[:, 2 * own :] = dv_scr[near_rows, :].astype(BF)
    far_ref[:, :own] = dk_scr[far_rows, :].astype(BF)
    far_ref[:, own:] = dv_scr[far_rows, :].astype(BF)
    for i in range(length // TILE):
        for j in range(pairs):
            block = dqt_scr[j * TILE : (j + 1) * TILE, i * TILE : (i + 1) * TILE] * 0.125
            grads_ref[i * TILE : (i + 1) * TILE, j * TILE : (j + 1) * TILE] = block.T.astype(BF)


def attend_back(part, parts, seq, pair_list, queries, queries_t, grads, grads_t, one_t, lse, delta, keys, keys_t, values, aux):
    length, features = queries.shape
    window = keys.shape[0]
    own = features // parts
    heads = lse.shape[0] // parts
    tall = pl.BlockSpec((length, own), lambda i, *_: (0, part))
    flat = pl.BlockSpec((own, length), lambda i, *_: (part, 0))
    tall_window = pl.BlockSpec((window, own), lambda i, *_: (0, part))
    rows = pl.BlockSpec((None, heads, length), lambda i, *_: (part, 0, 0))
    first = lambda i, *_: (0, 0)
    return pl.pallas_call(
        attend_back_kernel,
        grid_spec=pltpu.PrefetchScalarGridSpec(
            num_scalar_prefetch=4,
            grid=(1,),
            in_specs=[
                tall,
                flat,
                tall,
                flat,
                pl.BlockSpec((TILE, length), first),
                rows,
                rows,
                tall_window,
                pl.BlockSpec((own, window), lambda i, *_: (part, 0)),
                tall_window,
                pl.BlockSpec((window, TILE), first),
            ],
            out_specs=[
                pl.BlockSpec((length, 3 * own), first),
                pl.BlockSpec((window - length, 2 * own), first),
            ],
            scratch_shapes=[
                pltpu.VMEM((own, length), F32),
                pltpu.VMEM((window, own), F32),
                pltpu.VMEM((window, own), F32),
            ],
        ),
        out_shape=[
            jax.ShapeDtypeStruct((length, 3 * own), BF),
            jax.ShapeDtypeStruct((window - length, 2 * own), BF),
        ],
        compiler_params=pltpu.CompilerParams(vmem_limit_bytes=60 * VMEM_MIB),
        name="attend_back",
    )(
        *pair_list, seq.reshape(1).astype(jnp.int32), queries, queries_t, grads, grads_t, one_t, lse.reshape(parts, heads, length),
        delta.reshape(parts, heads, length), keys, keys_t, values, aux,
    )


def setup_kernel(
    lengths_ref, seq_ref, aux_ref, onet_ref, spread_ref, lo_ref, hi_ref, kt_ref, qt_ref, count_ref
):
    window, length = aux_ref.shape[0], spread_ref.shape[0]
    far = window - length
    seq = seq_ref[0]
    passages = lengths_ref.shape[1]
    ends, total = [], jnp.int32(0)
    for p in range(passages):
        total = total + lengths_ref[0, p]
        ends.append(total)
    window_start, own_start = seq * far, seq * length

    def segments(positions):
        found = jnp.zeros(positions.shape, jnp.int32)
        for end in ends:
            found = found + jnp.where(positions >= end, 1, 0)
        return found

    lane = lax.broadcasted_iota(jnp.int32, (TILE, TILE), 1)
    row = lax.broadcasted_iota(jnp.int32, (TILE, TILE), 0)

    def window_tile(i, carry):
        rows = pl.ds(pl.multiple_of(i * TILE, TILE), TILE)
        found = segments(window_start + i * TILE + row)
        apart = jnp.where((found != lane) & (lane <= passages), MASKED, 0.0)
        aux_ref[rows, :] = apart.astype(BF)
        return carry

    lax.fori_loop(0, window // TILE, window_tile, 0)

    def own_tile(i, carry):
        rows = pl.ds(pl.multiple_of(i * TILE, TILE), TILE)
        found = segments(own_start + i * TILE + row)
        same = (found == lane % 32) & (lane < 96) & (found < passages)
        spread_ref[rows, :] = jnp.where(same, 1.0, 0.0).astype(BF)
        found = segments(own_start + i * TILE + lane[:8])
        one = jnp.where(jnp.broadcast_to(found[:1], (TILE, TILE)) == row, 1.0, 0.0)
        onet_ref[:, rows] = one.astype(BF)
        return carry

    lax.fori_loop(0, length // TILE, own_tile, 0)

    def reach(first, low, high):
        begin, end = jnp.int32(0), jnp.int32(2 * length)
        for stop in ends:
            begin = jnp.where(stop <= first, stop, begin)
        for stop in reversed(ends):
            end = jnp.where(stop > first + TILE - 1, stop, end)
        begin = jnp.clip(begin, low, high) - low
        end = jnp.clip(end, low, high) - low
        return begin // TILE, (end + TILE - 1) // TILE

    for i in range(length // TILE):
        lo_ref[i], hi_ref[i] = reach(own_start + i * TILE, window_start, window_start + window)
    count = jnp.int32(0)
    for t in range(window // TILE):
        low, high = reach(window_start + t * TILE, own_start, own_start + length)

        def put(i, count):
            kt_ref[count] = t
            qt_ref[count] = i
            return count + 1

        count = lax.fori_loop(low, high, put, count)
    count_ref[0] = count


def setup(lengths, seq, length, window):
    tiles, window_tiles = length // TILE, window // TILE
    smem = pl.BlockSpec(memory_space=pltpu.SMEM)
    vmem = pl.BlockSpec(memory_space=pltpu.VMEM)
    number = lambda n: jax.ShapeDtypeStruct((n,), jnp.int32)
    return pl.pallas_call(
        setup_kernel,
        in_specs=[smem, smem],
        out_specs=[vmem] * 3 + [smem] * 5,
        out_shape=[
            jax.ShapeDtypeStruct((window, TILE), BF),
            jax.ShapeDtypeStruct((TILE, length), BF),
            jax.ShapeDtypeStruct((length, TILE), BF),
            number(tiles),
            number(tiles),
            number(tiles * window_tiles),
            number(tiles * window_tiles),
            number(1),
        ],
        compiler_params=pltpu.CompilerParams(vmem_limit_bytes=60 * VMEM_MIB),
        name="setup",
    )(lengths, seq.reshape(1).astype(jnp.int32))


def own_kernel(place_ref, x_ref, wq_ref, wk_ref, wv_ref, vec_ref, q_ref, qt_ref, k_ref, kt_ref, v_ref, vt_ref, xt_ref):
    x = x_ref[...]
    q = ((dot(x, wq_ref[...]) + vec_ref[BIAS_Q : BIAS_Q + 1, :]) .astype(BF).astype(F32) * 0.125).astype(BF)
    q_ref[...] = q
    qt_ref[...] = q.T
    k = dot(x, wk_ref[...]).astype(BF)
    k_ref[...] = k
    kt_ref[...] = k.T
    v = (dot(x, wv_ref[...]) + vec_ref[BIAS_V : BIAS_V + 1, :]).astype(BF)
    v_ref[...] = v
    vt_ref[...] = v.T
    xt_ref[...] = x.T


def far_kernel(place_ref, x_ref, wk_ref, wv_ref, vec_ref, k_in, kt_in, v_in, vt_in, k_ref, kt_ref, v_ref, vt_ref):
    x = x_ref[...]
    k = dot(x, wk_ref[...]).astype(BF)
    k_ref[...] = k
    kt_ref[...] = k.T
    v = (dot(x, wv_ref[...]) + vec_ref[BIAS_V : BIAS_V + 1, :]).astype(BF)
    v_ref[...] = v
    vt_ref[...] = v.T


def project(x, x_far, wq, wk, wv, vectors, seq):
    length, features = x.shape
    far = x_far.shape[0]
    window = length + far
    rows = 256
    place = jnp.stack([seq * (far // rows), (1 - seq) * (length // rows)]).astype(jnp.int32)
    row = lambda i, place: (i, 0)
    col = lambda i, place: (0, i)
    whole = lambda i, place: (0, 0)
    once = pl.Buffered(1)
    weight = pl.BlockSpec((features, features), whole, pipeline_mode=once)
    vector = pl.BlockSpec(vectors.shape, whole, pipeline_mode=once)
    tall = jax.ShapeDtypeStruct((length, features), BF)
    flat = jax.ShapeDtypeStruct((features, length), BF)
    tall_window = jax.ShapeDtypeStruct((window, features), BF)
    flat_window = jax.ShapeDtypeStruct((features, window), BF)

    def window_blocks(which):
        down = pl.BlockSpec((rows, features), lambda i, place: (place[which] + i, 0))
        across = pl.BlockSpec((features, rows), lambda i, place: (0, place[which] + i))
        return [down, across, down, across]

    limit = pltpu.CompilerParams(vmem_limit_bytes=60 * VMEM_MIB)
    q, qt, k, kt, v, vt, xt = pl.pallas_call(
        own_kernel,
        grid_spec=pltpu.PrefetchScalarGridSpec(
            num_scalar_prefetch=1,
            grid=(length // rows,),
            in_specs=[pl.BlockSpec((rows, features), row), weight, weight, weight, vector],
            out_specs=[pl.BlockSpec((rows, features), row), pl.BlockSpec((features, rows), col)]
            + window_blocks(0)
            + [pl.BlockSpec((features, rows), col)],
        ),
        out_shape=[tall, flat, tall_window, flat_window, tall_window, flat_window, flat],
        compiler_params=limit,
        name="project_own",
    )(place, x, wq, wk, wv, vectors)
    anywhere = pl.BlockSpec(memory_space=pl.ANY)
    k, kt, v, vt = pl.pallas_call(
        far_kernel,
        grid_spec=pltpu.PrefetchScalarGridSpec(
            num_scalar_prefetch=1,
            grid=(far // rows,),
            in_specs=[pl.BlockSpec((rows, features), row), weight, weight, vector] + [anywhere] * 4,
            out_specs=window_blocks(1),
        ),
        out_shape=[tall_window, flat_window, tall_window, flat_window],
        input_output_aliases={5: 0, 6: 1, 7: 2, 8: 3},
        compiler_params=limit,
        name="project_far",
    )(place, x_far, wk, wv, vectors, k, kt, v, vt)
    return q, qt, k, kt, v, vt, xt


def loss_kernel(partners_ref, lengths_ref, place_ref, every_ref, pooled_ref, loss_ref, parts_ref):
    every = every_ref[...]
    count, features = every.shape
    own, _ = pooled_ref.shape
    first = place_ref[0] * own
    scores = 100.0 * dot(every, every, ((1,), (1,)))
    row = lax.broadcasted_iota(jnp.int32, (count, count), 0)
    lane = lax.broadcasted_iota(jnp.int32, (count, count), 1)
    scores = jnp.where(row == lane, BIG_NEG, scores)
    top = jnp.max(scores, 0, keepdims=True)
    log_sums = top + jnp.log(jnp.sum(jnp.exp(scores - top), 0, keepdims=True))
    mine = every_ref[pl.ds(pl.multiple_of(first, own), own), :]
    near = 100.0 * dot(mine, every, ((1,), (1,)))
    own_row = lax.broadcasted_iota(jnp.int32, (own, count), 0)
    own_lane = lax.broadcasted_iota(jnp.int32, (own, count), 1)
    near = jnp.where(own_row + first == own_lane, BIG_NEG, near)
    top = jnp.max(near, 1, keepdims=True)
    own_sums = top + jnp.log(jnp.sum(jnp.exp(near - top), 1, keepdims=True))
    target = jnp.concatenate(
        [jnp.where(own_lane[:1] == partners_ref[first + i], 1.0, 0.0) for i in range(own)], 0
    )
    picked = jnp.sum(jnp.where(target > 0.0, near, 0.0), 1, keepdims=True)
    loss_ref[...] = jnp.broadcast_to(own_sums - picked, loss_ref.shape)
    lane_row = own_lane[:1]

    def aim(n, held):
        return jnp.where(lane_row == n, partners_ref[n], held)

    aims = lax.fori_loop(0, count, aim, jnp.full((1, count), -1, jnp.int32))
    targeted = jnp.where(aims == own_row + first, 1.0, 0.0)
    both = jnp.exp(near - own_sums) - target + (jnp.exp(near - log_sums) - targeted)
    high, middle, low = split3(both)
    grad = 100.0 * (dot(high, every) + dot(middle, every) + dot(low, every))
    pooled = pooled_ref[...]
    inverse = lax.rsqrt(jnp.sum(pooled * pooled, 1, keepdims=True) + 1e-06)
    grad = inverse * grad - pooled * (inverse * inverse * inverse * jnp.sum(pooled * grad, 1, keepdims=True))
    sizes = jnp.concatenate(
        [jnp.full((1, features), lengths_ref[0, i].astype(F32), F32) for i in range(own)], 0
    )
    high, middle, low = split3(grad / sizes)
    parts_ref[...] = jnp.zeros(parts_ref.shape, BF)
    parts_ref[0:own, :] = high
    parts_ref[32 : 32 + own, :] = middle
    parts_ref[64 : 64 + own, :] = low


def contrast(partners, lengths, place, every, pooled):
    own, features = pooled.shape
    smem = pl.BlockSpec(memory_space=pltpu.SMEM)
    vmem = pl.BlockSpec(memory_space=pltpu.VMEM)
    return pl.pallas_call(
        loss_kernel,
        in_specs=[smem, smem, smem, vmem, vmem],
        out_specs=[vmem, vmem],
        out_shape=[jax.ShapeDtypeStruct((own, TILE), F32), jax.ShapeDtypeStruct((TILE, features), BF)],
        compiler_params=pltpu.CompilerParams(vmem_limit_bytes=60 * VMEM_MIB),
        name="contrast",
    )(partners, lengths, place.reshape(1).astype(jnp.int32), every, pooled)


def gelu_parts(u):
    size = jnp.abs(u)
    base = 1.0 + (0.3275911 * math.sqrt(0.5)) * size
    t = pl.reciprocal(base, approx=True)
    t = t * (2.0 - base * t)
    bell = jnp.exp(-0.5 * (u * u))
    poly = t * (0.127414796 + t * (-0.142248368 + t * (0.7107068705 + t * (-0.7265760135 + t * 0.5307027145))))
    tail = poly * bell
    below = jnp.where(u < 0.0, tail, 1.0 - tail)
    return u * below, below + u * bell * (1.0 / math.sqrt(2.0 * math.pi))


def normalized(resid):
    center = resid - jnp.mean(resid, -1, keepdims=True)
    scale = lax.rsqrt(jnp.mean(center * center, -1, keepdims=True) + EPS_NORM)
    return center * scale, scale


def feed_kernel(
    cb_ref, x_ref, member_ref, wo_ref, w1_ref, w2_ref, vec_ref,
    n1_ref, r1_ref, h_ref, f_ref, gp_ref, n2_ref, r2_ref, pool_ref,
):
    vector = lambda which: vec_ref[which : which + 1, :]
    attended = dot(cb_ref[...], wo_ref[...]) + vector(BIAS_O)
    unit, scale = normalized(x_ref[...].astype(F32) + attended)
    n1_ref[...] = unit.astype(BF)
    r1_ref[...] = scale
    hidden = unit * vector(GAIN_1) + vector(SHIFT_1)
    low = hidden.astype(BF)
    h_ref[...] = low.T
    resid = hidden + vector(BIAS_S)
    chunk = vec_ref.shape[1]
    for part in range(w1_ref.shape[1] // chunk):
        cols = slice(part * chunk, (part + 1) * chunk)
        u = dot(low, w1_ref[:, cols]) + vector(BIAS_E + part)
        active, slope = gelu_parts(u)
        active = active.astype(BF)
        f_ref[cols, :] = active.T
        gp_ref[:, cols] = slope.astype(BF)
        resid = resid + dot(active, w2_ref[cols, :])
    unit, scale = normalized(resid)
    n2_ref[...] = unit.astype(BF)
    r2_ref[...] = scale
    out = unit * vector(GAIN_2) + vector(SHIFT_2)
    high, middle, _ = split3(out)
    part = dot(member_ref[...], high) + dot(member_ref[...], middle)

    @pl.when(pl.program_id(0) == 0)
    def _():
        pool_ref[...] = part

    @pl.when(pl.program_id(0) > 0)
    def _():
        pool_ref[...] += part


def feed(cb, x, one_t, pass_count, wo, w1, w2, vectors):
    length, features = x.shape
    hidden = w1.shape[1]
    rows = 256
    row = lambda i: (i, 0)
    whole = lambda i: (0, 0)
    once = pl.Buffered(1)

    def full(array):
        return pl.BlockSpec(array.shape, whole, pipeline_mode=once)

    return pl.pallas_call(
        feed_kernel,
        grid=(length // rows,),
        in_specs=[
            pl.BlockSpec((rows, features), row),
            pl.BlockSpec((rows, features), row),
            pl.BlockSpec((pass_count, rows), lambda i: (0, i)),
        ]
        + [full(a) for a in (wo, w1, w2, vectors)],
        out_specs=[
            pl.BlockSpec((rows, features), row),
            pl.BlockSpec((rows, 1), row),
            pl.BlockSpec((features, rows), lambda i: (0, i)),
            pl.BlockSpec((hidden, rows), lambda i: (0, i)),
            pl.BlockSpec((rows, hidden), row),
            pl.BlockSpec((rows, features), row),
            pl.BlockSpec((rows, 1), row),
            pl.BlockSpec((pass_count, features), whole),
        ],
        out_shape=[
            jax.ShapeDtypeStruct((length, features), BF),
            jax.ShapeDtypeStruct((length, 1), F32),
            jax.ShapeDtypeStruct((features, length), BF),
            jax.ShapeDtypeStruct((hidden, length), BF),
            jax.ShapeDtypeStruct((length, hidden), BF),
            jax.ShapeDtypeStruct((length, features), BF),
            jax.ShapeDtypeStruct((length, 1), F32),
            jax.ShapeDtypeStruct((pass_count, features), F32),
        ],
        compiler_params=pltpu.CompilerParams(vmem_limit_bytes=60 * VMEM_MIB),
        name="feed",
    )(cb, x, one_t, wo, w1, w2, vectors)


def norm_back(grad, unit, scale, gain):
    wide = grad * gain
    return scale * (
        wide - jnp.mean(wide, -1, keepdims=True) - unit * jnp.mean(wide * unit, -1, keepdims=True)
    )


def add_rows(ref, row, value):
    ref[row : row + 1, :] += jnp.sum(value, 0, keepdims=True)


def start_back_kernel(spread_ref, pooled_ref, n2_ref, r2_ref, g2_ref, dr_ref, dy_ref, sums_ref):
    @pl.when(pl.program_id(0) == 0)
    def _():
        sums_ref[...] = jnp.zeros(sums_ref.shape, F32)

    grad = dot(spread_ref[...], pooled_ref[...])
    unit = n2_ref[...].astype(F32)
    add_rows(sums_ref, 0, grad * unit)
    add_rows(sums_ref, 1, grad)
    dr = norm_back(grad, unit, r2_ref[...], g2_ref[GAIN_2 : GAIN_2 + 1, :])
    dr_ref[...] = dr
    dy = dr.astype(BF)
    dy_ref[...] = dy
    add_rows(sums_ref, 2, dy.astype(F32))


def start_back(spread, pooled_parts, n2, r2, g2):
    length, features = n2.shape
    rows = 256
    row = lambda i: (i, 0)
    whole = lambda i: (0, 0)
    return pl.pallas_call(
        start_back_kernel,
        grid=(length // rows,),
        in_specs=[
            pl.BlockSpec((rows, spread.shape[1]), row),
            pl.BlockSpec(pooled_parts.shape, whole),
            pl.BlockSpec((rows, features), row),
            pl.BlockSpec((rows, 1), row),
            pl.BlockSpec(g2.shape, whole),
        ],
        out_specs=[
            pl.BlockSpec((rows, features), row),
            pl.BlockSpec((rows, features), row),
            pl.BlockSpec((8, features), whole),
        ],
        out_shape=[
            jax.ShapeDtypeStruct((length, features), F32),
            jax.ShapeDtypeStruct((length, features), BF),
            jax.ShapeDtypeStruct((8, features), F32),
        ],
        compiler_params=pltpu.CompilerParams(vmem_limit_bytes=60 * VMEM_MIB),
        name="start_back",
    )(spread, pooled_parts, n2, r2, g2)


def expand_back_kernel(dy_ref, gp_ref, w2_ref, du_ref, wide_sums_ref):
    @pl.when(pl.program_id(0) == 0)
    def _():
        wide_sums_ref[...] = jnp.zeros(wide_sums_ref.shape, F32)

    dy = dy_ref[...]
    chunk = 512
    for start in range(0, w2_ref.shape[0], chunk):
        cols = slice(start, start + chunk)
        slope = gp_ref[:, cols].astype(F32)
        du = (slope * dot(dy, w2_ref[cols, :], ((1,), (1,)))).astype(BF)
        du_ref[:, cols] = du
        wide_sums_ref[0:1, cols] += jnp.sum(du.astype(F32), 0, keepdims=True)


def expand_back(dy, gp, w2):
    length, features = dy.shape
    hidden = gp.shape[1]
    rows = 256
    row = lambda i: (i, 0)
    whole = lambda i: (0, 0)
    return pl.pallas_call(
        expand_back_kernel,
        grid=(length // rows,),
        in_specs=[
            pl.BlockSpec((rows, features), row),
            pl.BlockSpec((rows, hidden), row),
            pl.BlockSpec(w2.shape, whole, pipeline_mode=pl.Buffered(1)),
        ],
        out_specs=[pl.BlockSpec((rows, hidden), row), pl.BlockSpec((8, hidden), whole)],
        out_shape=[jax.ShapeDtypeStruct((length, hidden), BF), jax.ShapeDtypeStruct((8, hidden), F32)],
        compiler_params=pltpu.CompilerParams(vmem_limit_bytes=60 * VMEM_MIB),
        name="expand_back",
    )(dy, gp, w2)


def hidden_back_kernel(dr2_ref, du_ref, n1_ref, r1_ref, w1_ref, wo_ref, g1_ref, ct_ref, dr1_ref, da_ref, dc_ref, dct_ref, delta_ref, sums_ref):
    @pl.when(pl.program_id(0) == 0)
    def _():
        sums_ref[...] = jnp.zeros(sums_ref.shape, F32)

    dh = dr2_ref[...] + dot(du_ref[...], w1_ref[...], ((1,), (1,)))
    unit = n1_ref[...].astype(F32)
    add_rows(sums_ref, 0, dh * unit)
    add_rows(sums_ref, 1, dh)
    dr = norm_back(dh, unit, r1_ref[...], g1_ref[GAIN_1 : GAIN_1 + 1, :])
    dr1_ref[...] = dr
    da = dr.astype(BF)
    da_ref[...] = da
    add_rows(sums_ref, 2, da.astype(F32))
    dc_ref[...] = dot(da, wo_ref[...], ((1,), (1,))).astype(BF)
    dct = dot(wo_ref[...], da, ((1,), (1,))).astype(BF)
    dct_ref[...] = dct
    product = dct.astype(F32) * ct_ref[...]
    size = product.shape[0] // HEADS
    delta_ref[...] = jnp.concatenate(
        [jnp.sum(product[head * size : (head + 1) * size], 0, keepdims=True) for head in range(HEADS)], 0
    )


def hidden_back(dr2, du, n1, r1, w1, wo, g1, ct):
    length, features = dr2.shape
    hidden = du.shape[1]
    rows = 256
    row = lambda i: (i, 0)
    whole = lambda i: (0, 0)
    once = pl.Buffered(1)

    def full(array):
        return pl.BlockSpec(array.shape, whole, pipeline_mode=once)

    return pl.pallas_call(
        hidden_back_kernel,
        grid=(length // rows,),
        in_specs=[
            pl.BlockSpec((rows, features), row),
            pl.BlockSpec((rows, hidden), row),
            pl.BlockSpec((rows, features), row),
            pl.BlockSpec((rows, 1), row),
            full(w1),
            full(wo),
            full(g1),
            pl.BlockSpec((features, rows), lambda i: (0, i)),
        ],
        out_specs=[
            pl.BlockSpec((rows, features), row),
            pl.BlockSpec((rows, features), row),
            pl.BlockSpec((rows, features), row),
            pl.BlockSpec((features, rows), lambda i: (0, i)),
            pl.BlockSpec((HEADS, rows), lambda i: (0, i)),
            pl.BlockSpec((8, features), whole),
        ],
        out_shape=[
            jax.ShapeDtypeStruct((length, features), F32),
            jax.ShapeDtypeStruct((length, features), BF),
            jax.ShapeDtypeStruct((length, features), BF),
            jax.ShapeDtypeStruct((features, length), BF),
            jax.ShapeDtypeStruct((HEADS, length), F32),
            jax.ShapeDtypeStruct((8, features), F32),
        ],
        compiler_params=pltpu.CompilerParams(vmem_limit_bytes=60 * VMEM_MIB),
        name="hidden_back",
    )(dr2, du, n1, r1, w1, wo, g1, ct)


def swap_seq(array):
    return lax.ppermute(array, "seq", [(0, 1), (1, 0)])


def swap_dp(array, bit):
    count = lax.axis_size("dp")
    return lax.ppermute(array, "dp", [(i, i ^ (1 << bit)) for i in range(count)])


def swap_crossed(array, bits):
    count = lax.axis_size("dp")
    pairs = [(2 * i + s, 2 * (i ^ (1 << bits[s])) + s) for i in range(count) for s in range(2)]
    return lax.ppermute(array, ("dp", "seq"), pairs)


def pick_half(array, axis, which):
    half = array.shape[axis] // 2
    return lax.dynamic_slice_in_dim(array, which * half, half, axis)


def join(mine, other, axis, place):
    return jnp.where(
        place == 0, jnp.concatenate([mine, other], axis), jnp.concatenate([other, mine], axis)
    )


def halving_axis(shape):
    rows, cols = shape
    if rows % 32 == 0:
        return 0
    if cols % 256 == 0:
        return 1
    return 0


def add_far_kernel(place_ref, grads_ref, far_ref, out_ref, sums_ref):
    own = grads_ref.shape[1] // 3
    far = far_ref.shape[0]
    out_ref[...] = grads_ref[...]
    rows = pl.ds(pl.multiple_of((1 - place_ref[0]) * far, TILE), far)
    out_ref[rows, own:] = (grads_ref[rows, own:].astype(F32) + far_ref[...].astype(F32)).astype(BF)
    sums_ref[...] = jnp.broadcast_to(jnp.sum(out_ref[...].astype(F32), 0, keepdims=True), sums_ref.shape)


def add_far(seq, grads, far):
    smem, vmem = pl.BlockSpec(memory_space=pltpu.SMEM), pl.BlockSpec(memory_space=pltpu.VMEM)
    return pl.pallas_call(
        add_far_kernel,
        in_specs=[smem, vmem, vmem],
        out_specs=[vmem, vmem],
        out_shape=[jax.ShapeDtypeStruct(grads.shape, BF), jax.ShapeDtypeStruct((8, grads.shape[1]), F32)],
        compiler_params=pltpu.CompilerParams(vmem_limit_bytes=60 * VMEM_MIB),
        name="add_far",
    )(seq.reshape(1).astype(jnp.int32), grads, far)


def pack_kernel(sums2_ref, sums1_ref, wide_ref, *refs):
    biases, out_ref = refs[:-1], refs[-1]
    features = out_ref.shape[1]
    out_ref[...] = jnp.zeros(out_ref.shape, F32)
    out_ref[0:3, :] = sums2_ref[0:3, :]
    out_ref[3:6, :] = sums1_ref[0:3, :]
    for part, bias in enumerate(biases):
        own = bias.shape[1] // 3
        cols = slice(part * own, (part + 1) * own)
        out_ref[6:7, cols] = bias[0:1, :own]
        out_ref[7:8, cols] = bias[0:1, 2 * own :]
    for row in range(wide_ref.shape[1] // features):
        out_ref[8 + row : 9 + row, :] = wide_ref[0:1, row * features : (row + 1) * features]


def pack_sums(sums2, sums1, wide_sums, bias_sums):
    rows = -(-(8 + wide_sums.shape[1] // sums2.shape[1]) // 8) * 8
    return pl.pallas_call(
        pack_kernel,
        out_shape=jax.ShapeDtypeStruct((rows, sums2.shape[1]), F32),
        compiler_params=pltpu.CompilerParams(vmem_limit_bytes=60 * VMEM_MIB),
        name="pack_sums",
    )(sums2, sums1, wide_sums, *bias_sums)


def tokens_kernel(parts, *refs):
    grads, weights, (first_ref, out_ref) = refs[:parts], refs[parts : parts + 3], refs[parts + 3 :]
    total = first_ref[...]
    for part in range(parts):
        own = grads[part].shape[1] // 3
        for which in range(3):
            total = total + dot(
                grads[part][:, which * own : (which + 1) * own],
                weights[which][:, part * own : (part + 1) * own],
                ((1,), (1,)),
            )
    out_ref[...] = total


def tokens_back(grads, weights, first):
    length, features = first.shape
    rows = 256
    row = lambda i: (i, 0)
    whole = lambda i: (0, 0)
    return pl.pallas_call(
        functools.partial(tokens_kernel, len(grads)),
        grid=(length // rows,),
        in_specs=[pl.BlockSpec((rows, grad.shape[1]), row) for grad in grads]
        + [pl.BlockSpec(weight.shape, whole, pipeline_mode=pl.Buffered(1)) for weight in weights]
        + [pl.BlockSpec((rows, features), row)],
        out_specs=pl.BlockSpec((rows, features), row),
        out_shape=jax.ShapeDtypeStruct((length, features), F32),
        compiler_params=pltpu.CompilerParams(vmem_limit_bytes=60 * VMEM_MIB),
        name="tokens_back",
    )(*grads, *weights, first)


WIDE = 384


def products_kernel(kinds, place_ref, *refs):
    count = len(kinds)
    half = count // 2
    send_ref, keep_ref = refs[-2:]
    step = pl.program_id(0)
    block = jnp.where(step < half, 1 - place_ref[0], place_ref[0]) * half + step % half
    for left, right in sorted(set(kinds)):
        mine = functools.reduce(jnp.logical_or, [block == n for n in range(count) if kinds[n] == (left, right)])

        @pl.when(mine & (step < half))
        def _(left=left, right=right):
            send_ref[...] = dot(refs[left][...], refs[right][...]).astype(BF)

        @pl.when(mine & (step >= half))
        def _(left=left, right=right):
            keep_ref[...] = dot(refs[left][...], refs[right][...]).astype(BF)


def products(blocks, seq):
    count, half = len(blocks), len(blocks) // 2
    operands, specs, kinds = [], [], []

    def block_of(step, place):
        return jnp.where(step < half, 1 - place[0], place[0]) * half + step % half

    def place_operand(side, array, split):
        for n, held in enumerate(operands):
            if held is array:
                return n
        cuts = [pair[side][1] if pair[side][0] is array else 0 for pair in blocks]
        if split:
            shape = (WIDE, array.shape[1]) if side == 0 else (array.shape[0], WIDE)

            def index(step, place):
                block = block_of(step, place)
                cut = functools.reduce(lambda held, n: jnp.where(block == n, cuts[n], held), range(count), 0)
                return (cut, 0) if side == 0 else (0, cut)

            specs.append(pl.BlockSpec(shape, index))
        else:
            specs.append(pl.BlockSpec(array.shape, lambda step, place: (0, 0), pipeline_mode=pl.Buffered(1)))
        operands.append(array)
        return len(operands) - 1

    for (left, row), (right, col) in blocks:
        kinds.append((place_operand(0, left, row is not None), place_operand(1, right, col is not None)))
    height = blocks[0][0][0].shape[0]
    out = jax.ShapeDtypeStruct((half * height, WIDE), BF)
    return pl.pallas_call(
        functools.partial(products_kernel, kinds),
        grid_spec=pltpu.PrefetchScalarGridSpec(
            num_scalar_prefetch=1,
            grid=(count,),
            in_specs=specs,
            out_specs=[
                pl.BlockSpec((height, WIDE), lambda g, place: (jnp.minimum(g, half - 1), 0)),
                pl.BlockSpec((height, WIDE), lambda g, place: (jnp.maximum(g - half, 0), 0)),
            ],
        ),
        out_shape=[out, out],
        compiler_params=pltpu.CompilerParams(vmem_limit_bytes=60 * VMEM_MIB),
        name="products",
    )(seq.reshape(1).astype(jnp.int32), *operands)


def fold_kernel(parts, place_ref, keep_ref, other_ref, *out_refs):
    total = (keep_ref[...].astype(F32) + other_ref[...].astype(F32)).astype(BF)
    for m in range(parts):

        @pl.when(pl.program_id(0) == m)
        def _(m=m):
            out_refs[m][...] = total


def fold(keep, other, place, parts):
    rows, cols = keep.shape[0] // parts, keep.shape[1]
    picked = pl.BlockSpec((rows, cols), lambda m, place: (place[0] ^ m, 0))
    return pl.pallas_call(
        functools.partial(fold_kernel, parts),
        grid_spec=pltpu.PrefetchScalarGridSpec(
            num_scalar_prefetch=1,
            grid=(parts,),
            in_specs=[picked, picked],
            out_specs=[pl.BlockSpec((rows, cols), lambda m, place: (0, 0))] * parts,
        ),
        out_shape=[jax.ShapeDtypeStruct((rows, cols), BF)] * parts,
        compiler_params=pltpu.CompilerParams(vmem_limit_bytes=60 * VMEM_MIB),
        name="fold",
    )(place.reshape(1).astype(jnp.int32), keep, other)


def assemble_kernel(targets, place_ref, own_ref, other_ref, *out_refs):
    shards, rows = own_ref.shape[0], own_ref.shape[1]
    step = pl.program_id(0)
    mine = step // (len(targets) // 2) == place_ref[0]
    for ref, offset, here in ((own_ref, place_ref[1], mine), (other_ref, place_ref[2], jnp.logical_not(mine))):
        for outs in sorted(set(targets)):
            ours = functools.reduce(jnp.logical_or, [step == n for n in range(len(targets)) if targets[n] == outs])

            @pl.when(here & ours)
            def _(ref=ref, offset=offset, outs=outs):
                for shard in range(shards):
                    value = ref[shard ^ (offset & (shards - 1))].astype(F32)
                    at = 0
                    for out in outs:
                        width = out_refs[out].shape[1]
                        out_refs[out][shard * rows : (shard + 1) * rows, :] = value[:, at : at + width]
                        at += width


def assemble(own, other, places, shapes, targets):
    shards, rows, _ = own.shape
    count = len(targets)
    half = count // 2
    group = shards // half

    def shard_block(which):
        def index(step, place):
            here = (step // half == place[0]) == (which == 1)
            return (jnp.where(here, (step % half) ^ (place[which] // group), 0), 0, 0)

        return pl.BlockSpec((group, rows, WIDE), index)

    out_specs = []
    for out, shape in enumerate(shapes):
        steps = [n for n in range(count) if out in targets[n]]

        def index(step, place, steps=steps):
            return (0, sum((jnp.where(step >= n, 1, 0) for n in steps[1:]), jnp.int32(0)))

        out_specs.append(pl.BlockSpec((shape[0], shape[1] // len(steps)), index))
    return pl.pallas_call(
        functools.partial(assemble_kernel, targets),
        grid_spec=pltpu.PrefetchScalarGridSpec(
            num_scalar_prefetch=1,
            grid=(count,),
            in_specs=[shard_block(1), shard_block(2)],
            out_specs=out_specs,
        ),
        out_shape=[jax.ShapeDtypeStruct(shape, F32) for shape in shapes],
        compiler_params=pltpu.CompilerParams(vmem_limit_bytes=60 * VMEM_MIB),
        name="assemble",
    )(jnp.stack(places).astype(jnp.int32), own, other)


class GradTotal:
    steps = 8

    def __init__(self, blocks):
        self.place(0)
        send, self.keep = products(blocks, self.seq)
        self.out = [send]

    def place(self, step):
        seq, dp = lax.axis_index("seq"), lax.axis_index("dp")
        self.step, self.seq, self.far = step, seq, (dp >> 2) & 3
        self.near = ((dp >> seq) & 1, (dp >> (1 - seq)) & 1)

    @classmethod
    def resumed(cls, step, out, got):
        total = cls.__new__(cls)
        total.place(step)
        total.out, total.got = list(out), list(got)
        return total

    def offset(self, seq):
        dp = lax.axis_index("dp")
        return ((dp >> seq) & 1) * 8 + ((dp >> (1 - seq)) & 1) * 4 + ((dp >> 2) & 3)

    def prepare(self):
        step = self.step
        if step in (1, 2):
            self.keep, *self.out = fold(self.keep, self.got[0], self.near[step - 1], 2)
        elif step == 3:
            self.keep, *self.out = fold(self.keep, self.got[0], self.far, 4)
        elif step == 4:
            total = self.keep.astype(F32)
            for other in self.got:
                total = total + other.astype(F32)
            self.out = [total.astype(BF)]
        elif step == 5:
            self.out = [jnp.stack(self.out + self.got)]
        elif step > 5:
            self.out = [jnp.concatenate(self.out + self.got)]

    def exchange(self):
        step, count = self.step, lax.axis_size("dp")
        if step in (0, 7):
            self.got = [swap_seq(self.out[0])]
        elif step in (1, 6):
            self.got = [swap_crossed(self.out[0], (0, 1))]
        elif step in (2, 5):
            self.got = [swap_crossed(self.out[0], (1, 0))]
        else:
            sends = self.out if step == 3 else self.out * 3
            self.got = [
                lax.ppermute(send, "dp", [(i, i ^ (m << 2)) for i in range(count)])
                for m, send in zip((1, 2, 3), sends)
            ]
        self.step += 1

    def done(self):
        return self.step == self.steps

    def whole(self, shapes, targets):
        places = [self.seq, self.offset(self.seq), self.offset(1 - self.seq)]
        return assemble(self.out[0], self.got[0], places, shapes, targets)


def plain_total(partial):
    seq, index = lax.axis_index("seq"), lax.axis_index("dp")
    block = (pick_half(partial, 0, seq).astype(F32) + swap_seq(pick_half(partial, 0, 1 - seq)).astype(F32)).astype(BF)
    steps = []
    for bit in range(int(math.log2(lax.axis_size("dp")))):
        place, axis = (index >> bit) & 1, halving_axis(block.shape)
        steps.append((bit, place, axis))
        other = swap_dp(pick_half(block, axis, 1 - place), bit)
        block = (pick_half(block, axis, place).astype(F32) + other.astype(F32)).astype(BF)
    for bit, place, axis in reversed(steps):
        block = join(block, swap_dp(block, bit), axis, place)
    return join(block, swap_seq(block), 0, seq).astype(F32)


class Swap:
    def __init__(self, array):
        self.out, self.step = [array], 0

    def prepare(self):
        pass

    def exchange(self):
        self.got = [swap_seq(self.out[0])]
        self.step = 1

    def done(self):
        return self.step == 1


class Small:
    def __init__(self, partial):
        self.block, self.step = partial, 0
        self.steps = 1 + int(math.log2(lax.axis_size("dp")))

    def prepare(self):
        if self.step:
            self.block = self.block + self.got[0]
        self.out = [self.block]

    def exchange(self):
        block = self.out[0]
        self.block = block
        self.got = [swap_seq(block) if self.step == 0 else swap_dp(block, self.step - 1)]
        self.step += 1

    def done(self):
        return self.step == self.steps

    def whole(self):
        return self.block + self.got[0]


def fence(*values):
    return lax.optimization_barrier(values)


def beside(sums, work, *inputs):
    live = [total for total in sums if not total.done()]
    for total in live:
        total.prepare()
    inputs, sends = fence(inputs, [total.out for total in live])
    for total, send in zip(live, sends):
        total.out = send
        total.exchange()
    result, received = fence(work(*inputs), [total.got for total in live])
    for total, got in zip(live, received):
        total.got = got
    return result


def body(
    tokens, lengths, partners, query_proj, query_bias, key_proj, value_proj, value_bias, output_proj, output_bias,
    first_gain, first_shift, expand_proj, expand_bias, shrink_proj, shrink_bias, second_gain, second_shift,
):
    _, length, features = tokens.shape
    pass_count = lengths.shape[1]
    seq = lax.axis_index("seq")
    dp = lax.axis_index("dp")
    far = length // 2
    window = length + far
    x = tokens[0]

    x_far = swap_seq(lax.dynamic_slice_in_dim(x, (1 - seq) * far, far, 0))
    vectors = jnp.concatenate(
        [
            jnp.stack(
                [
                    output_bias, first_gain, first_shift, shrink_bias, second_gain, second_shift, query_bias, value_bias,
                ]
            ),
            expand_bias.reshape(-1, features),
        ]
    )
    aux, one_t, spread, key_lo, key_hi, *pair_list = setup(lengths, seq, length, window)
    queries, queries_t, keys, keys_t, values, values_t, x_t = project(
        x, x_far, query_proj, key_proj, value_proj, vectors, seq
    )
    context_low, context_t, context_low_t, lse = attend(queries_t, one_t, keys, values_t, aux, key_lo, key_hi)
    unit1, scale1, hidden_t, active_t, slope, unit2, scale2, pooled_part = feed(
        context_low, x, one_t, pass_count, output_proj, expand_proj, shrink_proj, vectors
    )

    lengths_wide = lengths.reshape(pass_count, 1).astype(F32)
    pooled = (pooled_part + swap_seq(pooled_part)) / lengths_wide
    inverse = lax.rsqrt(jnp.sum(pooled * pooled, -1, keepdims=True) + 1e-06)
    every = (pooled * inverse).astype(BF)
    for bit in range(int(math.log2(lax.axis_size("dp")))):
        every = join(every, swap_dp(every, bit), 0, (dp >> bit) & 1)
    passage_loss, pooled_parts = contrast(partners, lengths, dp, every, pooled)
    passage_loss = passage_loss[:, 0]

    grad_second, grad_shrunk, sums2 = start_back(spread, pooled_parts, unit2, scale2, vectors)
    fast = lax.axis_size("dp") == 16
    grad_shrink = dot(active_t, grad_shrunk).astype(BF)
    grad_expanded, wide_sums = expand_back(grad_shrunk, slope, shrink_proj)
    grad_expand = dot(hidden_t, grad_expanded).astype(BF)
    grad_second, grad_expanded, grad_shrink, grad_expand = fence(
        grad_second, grad_expanded, grad_shrink, grad_expand
    )
    shrink_total, expand_total = lax.psum((grad_shrink, grad_expand), ("dp", "seq"))
    grad_first, grad_attended, grad_context, grad_context_t, delta, sums1 = hidden_back(
        grad_second, grad_expanded, unit1, scale1, expand_proj, output_proj, vectors, context_t
    )
    sums = []
    parts, swaps, grads = 2, [], []
    for part in range(parts):

        def attention_work(grad_context):
            return attend_back(
                part, parts, seq, pair_list, queries, queries_t, grad_context, grad_context_t, one_t, lse, delta, keys,
                keys_t, values, aux,
            )

        near, far_part = beside(swaps[-1:], attention_work, grad_context)
        grads.append(near)
        swaps.append(Swap(far_part))
    early = [add_far(seq, near, swap.got[0]) for near, swap in zip(grads[:-1], swaps)]
    early = beside(swaps[-1:], lambda early: early, early)
    grads, bias_sums = zip(*early, add_far(seq, grads[-1], swaps[-1].got[0]))
    small = pack_sums(sums2, sums1, wide_sums, bias_sums)
    square = query_proj.shape
    own = features // parts

    def near_rounds(small, context_low_t, grad_attended, x_t, grad_first, *grads):
        small_sum = Small(small)
        sums, rest = [small_sum], ()
        if fast:
            late_sum = GradTotal(
                [((context_low_t, None), (grad_attended, n)) for n in range(parts)]
                + [((x_t, None), (grad, n)) for grad in grads for n in range(3)]
            )
            sums.append(late_sum)
        tokens_grad = beside(
            sums, lambda first, *grads: tokens_back(grads, (query_proj, key_proj, value_proj), first), grad_first, *grads
        )
        while not small_sum.done():
            beside(sums, lambda _: (), small)
        if fast:
            rest = (late_sum.out, late_sum.got)
        else:
            cut = lambda which: jnp.concatenate([grad[:, which * own : (which + 1) * own] for grad in grads], 1)
            rest = [
                plain_total(dot(left, right).astype(BF))
                for left, right in ((context_low_t, grad_attended), *((x_t, cut(n)) for n in range(3)))
            ]
        return small_sum.whole(), tokens_grad, rest

    def nothing(small, context_low_t, grad_attended, x_t, grad_first, *grads):
        if fast:
            shard = jnp.zeros((4 * parts * features // 32, own), BF)
            return small, grad_first, ([shard], [shard] * 3)
        return small, grad_first, [jnp.zeros(square, F32)] * 4

    small, tokens_grad, rest = lax.cond(
        lengths[0, 0] > 0, near_rounds, nothing, small, context_low_t, grad_attended, x_t, grad_first, *grads
    )
    tokens_grad = tokens_grad[None]
    if fast:
        late_sum = GradTotal.resumed(5, *rest)
        shrink_total = beside([late_sum], lambda total: total.astype(F32), shrink_total)
        expand_total = beside([late_sum], lambda total: total.astype(F32), expand_total)
        beside([late_sum], lambda _: (), expand_total)
        output_total, query_total, key_total, value_total = late_sum.whole(
            [square] * 4, [(0,)] * parts + [(1,), (2,), (3,)] * parts
        )
    else:
        shrink_total, expand_total = shrink_total.astype(F32), expand_total.astype(F32)
        output_total, query_total, key_total, value_total = rest
    return (
        passage_loss,
        tokens_grad,
        query_total,
        small[6],
        key_total,
        value_total,
        small[7],
        output_total,
        small[5],
        small[3],
        small[4],
        expand_total,
        small[8 : 8 + expand_bias.shape[0] // features].reshape(-1),
        shrink_total,
        small[2],
        small[0],
        small[1],
    )


def solution(mesh):
    placed = (P("dp", "seq", None), P("dp", None)) + (P(),) * 16
    return jax.shard_map(
        body,
        mesh=mesh,
        in_specs=placed,
        out_specs=(P("dp"), P("dp", "seq", None)) + (P(),) * 15,
        check_vma=False,
    )
```

```python
import functools
import math

import jax
import jax.numpy as jnp
from jax import lax
from jax.experimental import pallas as pl
from jax.experimental.pallas import tpu as pltpu
from jax.sharding import PartitionSpec as P

HEADS = 12
EPS_NORM = 1e-12
BIG_NEG = -1000000000.0
HIGH = lax.Precision.HIGHEST
BF = jnp.bfloat16
F32 = jnp.float32
TILE = 128
MASKED = -float(2**30)
BIAS_O, GAIN_1, SHIFT_1, BIAS_S, GAIN_2, SHIFT_2, BIAS_Q, BIAS_V = range(8)
VMEM_MIB = 1 << 20


def dot(left, right, over=((1,), (0,))):
    return lax.dot_general(left, right, (over, ((), ())), preferred_element_type=F32)


def split3(value):
    high = value.astype(BF)
    rest = value - high.astype(F32)
    middle = rest.astype(BF)
    low = (rest - middle.astype(F32)).astype(BF)
    return high, middle, low


def split_lanes(pair):
    row = lax.broadcasted_iota(jnp.int32, (TILE, 1), 0)
    first = jnp.where(row < TILE // 2, 1.0, 0.0).astype(BF)
    second = jnp.where(row < TILE // 2, 0.0, 1.0).astype(BF)
    return jnp.concatenate([pair * first, pair * second], 1)


def split_rows(pair):
    lane = lax.broadcasted_iota(jnp.int32, (1, TILE), 1)
    first = jnp.where(lane < TILE // 2, 1.0, 0.0).astype(BF)
    second = jnp.where(lane < TILE // 2, 0.0, 1.0).astype(BF)
    return jnp.concatenate([pair * first, pair * second], 0)


def lanes_to_rows(both):
    return jnp.concatenate([both[:, :TILE], both[:, TILE:]], 0)


def attend_kernel(
    lo_ref, hi_ref, qt_ref, onet_ref, k_ref, vt_ref, aux_ref, c_ref, ct_ref, ctb_ref, lse_ref, s_scr, q_scr, m_scr, o_scr
):
    lo, hi = lo_ref[pl.program_id(0)], hi_ref[pl.program_id(0)]
    pairs = k_ref.shape[1] // TILE
    m_scr[...] = jnp.full(m_scr.shape, 2.0 * MASKED, F32)
    o_scr[...] = jnp.zeros(o_scr.shape, F32)
    one = onet_ref[...]
    for j in range(pairs):
        q_scr[j, :TILE, :] = split_lanes(qt_ref[j * TILE : (j + 1) * TILE, :])
        q_scr[j, TILE:, :] = jnp.concatenate([one, one], 1)
    extra = o_scr.shape[1] - TILE
    row = lax.broadcasted_iota(jnp.int32, (extra, 2 * TILE), 0)
    lane = lax.broadcasted_iota(jnp.int32, (extra, 2 * TILE), 1)
    ones = jnp.where(row == lane // TILE, 1.0, 0.0).astype(BF)

    count = (hi - lo + 1) // 2
    lo = jnp.minimum(lo, k_ref.shape[0] // TILE - 2 * count)

    def scores(step, carry):
        start = pl.multiple_of((lo + 2 * step) * TILE, TILE)
        for half in range(2):
            rows = pl.ds(pl.multiple_of(start + half * TILE, TILE), TILE)
            aux = aux_ref[rows, :]
            for j in range(pairs):
                keys = jnp.concatenate([k_ref[rows, j * TILE : (j + 1) * TILE], aux], 1)
                s = dot(keys, q_scr[j])
                s_scr[2 * step + half, j] = s
                m_scr[j] = jnp.maximum(m_scr[j], jnp.max(s.reshape(TILE // 8, 8, 2 * TILE), 0))
        return carry

    lax.fori_loop(0, count, scores, 0)
    for j in range(pairs):
        m_scr[j] = jnp.broadcast_to(jnp.max(m_scr[j], 0, keepdims=True), (8, 2 * TILE))

    def weigh(step, carry):
        start = pl.multiple_of((lo + 2 * step) * TILE, TILE)
        for j in range(pairs):
            values, weights = [], []
            for half in range(2):
                cols = pl.ds(pl.multiple_of(start + half * TILE, TILE), TILE)
                p = jnp.exp(s_scr[2 * step + half, j] - m_scr[j, 0:1, :]).astype(BF)
                values.append(
                    jnp.concatenate([split_lanes(vt_ref[j * TILE : (j + 1) * TILE, cols]), ones], 0)
                )
                weights.append(lanes_to_rows(p))
            o_scr[j] += dot(jnp.concatenate(values, 1), jnp.concatenate(weights, 0))
        return carry

    lax.fori_loop(0, count, weigh, 0)
    half = TILE // 2
    for j in range(pairs):
        cols = slice(j * TILE, (j + 1) * TILE)
        total = o_scr[j, TILE : TILE + 2, :]
        inverse = 1.0 / total
        ct = jnp.concatenate(
            [o_scr[j, :half, :] * inverse[0:1], o_scr[j, half:TILE, :] * inverse[1:2]], 0
        )
        ct_ref[cols, :] = ct
        ctb_ref[cols, :] = ct.astype(BF)
        c_ref[:, cols] = ct.T.astype(BF)
        top = jnp.concatenate([m_scr[j, 0:1, :TILE], m_scr[j, 0:1, TILE:]], 0)
        lse_ref[2 * j : 2 * j + 2, :] = top + jnp.log(total)


def attend(queries_t, one_t, keys, values_t, aux, lo, hi):
    features, length = queries_t.shape
    window = keys.shape[0]
    pairs = features // TILE
    row = lambda i, *_: (i, 0)
    col = lambda i, *_: (0, i)
    whole = lambda i, *_: (0, 0)
    return pl.pallas_call(
        attend_kernel,
        grid_spec=pltpu.PrefetchScalarGridSpec(
            num_scalar_prefetch=2,
            grid=(length // TILE,),
            in_specs=[
                pl.BlockSpec((features, TILE), col),
                pl.BlockSpec((TILE, TILE), col),
                pl.BlockSpec((window, features), whole),
                pl.BlockSpec((features, window), whole),
                pl.BlockSpec((window, TILE), whole),
            ],
            out_specs=[
                pl.BlockSpec((TILE, features), row),
                pl.BlockSpec((features, TILE), col),
                pl.BlockSpec((features, TILE), col),
                pl.BlockSpec((2 * pairs, TILE), col),
            ],
            scratch_shapes=[
                pltpu.VMEM((window // TILE, pairs, TILE, 2 * TILE), F32),
                pltpu.VMEM((pairs, 2 * TILE, 2 * TILE), BF),
                pltpu.VMEM((pairs, 8, 2 * TILE), F32),
                pltpu.VMEM((pairs, TILE + 16, TILE), F32),
            ],
        ),
        out_shape=[
            jax.ShapeDtypeStruct((length, features), BF),
            jax.ShapeDtypeStruct((features, length), F32),
            jax.ShapeDtypeStruct((features, length), BF),
            jax.ShapeDtypeStruct((2 * pairs, length), F32),
        ],
        compiler_params=pltpu.CompilerParams(vmem_limit_bytes=60 * VMEM_MIB),
        name="attend",
    )(lo, hi, queries_t, one_t, keys, values_t, aux)


def attend_back_kernel(
    kt_ref, qt_list_ref, count_ref, place_ref, q_ref, qt_ref, dc_ref, dct_ref, onet_ref, lse_ref, delta_ref, k_ref, keys_t_ref,
    v_ref, aux_ref, grads_ref, far_ref, sums_ref, dqt_scr, dk_scr, dv_scr,
):
    pairs = q_ref.shape[1] // TILE
    dqt_scr[...] = jnp.zeros(dqt_scr.shape, F32)
    dk_scr[...] = jnp.zeros(dk_scr.shape, F32)
    dv_scr[...] = jnp.zeros(dv_scr.shape, F32)

    def tile(n):
        krows = pl.ds(pl.multiple_of(kt_ref[n] * TILE, TILE), TILE)
        rows = pl.ds(pl.multiple_of(qt_list_ref[n] * TILE, TILE), TILE)
        one = onet_ref[:, rows]
        ones = jnp.concatenate([one, one], 1)
        aux = aux_ref[krows, :]
        for j in range(pairs):
            cols = slice(j * TILE, (j + 1) * TILE)
            keys = jnp.concatenate([k_ref[krows, cols], aux], 1)
            queries_t = jnp.concatenate([split_lanes(qt_ref[cols, rows]), ones], 0)
            lse = jnp.concatenate([lse_ref[2 * j : 2 * j + 1, rows], lse_ref[2 * j + 1 : 2 * j + 2, rows]], 1)
            p = jnp.exp(dot(keys, queries_t) - lse)
            delta = jnp.concatenate([delta_ref[2 * j : 2 * j + 1, rows], delta_ref[2 * j + 1 : 2 * j + 2, rows]], 1)
            ds = (p * (dot(v_ref[krows, cols], split_lanes(dct_ref[cols, rows])) - delta)).astype(BF)
            dv_scr[krows, cols] += dot(p.astype(BF), split_rows(dc_ref[rows, cols]))
            dk_scr[krows, cols] += dot(ds, split_rows(q_ref[rows, cols]))
            dqt_scr[cols, rows] += dot(split_lanes(keys_t_ref[cols, krows]), lanes_to_rows(ds))

    count = count_ref[0]

    def two(step, carry):
        tile(2 * step)
        tile(2 * step + 1)
        return carry

    lax.fori_loop(0, count // 2, two, 0)

    @pl.when(count % 2 == 1)
    def _():
        tile(count - 1)

    length, own = q_ref.shape
    far = k_ref.shape[0] - length
    near_start = place_ref[0] * far
    far_rows = pl.ds(pl.multiple_of((1 - place_ref[0]) * length, TILE), far)
    grads_ref[far_rows, :own] = jnp.zeros((far, own), BF)
    grads_ref[:, own : 2 * own] = dk_scr[...].astype(BF)
    grads_ref[:, 2 * own :] = dv_scr[...].astype(BF)
    for i in range(length // TILE):
        rows = pl.ds(pl.multiple_of(near_start + i * TILE, TILE), TILE)
        for j in range(pairs):
            block = dqt_scr[j * TILE : (j + 1) * TILE, i * TILE : (i + 1) * TILE] * 0.125
            grads_ref[rows, j * TILE : (j + 1) * TILE] = block.T.astype(BF)
    far_ref[...] = grads_ref[far_rows, own:]
    sums_ref[...] = jnp.broadcast_to(jnp.sum(grads_ref[...].astype(F32), 0, keepdims=True), sums_ref.shape)


def attend_back(part, parts, seq, pair_list, queries, queries_t, grads, grads_t, one_t, lse, delta, keys, keys_t, values, aux):
    length, features = queries.shape
    window = keys.shape[0]
    own = features // parts
    heads = lse.shape[0] // parts
    tall = pl.BlockSpec((length, own), lambda i, *_: (0, part))
    flat = pl.BlockSpec((own, length), lambda i, *_: (part, 0))
    tall_window = pl.BlockSpec((window, own), lambda i, *_: (0, part))
    rows = pl.BlockSpec((None, heads, length), lambda i, *_: (part, 0, 0))
    first = lambda i, *_: (0, 0)
    return pl.pallas_call(
        attend_back_kernel,
        grid_spec=pltpu.PrefetchScalarGridSpec(
            num_scalar_prefetch=4,
            grid=(1,),
            in_specs=[
                tall,
                flat,
                tall,
                flat,
                pl.BlockSpec((TILE, length), first),
                rows,
                rows,
                tall_window,
                pl.BlockSpec((own, window), lambda i, *_: (part, 0)),
                tall_window,
                pl.BlockSpec((window, TILE), first),
            ],
            out_specs=[
                pl.BlockSpec((window, 3 * own), first),
                pl.BlockSpec((window - length, 2 * own), first),
                pl.BlockSpec((8, 3 * own), first),
            ],
            scratch_shapes=[
                pltpu.VMEM((own, length), F32),
                pltpu.VMEM((window, own), F32),
                pltpu.VMEM((window, own), F32),
            ],
        ),
        out_shape=[
            jax.ShapeDtypeStruct((window, 3 * own), BF),
            jax.ShapeDtypeStruct((window - length, 2 * own), BF),
            jax.ShapeDtypeStruct((8, 3 * own), F32),
        ],
        compiler_params=pltpu.CompilerParams(vmem_limit_bytes=60 * VMEM_MIB),
        name="attend_back",
    )(
        *pair_list, seq.reshape(1).astype(jnp.int32), queries, queries_t, grads, grads_t, one_t, lse.reshape(parts, heads, length),
        delta.reshape(parts, heads, length), keys, keys_t, values, aux,
    )


def setup_kernel(
    lengths_ref, seq_ref, *refs
):
    biases, (vec_ref, aux_ref, onet_ref, spread_ref, lo_ref, hi_ref, kt_ref, qt_ref, count_ref) = refs[:-9], refs[-9:]
    for row, bias in enumerate(biases):
        vec_ref[row : row + 1, :] = bias[...].reshape(1, -1)
    window, length = aux_ref.shape[0], spread_ref.shape[0]
    far = window - length
    seq = seq_ref[0]
    passages = lengths_ref.shape[1]
    ends, total = [], jnp.int32(0)
    for p in range(passages):
        total = total + lengths_ref[0, p]
        ends.append(total)
    window_start, own_start = seq * far, seq * length

    def segments(positions):
        found = jnp.zeros(positions.shape, jnp.int32)
        for end in ends:
            found = found + jnp.where(positions >= end, 1, 0)
        return found

    lane = lax.broadcasted_iota(jnp.int32, (TILE, TILE), 1)
    row = lax.broadcasted_iota(jnp.int32, (TILE, TILE), 0)

    def window_tile(i, carry):
        found = segments(window_start + i * TILE + row)
        apart = jnp.where((found != lane) & (lane <= passages), MASKED, 0.0)
        aux_ref[pl.ds(pl.multiple_of(i * TILE, TILE), TILE), :] = apart.astype(BF)
        own = i - seq * (far // TILE)

        @pl.when((own >= 0) & (own < length // TILE))
        def _():
            rows = pl.ds(pl.multiple_of(own * TILE, TILE), TILE)
            same = (found == lane % 32) & (lane < 96) & (found < passages)
            spread_ref[rows, :] = jnp.where(same, 1.0, 0.0).astype(BF)
            across = segments(own_start + own * TILE + lane[:8])
            one = jnp.where(jnp.broadcast_to(across[:1], (TILE, TILE)) == row, 1.0, 0.0)
            onet_ref[:, rows] = one.astype(BF)

        return carry

    lax.fori_loop(0, window // TILE, window_tile, 0)

    def reach(first, low, high):
        begin, end = jnp.int32(0), jnp.int32(2 * length)
        for stop in ends:
            begin = jnp.where(stop <= first, stop, begin)
        for stop in reversed(ends):
            end = jnp.where(stop > first + TILE - 1, stop, end)
        begin = jnp.clip(begin, low, high) - low
        end = jnp.clip(end, low, high) - low
        return begin // TILE, (end + TILE - 1) // TILE

    for i in range(length // TILE):
        lo_ref[i], hi_ref[i] = reach(own_start + i * TILE, window_start, window_start + window)
    count = jnp.int32(0)
    for t in range(window // TILE):
        low, high = reach(window_start + t * TILE, own_start, own_start + length)

        def put(i, count):
            kt_ref[count] = t
            qt_ref[count] = i
            return count + 1

        count = lax.fori_loop(low, high, put, count)
    count_ref[0] = count


def setup(lengths, seq, length, window, vectors):
    tiles, window_tiles = length // TILE, window // TILE
    smem = pl.BlockSpec(memory_space=pltpu.SMEM)
    vmem = pl.BlockSpec(memory_space=pltpu.VMEM)
    number = lambda n: jax.ShapeDtypeStruct((n,), jnp.int32)
    return pl.pallas_call(
        setup_kernel,
        in_specs=[smem, smem] + [vmem] * len(vectors),
        out_specs=[vmem] * 4 + [smem] * 5,
        out_shape=[
            jax.ShapeDtypeStruct((len(vectors), vectors[0].shape[0]), F32),
            jax.ShapeDtypeStruct((window, TILE), BF),
            jax.ShapeDtypeStruct((TILE, length), BF),
            jax.ShapeDtypeStruct((length, TILE), BF),
            number(tiles),
            number(tiles),
            number(tiles * window_tiles),
            number(tiles * window_tiles),
            number(1),
        ],
        compiler_params=pltpu.CompilerParams(vmem_limit_bytes=60 * VMEM_MIB),
        name="setup",
    )(lengths, seq.reshape(1).astype(jnp.int32), *vectors)


def own_kernel(place_ref, x_ref, wq_ref, wk_ref, wv_ref, vec_ref, q_ref, qt_ref, k_ref, kt_ref, v_ref, vt_ref, xt_ref):
    x = x_ref[...]
    q = ((dot(x, wq_ref[...]) + vec_ref[BIAS_Q : BIAS_Q + 1, :]) .astype(BF).astype(F32) * 0.125).astype(BF)
    q_ref[...] = q
    qt_ref[...] = q.T
    k = dot(x, wk_ref[...]).astype(BF)
    k_ref[...] = k
    kt_ref[...] = k.T
    v = (dot(x, wv_ref[...]) + vec_ref[BIAS_V : BIAS_V + 1, :]).astype(BF)
    v_ref[...] = v
    vt_ref[...] = v.T
    xt_ref[...] = x.T


def far_kernel(
    place_ref, x_ref, wk_ref, wv_ref, vec_ref, k_in, kt_in, v_in, vt_in, xt_in, k_ref, kt_ref, v_ref, vt_ref, xt_ref
):
    x = x_ref[...]
    k = dot(x, wk_ref[...]).astype(BF)
    k_ref[...] = k
    kt_ref[...] = k.T
    v = (dot(x, wv_ref[...]) + vec_ref[BIAS_V : BIAS_V + 1, :]).astype(BF)
    v_ref[...] = v
    vt_ref[...] = v.T
    xt_ref[...] = x.T


def project(x, x_far, wq, wk, wv, vectors, seq):
    length, features = x.shape
    far = x_far.shape[0]
    window = length + far
    rows = 256
    place = jnp.stack([seq * (far // rows), (1 - seq) * (length // rows)]).astype(jnp.int32)
    row = lambda i, place: (i, 0)
    col = lambda i, place: (0, i)
    whole = lambda i, place: (0, 0)
    once = pl.Buffered(1)
    weight = pl.BlockSpec((features, features), whole, pipeline_mode=once)
    vector = pl.BlockSpec(vectors.shape, whole, pipeline_mode=once)
    tall = jax.ShapeDtypeStruct((length, features), BF)
    flat = jax.ShapeDtypeStruct((features, length), BF)
    tall_window = jax.ShapeDtypeStruct((window, features), BF)
    flat_window = jax.ShapeDtypeStruct((features, window), BF)

    def window_blocks(which):
        down = pl.BlockSpec((rows, features), lambda i, place: (place[which] + i, 0))
        across = pl.BlockSpec((features, rows), lambda i, place: (0, place[which] + i))
        return [down, across, down, across, across]

    limit = pltpu.CompilerParams(vmem_limit_bytes=60 * VMEM_MIB)
    q, qt, k, kt, v, vt, xt = pl.pallas_call(
        own_kernel,
        grid_spec=pltpu.PrefetchScalarGridSpec(
            num_scalar_prefetch=1,
            grid=(length // rows,),
            in_specs=[pl.BlockSpec((rows, features), row), weight, weight, weight, vector],
            out_specs=[pl.BlockSpec((rows, features), row), pl.BlockSpec((features, rows), col)]
            + window_blocks(0),
        ),
        out_shape=[tall, flat, tall_window, flat_window, tall_window, flat_window, flat_window],
        compiler_params=limit,
        name="project_own",
    )(place, x, wq, wk, wv, vectors)
    anywhere = pl.BlockSpec(memory_space=pl.ANY)
    k, kt, v, vt, xt = pl.pallas_call(
        far_kernel,
        grid_spec=pltpu.PrefetchScalarGridSpec(
            num_scalar_prefetch=1,
            grid=(far // rows,),
            in_specs=[pl.BlockSpec((rows, features), row), weight, weight, vector] + [anywhere] * 5,
            out_specs=window_blocks(1),
        ),
        out_shape=[tall_window, flat_window, tall_window, flat_window, flat_window],
        input_output_aliases={5: 0, 6: 1, 7: 2, 8: 3, 9: 4},
        compiler_params=limit,
        name="project_far",
    )(place, x_far, wk, wv, vectors, k, kt, v, vt, xt)
    return q, qt, k, kt, v, vt, xt


def loss_kernel(partners_ref, lengths_ref, place_ref, given_ref, pooled_ref, loss_ref, parts_ref, every_ref):
    own, _ = pooled_ref.shape
    for n in range(given_ref.shape[0] // own):
        every_ref[n * own : (n + 1) * own, :] = given_ref[
            pl.ds(pl.multiple_of((place_ref[0] ^ n) * own, own), own), :
        ]
    every = every_ref[...]
    count, features = every.shape
    first = place_ref[0] * own
    scores = 100.0 * dot(every, every, ((1,), (1,)))
    row = lax.broadcasted_iota(jnp.int32, (count, count), 0)
    lane = lax.broadcasted_iota(jnp.int32, (count, count), 1)
    scores = jnp.where(row == lane, BIG_NEG, scores)
    top = jnp.max(scores, 0, keepdims=True)
    log_sums = top + jnp.log(jnp.sum(jnp.exp(scores - top), 0, keepdims=True))
    mine = every_ref[pl.ds(pl.multiple_of(first, own), own), :]
    near = 100.0 * dot(mine, every, ((1,), (1,)))
    own_row = lax.broadcasted_iota(jnp.int32, (own, count), 0)
    own_lane = lax.broadcasted_iota(jnp.int32, (own, count), 1)
    near = jnp.where(own_row + first == own_lane, BIG_NEG, near)
    top = jnp.max(near, 1, keepdims=True)
    own_sums = top + jnp.log(jnp.sum(jnp.exp(near - top), 1, keepdims=True))
    target = jnp.concatenate(
        [jnp.where(own_lane[:1] == partners_ref[first + i], 1.0, 0.0) for i in range(own)], 0
    )
    picked = jnp.sum(jnp.where(target > 0.0, near, 0.0), 1, keepdims=True)
    loss_ref[...] = jnp.broadcast_to(own_sums - picked, loss_ref.shape)
    lane_row = own_lane[:1]

    def aim(n, held):
        return jnp.where(lane_row == n, partners_ref[n], held)

    aims = lax.fori_loop(0, count, aim, jnp.full((1, count), -1, jnp.int32))
    targeted = jnp.where(aims == own_row + first, 1.0, 0.0)
    both = jnp.exp(near - own_sums) - target + (jnp.exp(near - log_sums) - targeted)
    high, middle, low = split3(both)
    grad = 100.0 * (dot(high, every) + dot(middle, every) + dot(low, every))
    pooled = pooled_ref[...]
    inverse = lax.rsqrt(jnp.sum(pooled * pooled, 1, keepdims=True) + 1e-06)
    grad = inverse * grad - pooled * (inverse * inverse * inverse * jnp.sum(pooled * grad, 1, keepdims=True))
    sizes = jnp.concatenate(
        [jnp.full((1, features), lengths_ref[0, i].astype(F32), F32) for i in range(own)], 0
    )
    high, middle, low = split3(grad / sizes)
    parts_ref[...] = jnp.zeros(parts_ref.shape, BF)
    parts_ref[0:own, :] = high
    parts_ref[32 : 32 + own, :] = middle
    parts_ref[64 : 64 + own, :] = low


def contrast(partners, lengths, place, every, pooled):
    own, features = pooled.shape
    smem = pl.BlockSpec(memory_space=pltpu.SMEM)
    vmem = pl.BlockSpec(memory_space=pltpu.VMEM)
    return pl.pallas_call(
        loss_kernel,
        in_specs=[smem, smem, smem, vmem, vmem],
        out_specs=[vmem, vmem],
        out_shape=[jax.ShapeDtypeStruct((own, TILE), F32), jax.ShapeDtypeStruct((TILE, features), BF)],
        scratch_shapes=[pltpu.VMEM(every.shape, BF)],
        compiler_params=pltpu.CompilerParams(vmem_limit_bytes=60 * VMEM_MIB),
        name="contrast",
    )(partners, lengths, place.reshape(1).astype(jnp.int32), every, pooled)


def gelu_parts(u):
    size = jnp.abs(u)
    base = 1.0 + (0.3275911 * math.sqrt(0.5)) * size
    t = pl.reciprocal(base, approx=True)
    t = t * (2.0 - base * t)
    bell = jnp.exp(-0.5 * (u * u))
    poly = t * (0.127414796 + t * (-0.142248368 + t * (0.7107068705 + t * (-0.7265760135 + t * 0.5307027145))))
    tail = poly * bell
    below = jnp.where(u < 0.0, tail, 1.0 - tail)
    return u * below, below + u * bell * (1.0 / math.sqrt(2.0 * math.pi))


def normalized(resid):
    center = resid - jnp.mean(resid, -1, keepdims=True)
    scale = lax.rsqrt(jnp.mean(center * center, -1, keepdims=True) + EPS_NORM)
    return center * scale, scale


def feed_kernel(
    cb_ref, x_ref, member_ref, wo_ref, vec_ref, be_ref, w1_ref, w2_ref,
    n1_ref, r1_ref, h_ref, n2_ref, r2_ref, pool_ref, f_ref, gp_ref, low_scr, resid_scr,
):
    vector = lambda which: vec_ref[which : which + 1, :]
    length = cb_ref.shape[0]
    rows = 256

    @pl.when(pl.program_id(0) == 0)
    def _():
        for start in range(0, length, rows):
            at = slice(start, start + rows)
            attended = dot(cb_ref[at, :], wo_ref[...]) + vector(BIAS_O)
            unit, scale = normalized(x_ref[at, :].astype(F32) + attended)
            n1_ref[at, :] = unit.astype(BF)
            r1_ref[at, :] = scale
            hidden = unit * vector(GAIN_1) + vector(SHIFT_1)
            low = hidden.astype(BF)
            low_scr[at, :] = low
            h_ref[:, at] = low.T
            resid_scr[at, :] = hidden + vector(BIAS_S)

    for start in range(0, length, rows):
        at = slice(start, start + rows)
        active, slope = gelu_parts(dot(low_scr[at, :], w1_ref[...]) + be_ref[...])
        active = active.astype(BF)
        f_ref[:, at] = active.T
        gp_ref[at, :] = slope.astype(BF)
        resid_scr[at, :] += dot(active, w2_ref[...])

    @pl.when(pl.program_id(0) == pl.num_programs(0) - 1)
    def _():
        part = jnp.zeros(pool_ref.shape, F32)
        for start in range(0, length, rows):
            at = slice(start, start + rows)
            unit, scale = normalized(resid_scr[at, :])
            n2_ref[at, :] = unit.astype(BF)
            r2_ref[at, :] = scale
            high, middle, _ = split3(unit * vector(GAIN_2) + vector(SHIFT_2))
            members = member_ref[:, at]
            part = part + dot(members, high) + dot(members, middle)
        pool_ref[...] = part


def feed(cb, x, one_t, pass_count, wo, w1, w2, vectors, expand_bias):
    length, features = x.shape
    hidden = w1.shape[1]
    chunk = 512
    row = lambda i: (i, 0)
    col = lambda i: (0, i)
    whole = lambda i: (0, 0)

    def full(array, shape=None):
        return pl.BlockSpec(shape or array.shape, whole, pipeline_mode=pl.Buffered(1))

    return pl.pallas_call(
        feed_kernel,
        grid=(hidden // chunk,),
        in_specs=[full(cb), full(x), full(one_t, (pass_count, length)), full(wo), full(vectors)]
        + [
            pl.BlockSpec((1, chunk), col),
            pl.BlockSpec((features, chunk), col),
            pl.BlockSpec((chunk, features), row),
        ],
        out_specs=[
            pl.BlockSpec((length, features), whole),
            pl.BlockSpec((length, 1), whole),
            pl.BlockSpec((features, length), whole),
            pl.BlockSpec((length, features), whole),
            pl.BlockSpec((length, 1), whole),
            pl.BlockSpec((pass_count, features), whole),
            pl.BlockSpec((chunk, length), row),
            pl.BlockSpec((length, chunk), col),
        ],
        out_shape=[
            jax.ShapeDtypeStruct((length, features), BF),
            jax.ShapeDtypeStruct((length, 1), F32),
            jax.ShapeDtypeStruct((features, length), BF),
            jax.ShapeDtypeStruct((length, features), BF),
            jax.ShapeDtypeStruct((length, 1), F32),
            jax.ShapeDtypeStruct((pass_count, features), F32),
            jax.ShapeDtypeStruct((hidden, length), BF),
            jax.ShapeDtypeStruct((length, hidden), BF),
        ],
        scratch_shapes=[pltpu.VMEM((length, features), BF), pltpu.VMEM((length, features), F32)],
        compiler_params=pltpu.CompilerParams(vmem_limit_bytes=60 * VMEM_MIB),
        name="feed",
    )(cb, x, one_t, wo, vectors, expand_bias.reshape(1, -1), w1, w2)


def norm_back(grad, unit, scale, gain):
    wide = grad * gain
    return scale * (
        wide - jnp.mean(wide, -1, keepdims=True) - unit * jnp.mean(wide * unit, -1, keepdims=True)
    )


def add_rows(ref, row, value):
    ref[row : row + 1, :] += jnp.sum(value, 0, keepdims=True)


def feed_grads_kernel(
    spread_ref, pooled_ref, n2_ref, r2_ref, vec_ref, ht_ref, w2_ref, gp_ref, ft_ref,
    dy_ref, sums_ref, shrink_ref, expand_ref, du_ref, wide_sums_ref,
):
    rows = 256
    tiles = dy_ref.shape[0] // rows

    @pl.when(pl.program_id(0) == 0)
    def _():
        sums_ref[...] = jnp.zeros(sums_ref.shape, F32)
        for i in range(tiles):
            at = slice(i * rows, (i + 1) * rows)
            grad = dot(spread_ref[at, :], pooled_ref[...])
            unit = n2_ref[at, :].astype(F32)
            add_rows(sums_ref, 0, grad * unit)
            add_rows(sums_ref, 1, grad)
            dy = norm_back(grad, unit, r2_ref[at, :], vec_ref[GAIN_2 : GAIN_2 + 1, :]).astype(BF)
            dy_ref[at, :] = dy
            add_rows(sums_ref, 2, dy.astype(F32))

    total = jnp.zeros((1, du_ref.shape[1]), F32)
    for i in range(0, tiles, 2):
        at = slice(i * rows, (i + 2) * rows)
        du = (gp_ref[at, :].astype(F32) * dot(dy_ref[at, :], w2_ref[...], ((1,), (1,)))).astype(BF)
        du_ref[at, :] = du
        total = total + jnp.sum(du.astype(F32), 0, keepdims=True)
    wide_sums_ref[...] = jnp.broadcast_to(total, wide_sums_ref.shape)
    expand_ref[...] = dot(ht_ref[...], du_ref[...]).astype(BF)
    shrink_ref[...] = dot(ft_ref[...], dy_ref[...]).astype(BF)


def feed_grads(spread, pooled_parts, n2, r2, vectors, ht, w2, gp, ft):
    length, features = n2.shape
    hidden = gp.shape[1]
    chunk = 512
    row = lambda i: (i, 0)
    col = lambda i: (0, i)
    whole = lambda i: (0, 0)

    def full(array):
        return pl.BlockSpec(array.shape, whole, pipeline_mode=pl.Buffered(1))

    return pl.pallas_call(
        feed_grads_kernel,
        grid=(hidden // chunk,),
        in_specs=[full(a) for a in (spread, pooled_parts, n2, r2, vectors, ht)]
        + [
            pl.BlockSpec((chunk, features), row),
            pl.BlockSpec((length, chunk), col),
            pl.BlockSpec((chunk, length), row),
        ],
        out_specs=[
            pl.BlockSpec((length, features), whole),
            pl.BlockSpec((8, features), whole),
            pl.BlockSpec((chunk, features), row),
            pl.BlockSpec((features, chunk), col),
            pl.BlockSpec((length, chunk), col),
            pl.BlockSpec((8, chunk), col),
        ],
        out_shape=[
            jax.ShapeDtypeStruct((length, features), BF),
            jax.ShapeDtypeStruct((8, features), F32),
            jax.ShapeDtypeStruct((hidden, features), BF),
            jax.ShapeDtypeStruct((features, hidden), BF),
            jax.ShapeDtypeStruct((length, hidden), BF),
            jax.ShapeDtypeStruct((8, hidden), F32),
        ],
        compiler_params=pltpu.CompilerParams(vmem_limit_bytes=60 * VMEM_MIB),
        name="feed_grads",
    )(spread, pooled_parts, n2, r2, vectors, ht, w2, gp, ft)


def hidden_back_kernel(
    dy_ref, du_ref, n1_ref, r1_ref, w1_ref, wo_ref, g1_ref, ct_ref, da_ref, dc_ref, dct_ref, delta_ref, sums_ref
):
    @pl.when(pl.program_id(0) == 0)
    def _():
        sums_ref[...] = jnp.zeros(sums_ref.shape, F32)

    dh = dy_ref[...].astype(F32) + dot(du_ref[...], w1_ref[...], ((1,), (1,)))
    unit = n1_ref[...].astype(F32)
    add_rows(sums_ref, 0, dh * unit)
    add_rows(sums_ref, 1, dh)
    dr = norm_back(dh, unit, r1_ref[...], g1_ref[GAIN_1 : GAIN_1 + 1, :])
    da = dr.astype(BF)
    da_ref[...] = da
    add_rows(sums_ref, 2, da.astype(F32))
    dc_ref[...] = dot(da, wo_ref[...], ((1,), (1,))).astype(BF)
    dct = dot(wo_ref[...], da, ((1,), (1,))).astype(BF)
    dct_ref[...] = dct
    product = dct.astype(F32) * ct_ref[...]
    size = product.shape[0] // HEADS
    delta_ref[...] = jnp.concatenate(
        [jnp.sum(product[head * size : (head + 1) * size], 0, keepdims=True) for head in range(HEADS)], 0
    )


def hidden_back(dy, du, n1, r1, w1, wo, g1, ct):
    length, features = dy.shape
    hidden = du.shape[1]
    rows = 256
    row = lambda i: (i, 0)
    whole = lambda i: (0, 0)
    once = pl.Buffered(1)

    def full(array):
        return pl.BlockSpec(array.shape, whole, pipeline_mode=once)

    return pl.pallas_call(
        hidden_back_kernel,
        grid=(length // rows,),
        in_specs=[
            pl.BlockSpec((rows, features), row),
            pl.BlockSpec((rows, hidden), row),
            pl.BlockSpec((rows, features), row),
            pl.BlockSpec((rows, 1), row),
            full(w1),
            full(wo),
            full(g1),
            pl.BlockSpec((features, rows), lambda i: (0, i)),
        ],
        out_specs=[
            pl.BlockSpec((rows, features), row),
            pl.BlockSpec((rows, features), row),
            pl.BlockSpec((features, rows), lambda i: (0, i)),
            pl.BlockSpec((HEADS, rows), lambda i: (0, i)),
            pl.BlockSpec((8, features), whole),
        ],
        out_shape=[
            jax.ShapeDtypeStruct((length, features), BF),
            jax.ShapeDtypeStruct((length, features), BF),
            jax.ShapeDtypeStruct((features, length), BF),
            jax.ShapeDtypeStruct((HEADS, length), F32),
            jax.ShapeDtypeStruct((8, features), F32),
        ],
        compiler_params=pltpu.CompilerParams(vmem_limit_bytes=60 * VMEM_MIB),
        name="hidden_back",
    )(dy, du, n1, r1, w1, wo, g1, ct)


def swap_seq(array):
    return lax.ppermute(array, "seq", [(0, 1), (1, 0)])


def swap_dp(array, bit):
    count = lax.axis_size("dp")
    return lax.ppermute(array, "dp", [(i, i ^ (1 << bit)) for i in range(count)])


def swap_crossed(array, bits):
    count = lax.axis_size("dp")
    pairs = [(2 * i + s, 2 * (i ^ (1 << bits[s])) + s) for i in range(count) for s in range(2)]
    return lax.ppermute(array, ("dp", "seq"), pairs)


def pick_half(array, axis, which):
    half = array.shape[axis] // 2
    return lax.dynamic_slice_in_dim(array, which * half, half, axis)


def join(mine, other, axis, place):
    return jnp.where(
        place == 0, jnp.concatenate([mine, other], axis), jnp.concatenate([other, mine], axis)
    )


def halving_axis(shape):
    rows, cols = shape
    if rows % 32 == 0:
        return 0
    if cols % 256 == 0:
        return 1
    return 0


def pack_kernel(sums2_ref, sums1_ref, wide_ref, *refs):
    biases, out_ref = refs[:-1], refs[-1]
    features = out_ref.shape[1]
    out_ref[...] = jnp.zeros(out_ref.shape, F32)
    out_ref[0:3, :] = sums2_ref[0:3, :]
    out_ref[3:6, :] = sums1_ref[0:3, :]
    for part, bias in enumerate(biases):
        own = bias.shape[1] // 3
        cols = slice(part * own, (part + 1) * own)
        out_ref[6:7, cols] = bias[0:1, :own]
        out_ref[7:8, cols] = bias[0:1, 2 * own :]
    for row in range(wide_ref.shape[1] // features):
        out_ref[8 + row : 9 + row, :] = wide_ref[0:1, row * features : (row + 1) * features]


def pack_sums(sums2, sums1, wide_sums, bias_sums):
    rows = -(-(8 + wide_sums.shape[1] // sums2.shape[1]) // 8) * 8
    return pl.pallas_call(
        pack_kernel,
        out_shape=jax.ShapeDtypeStruct((rows, sums2.shape[1]), F32),
        compiler_params=pltpu.CompilerParams(vmem_limit_bytes=60 * VMEM_MIB),
        name="pack_sums",
    )(sums2, sums1, wide_sums, *bias_sums)


def tokens_kernel(parts, place_ref, *refs):
    grads, fars, weights = refs[:parts], refs[parts : 2 * parts], refs[2 * parts : 2 * parts + 3]
    first_ref, out_ref = refs[2 * parts + 3 :]

    def back(source, part, which, at):
        own = grads[part].shape[1] // 3
        weight = weights[which][:, part * own : (part + 1) * own]
        return dot(source[:, at * own : (at + 1) * own], weight, ((1,), (1,)))

    total = first_ref[...].astype(F32)
    for part in range(parts):
        for which in range(3):
            total = total + back(grads[part], part, which, which)
    out_ref[...] = total
    tile = pl.program_id(0) - (1 - place_ref[0]) * 2

    @pl.when((tile >= 0) & (tile < 2))
    def _():
        total = out_ref[...]
        for part in range(parts):
            for which in (1, 2):
                total = total + back(fars[part], part, which, which - 1)
        out_ref[...] = total


def tokens_back(seq, grads, fars, weights, first):
    length, features = first.shape
    rows = fars[0].shape[0] // 2
    row = lambda i, place: (i, 0)
    whole = lambda i, place: (0, 0)
    return pl.pallas_call(
        functools.partial(tokens_kernel, len(grads)),
        grid_spec=pltpu.PrefetchScalarGridSpec(
            num_scalar_prefetch=1,
            grid=(length // rows,),
            in_specs=[pl.BlockSpec((rows, grad.shape[1]), lambda i, place: (place[0] * 2 + i, 0)) for grad in grads]
            + [
                pl.BlockSpec((rows, far.shape[1]), lambda i, place: (jnp.clip(i - (1 - place[0]) * 2, 0, 1), 0))
                for far in fars
            ]
            + [pl.BlockSpec(weight.shape, whole, pipeline_mode=pl.Buffered(1)) for weight in weights]
            + [pl.BlockSpec((rows, features), row)],
            out_specs=pl.BlockSpec((rows, features), row),
        ),
        out_shape=jax.ShapeDtypeStruct((length, features), F32),
        compiler_params=pltpu.CompilerParams(vmem_limit_bytes=60 * VMEM_MIB),
        name="tokens_back",
    )(seq.reshape(1).astype(jnp.int32), *grads, *fars, *weights, first)


WIDE = 768


def products_kernel(kinds, place_ref, *refs):
    count = len(kinds)
    half = count // 2
    send_ref, keep_ref = refs[-2:]
    step = pl.program_id(0)
    block = jnp.where(step < half, 1 - place_ref[0], place_ref[0]) * half + step % half
    for left, right in sorted(set(kinds)):
        mine = functools.reduce(jnp.logical_or, [block == n for n in range(count) if kinds[n] == (left, right)])

        @pl.when(mine & (step < half))
        def _(left=left, right=right):
            send_ref[...] = dot(refs[left][...], refs[right][...]).astype(BF)

        @pl.when(mine & (step >= half))
        def _(left=left, right=right):
            keep_ref[...] = dot(refs[left][...], refs[right][...]).astype(BF)


def products(blocks, seq):
    count, half = len(blocks), len(blocks) // 2
    operands, specs, kinds = [], [], []

    def block_of(step, place):
        return jnp.where(step < half, 1 - place[0], place[0]) * half + step % half

    def place_operand(side, array, split):
        for n, held in enumerate(operands):
            if held is array:
                return n
        cuts = [pair[side][1] if pair[side][0] is array else 0 for pair in blocks]
        if split:
            shape = (WIDE, array.shape[1]) if side == 0 else (array.shape[0], WIDE)

            def index(step, place):
                block = block_of(step, place)
                cut = functools.reduce(lambda held, n: jnp.where(block == n, cuts[n], held), range(count), 0)
                return (cut, 0) if side == 0 else (0, cut)

            specs.append(pl.BlockSpec(shape, index))
        else:
            specs.append(pl.BlockSpec(array.shape, lambda step, place: (0, 0), pipeline_mode=pl.Buffered(1)))
        operands.append(array)
        return len(operands) - 1

    for (left, row), (right, col) in blocks:
        kinds.append((place_operand(0, left, row is not None), place_operand(1, right, col is not None)))
    height = blocks[0][0][0].shape[0]
    out = jax.ShapeDtypeStruct((half * height, WIDE), BF)
    return pl.pallas_call(
        functools.partial(products_kernel, kinds),
        grid_spec=pltpu.PrefetchScalarGridSpec(
            num_scalar_prefetch=1,
            grid=(count,),
            in_specs=specs,
            out_specs=[
                pl.BlockSpec((height, WIDE), lambda g, place: (jnp.minimum(g, half - 1), 0)),
                pl.BlockSpec((height, WIDE), lambda g, place: (jnp.maximum(g - half, 0), 0)),
            ],
        ),
        out_shape=[out, out],
        compiler_params=pltpu.CompilerParams(vmem_limit_bytes=60 * VMEM_MIB),
        name="products",
    )(seq.reshape(1).astype(jnp.int32), *operands)


def fold_kernel(place_ref, keep_ref, other_ref, *out_refs):
    total = (keep_ref[...].astype(F32) + other_ref[...].astype(F32)).astype(BF)
    for m, out_ref in enumerate(out_refs):

        @pl.when(pl.program_id(0) == m)
        def _(out_ref=out_ref):
            out_ref[...] = total


def fold(keep, other, place, parts, first, count):
    rows, cols = keep.shape[0] // parts, keep.shape[1]
    picked = pl.BlockSpec((rows, cols), lambda m, place: (place[0] ^ (m + first), 0))
    return pl.pallas_call(
        fold_kernel,
        grid_spec=pltpu.PrefetchScalarGridSpec(
            num_scalar_prefetch=1,
            grid=(count,),
            in_specs=[picked, picked],
            out_specs=[pl.BlockSpec((rows, cols), lambda m, place: (0, 0))] * count,
        ),
        out_shape=[jax.ShapeDtypeStruct((rows, cols), BF)] * count,
        compiler_params=pltpu.CompilerParams(vmem_limit_bytes=60 * VMEM_MIB),
        name="fold",
    )(place.reshape(1).astype(jnp.int32), keep, other)


def assemble_kernel(targets, place_ref, own_ref, other_ref, *out_refs):
    shards, rows = own_ref.shape[0], own_ref.shape[1]
    step = pl.program_id(0)
    mine = step // (len(targets) // 2) == place_ref[0]
    for ref, offset, here in ((own_ref, place_ref[1], mine), (other_ref, place_ref[2], jnp.logical_not(mine))):
        for outs in sorted(set(targets)):
            ours = functools.reduce(jnp.logical_or, [step == n for n in range(len(targets)) if targets[n] == outs])

            @pl.when(here & ours)
            def _(ref=ref, offset=offset, outs=outs):
                for shard in range(shards):
                    value = ref[shard ^ (offset & (shards - 1))].astype(F32)
                    at = 0
                    for out in outs:
                        width = out_refs[out].shape[1]
                        out_refs[out][shard * rows : (shard + 1) * rows, :] = value[:, at : at + width]
                        at += width


def assemble(own, other, places, shapes, targets):
    shards, rows, _ = own.shape
    count = len(targets)
    half = count // 2
    group = shards // half

    def shard_block(which):
        def index(step, place):
            here = (step // half == place[0]) == (which == 1)
            return (jnp.where(here, (step % half) ^ (place[which] // group), 0), 0, 0)

        return pl.BlockSpec((group, rows, WIDE), index)

    out_specs = []
    for out, shape in enumerate(shapes):
        steps = [n for n in range(count) if out in targets[n]]

        def index(step, place, steps=steps):
            return (0, sum((jnp.where(step >= n, 1, 0) for n in steps[1:]), jnp.int32(0)))

        out_specs.append(pl.BlockSpec((shape[0], shape[1] // len(steps)), index))
    return pl.pallas_call(
        functools.partial(assemble_kernel, targets),
        grid_spec=pltpu.PrefetchScalarGridSpec(
            num_scalar_prefetch=1,
            grid=(count,),
            in_specs=[shard_block(1), shard_block(2)],
            out_specs=out_specs,
        ),
        out_shape=[jax.ShapeDtypeStruct(shape, F32) for shape in shapes],
        compiler_params=pltpu.CompilerParams(vmem_limit_bytes=60 * VMEM_MIB),
        name="assemble",
    )(jnp.stack(places).astype(jnp.int32), own, other)


class GradTotal:
    steps = 8

    def __init__(self, blocks):
        self.place(0)
        send, self.keep = products(blocks, self.seq)
        self.out = [send]

    def place(self, step):
        seq, dp = lax.axis_index("seq"), lax.axis_index("dp")
        self.step, self.seq, self.far = step, seq, (dp >> 2) & 3
        self.near = ((dp >> seq) & 1, (dp >> (1 - seq)) & 1)

    @classmethod
    def resumed(cls, step, out):
        total = cls.__new__(cls)
        total.place(step)
        total.out, total.got = [out], None
        return total

    def offset(self, seq):
        dp = lax.axis_index("dp")
        return ((dp >> seq) & 1) * 8 + ((dp >> (1 - seq)) & 1) * 4 + ((dp >> 2) & 3)

    def cut(self, place, parts):
        self.out = fold(self.keep, self.got[0], place, parts, 1, parts - 1)
        (self.keep,) = fold(self.keep, self.got[0], place, parts, 0, 1)

    def prepare(self):
        step = self.step
        if step in (1, 2):
            self.cut(self.near[step - 1], 2)
        elif step == 3:
            self.cut(self.far, 4)
        elif step == 4:
            total = self.keep.astype(F32)
            for other in self.got:
                total = total + other.astype(F32)
            self.out = [total.astype(BF)]
        elif step == 5:
            self.out = [jnp.stack(self.out + self.got)]
        elif step > 5 and self.got:
            self.out, self.got = [jnp.concatenate(self.out + self.got)], None

    def exchange(self):
        step, count = self.step, lax.axis_size("dp")
        if step in (0, 7):
            self.got = [swap_seq(self.out[0])]
        elif step in (1, 6):
            self.got = [swap_crossed(self.out[0], (0, 1))]
        elif step in (2, 5):
            self.got = [swap_crossed(self.out[0], (1, 0))]
        else:
            sends = self.out if step == 3 else self.out * 3
            self.got = [
                lax.ppermute(send, "dp", [(i, i ^ (m << 2)) for i in range(count)])
                for m, send in zip((1, 2, 3), sends)
            ]
        self.step += 1

    def done(self):
        return self.step == self.steps

    def whole(self, shapes, targets):
        places = [self.seq, self.offset(self.seq), self.offset(1 - self.seq)]
        return assemble(self.out[0], self.got[0], places, shapes, targets)


def plain_total(partial):
    seq, index = lax.axis_index("seq"), lax.axis_index("dp")
    block = (pick_half(partial, 0, seq).astype(F32) + swap_seq(pick_half(partial, 0, 1 - seq)).astype(F32)).astype(BF)
    steps = []
    for bit in range(int(math.log2(lax.axis_size("dp")))):
        place, axis = (index >> bit) & 1, halving_axis(block.shape)
        steps.append((bit, place, axis))
        other = swap_dp(pick_half(block, axis, 1 - place), bit)
        block = (pick_half(block, axis, place).astype(F32) + other.astype(F32)).astype(BF)
    for bit, place, axis in reversed(steps):
        block = join(block, swap_dp(block, bit), axis, place)
    return join(block, swap_seq(block), 0, seq).astype(F32)


class Swap:
    def __init__(self, array):
        self.out, self.step = [array], 0

    def prepare(self):
        pass

    def exchange(self):
        self.got = [swap_seq(self.out[0])]
        self.step = 1

    def done(self):
        return self.step == 1


class Small:
    def __init__(self, partial):
        self.block, self.step = partial, 0
        self.steps = 1 + int(math.log2(lax.axis_size("dp")))

    def prepare(self):
        if self.step:
            self.block = self.block + self.got[0]
        self.out = [self.block]

    def exchange(self):
        block = self.out[0]
        self.block = block
        self.got = [swap_seq(block) if self.step == 0 else swap_dp(block, self.step - 1)]
        self.step += 1

    def done(self):
        return self.step == self.steps

    def whole(self):
        return self.block + self.got[0]


def fence(*values):
    return lax.optimization_barrier(values)


def beside(sums, work, *inputs):
    live = [total for total in sums if not total.done()]
    for total in live:
        total.prepare()
    inputs, sends = fence(inputs, [total.out for total in live])
    for total, send in zip(live, sends):
        total.out = send
        total.exchange()
    result, received = fence(work(*inputs), [total.got for total in live])
    for total, got in zip(live, received):
        total.got = got
    return result


def body(
    tokens, lengths, partners, query_proj, query_bias, key_proj, value_proj, value_bias, output_proj, output_bias,
    first_gain, first_shift, expand_proj, expand_bias, shrink_proj, shrink_bias, second_gain, second_shift,
):
    _, length, features = tokens.shape
    pass_count = lengths.shape[1]
    seq = lax.axis_index("seq")
    dp = lax.axis_index("dp")
    far = length // 2
    window = length + far
    x = tokens[0]

    x_far = swap_seq(lax.dynamic_slice_in_dim(x, (1 - seq) * far, far, 0))
    vectors, aux, one_t, spread, key_lo, key_hi, *pair_list = setup(
        lengths,
        seq,
        length,
        window,
        (output_bias, first_gain, first_shift, shrink_bias, second_gain, second_shift, query_bias, value_bias),
    )
    queries, queries_t, keys, keys_t, values, values_t, x_t = project(
        x, x_far, query_proj, key_proj, value_proj, vectors, seq
    )
    context_low, context_t, context_low_t, lse = attend(queries_t, one_t, keys, values_t, aux, key_lo, key_hi)
    unit1, scale1, hidden_t, unit2, scale2, pooled_part, active_t, slope = feed(
        context_low, x, one_t, pass_count, output_proj, expand_proj, shrink_proj, vectors, expand_bias
    )

    lengths_wide = lengths.reshape(pass_count, 1).astype(F32)
    pooled = (pooled_part + swap_seq(pooled_part)) / lengths_wide
    inverse = lax.rsqrt(jnp.sum(pooled * pooled, -1, keepdims=True) + 1e-06)
    every = (pooled * inverse).astype(BF)
    bits = int(math.log2(lax.axis_size("dp")))
    for low in range(0, bits, 2):
        others = [
            lax.ppermute(every, "dp", [(i, i ^ (m << low)) for i in range(1 << bits)])
            for m in range(1, 1 << min(2, bits - low))
        ]
        every = jnp.concatenate([every, *others])
    passage_loss, pooled_parts = contrast(partners, lengths, dp, every, pooled)
    passage_loss = passage_loss[:, 0]

    fast = lax.axis_size("dp") == 16
    grad_shrunk, sums2, grad_shrink, grad_expand, grad_expanded, wide_sums = feed_grads(
        spread, pooled_parts, unit2, scale2, vectors, hidden_t, shrink_proj, slope, active_t
    )
    grad_shrunk, grad_expanded, grad_shrink, grad_expand = fence(
        grad_shrunk, grad_expanded, grad_shrink, grad_expand
    )
    shrink_total, expand_total = lax.psum((grad_shrink, grad_expand), ("dp", "seq"))
    grad_attended, grad_context, grad_context_t, delta, sums1 = hidden_back(
        grad_shrunk, grad_expanded, unit1, scale1, expand_proj, output_proj, vectors, context_t
    )
    parts, swaps, grads, bias_sums = 1, [], [], []
    for part in range(parts):

        def attention_work(grad_context):
            return attend_back(
                part, parts, seq, pair_list, queries, queries_t, grad_context, grad_context_t, one_t, lse, delta, keys,
                keys_t, values, aux,
            )

        grad, far_part, bias_sum = beside(swaps[-1:], attention_work, grad_context)
        grads.append(grad)
        bias_sums.append(bias_sum)
        swaps.append(Swap(far_part))
    small = pack_sums(sums2, sums1, wide_sums, bias_sums)
    square = query_proj.shape
    own = features // parts

    def near_rounds(small, context_low_t, grad_attended, x_t, far_part, *grads):
        small_sum = Small(small)
        sums, rest = [small_sum], ()
        if fast:
            late_sum = GradTotal(
                [((context_low_t, None), (grad_attended, None))]
                + [((x_t, None), (grads[0], n)) for n in range(3)]
            )
            sums.append(late_sum)
        last = Swap(far_part)
        beside(sums + [last], lambda _: (), small)
        tokens_grad = beside(
            sums,
            lambda far_part, *grads: tokens_back(
                seq, grads, (far_part,), (query_proj, key_proj, value_proj), grad_attended
            ),
            last.got[0],
            *grads,
        )
        while not small_sum.done() or fast and late_sum.step < 7:
            beside(sums, lambda _: (), small)
        if fast:
            late_sum.prepare()
            rest = late_sum.out[0]
        else:
            cut = lambda which: jnp.concatenate([grad[:, which * own : (which + 1) * own] for grad in grads], 1)
            rest = [
                plain_total(dot(left, right).astype(BF))
                for left, right in ((context_low_t, grad_attended), *((x_t, cut(n)) for n in range(3)))
            ]
        return small_sum.whole(), tokens_grad, rest

    def nothing(small, context_low_t, grad_attended, x_t, far_part, *grads):
        if fast:
            shards = jnp.zeros((16, 2 * features // 16, features), BF)
            return small, jnp.zeros((length, features), F32), shards
        return small, jnp.zeros((length, features), F32), [jnp.zeros(square, F32)] * 4

    small, tokens_grad, rest = lax.cond(
        lengths[0, 0] > 0, near_rounds, nothing, small, context_low_t, grad_attended, x_t, swaps[0].out[0],
        *grads,
    )
    tokens_grad = tokens_grad[None]
    if fast:
        late_sum = GradTotal.resumed(7, rest)
        shrink_total, expand_total = beside(
            [late_sum], lambda *totals: [total.astype(F32) for total in totals], shrink_total, expand_total
        )
        output_total, query_total, key_total, value_total = late_sum.whole(
            [square] * 4, [(0,), (1,), (2,), (3,)]
        )
    else:
        shrink_total, expand_total = shrink_total.astype(F32), expand_total.astype(F32)
        output_total, query_total, key_total, value_total = rest
    return (
        passage_loss,
        tokens_grad,
        query_total,
        small[6],
        key_total,
        value_total,
        small[7],
        output_total,
        small[5],
        small[3],
        small[4],
        expand_total,
        small[8 : 8 + expand_bias.shape[0] // features].reshape(-1),
        shrink_total,
        small[2],
        small[0],
        small[1],
    )


def solution(mesh):
    placed = (P("dp", "seq", None), P("dp", None)) + (P(),) * 16
    return jax.shard_map(
        body,
        mesh=mesh,
        in_specs=placed,
        out_specs=(P("dp"), P("dp", "seq", None)) + (P(),) * 15,
        check_vma=False,
    )
```

```python
import functools
import math

import jax
import jax.numpy as jnp
from jax import lax
from jax.experimental import pallas as pl
from jax.experimental.pallas import tpu as pltpu
from jax.sharding import PartitionSpec as P

HEADS = 12
EPS_NORM = 1e-12
BIG_NEG = -1000000000.0
HIGH = lax.Precision.HIGHEST
BF = jnp.bfloat16
F32 = jnp.float32
TILE = 128
MASKED = -float(2**30)
BIAS_O, GAIN_1, SHIFT_1, BIAS_S, GAIN_2, SHIFT_2, BIAS_Q, BIAS_V = range(8)
VMEM_MIB = 1 << 20


def dot(left, right, over=((1,), (0,))):
    return lax.dot_general(left, right, (over, ((), ())), preferred_element_type=F32)


def split3(value):
    high = value.astype(BF)
    rest = value - high.astype(F32)
    middle = rest.astype(BF)
    low = (rest - middle.astype(F32)).astype(BF)
    return high, middle, low


def split_lanes(pair):
    row = lax.broadcasted_iota(jnp.int32, (TILE, 1), 0)
    first = jnp.where(row < TILE // 2, 1.0, 0.0).astype(BF)
    second = jnp.where(row < TILE // 2, 0.0, 1.0).astype(BF)
    return jnp.concatenate([pair * first, pair * second], 1)


def split_rows(pair):
    lane = lax.broadcasted_iota(jnp.int32, (1, TILE), 1)
    first = jnp.where(lane < TILE // 2, 1.0, 0.0).astype(BF)
    second = jnp.where(lane < TILE // 2, 0.0, 1.0).astype(BF)
    return jnp.concatenate([pair * first, pair * second], 0)


def lanes_to_rows(both):
    return jnp.concatenate([both[:, :TILE], both[:, TILE:]], 0)


def attend_kernel(
    lo_ref, hi_ref, qt_ref, onet_ref, k_ref, vt_ref, aux_ref, c_ref, ct_ref, ctb_ref, lse_ref, s_scr, q_scr, m_scr, o_scr
):
    lo, hi = lo_ref[pl.program_id(0)], hi_ref[pl.program_id(0)]
    pairs = k_ref.shape[1] // TILE
    m_scr[...] = jnp.full(m_scr.shape, 2.0 * MASKED, F32)
    o_scr[...] = jnp.zeros(o_scr.shape, F32)
    one = onet_ref[...]
    for j in range(pairs):
        q_scr[j, :TILE, :] = split_lanes(qt_ref[j * TILE : (j + 1) * TILE, :])
        q_scr[j, TILE:, :] = jnp.concatenate([one, one], 1)
    extra = o_scr.shape[1] - TILE
    row = lax.broadcasted_iota(jnp.int32, (extra, 2 * TILE), 0)
    lane = lax.broadcasted_iota(jnp.int32, (extra, 2 * TILE), 1)
    ones = jnp.where(row == lane // TILE, 1.0, 0.0).astype(BF)

    count = (hi - lo + 1) // 2
    lo = jnp.minimum(lo, k_ref.shape[0] // TILE - 2 * count)

    def scores(step, carry):
        rows = pl.ds(pl.multiple_of((lo + 2 * step) * TILE, TILE), 2 * TILE)
        aux = aux_ref[rows, :]
        for j in range(pairs):
            keys = jnp.concatenate([k_ref[rows, j * TILE : (j + 1) * TILE], aux], 1)
            s = dot(keys, q_scr[j])
            s_scr[step, j] = s
            m_scr[j] = jnp.maximum(m_scr[j], jnp.max(s.reshape(TILE // 4, 8, 2 * TILE), 0))
        return carry

    lax.fori_loop(0, count, scores, 0)
    for j in range(pairs):
        m_scr[j] = jnp.broadcast_to(jnp.max(m_scr[j], 0, keepdims=True), (8, 2 * TILE))

    def weigh(step, carry):
        start = pl.multiple_of((lo + 2 * step) * TILE, TILE)
        for j in range(pairs):
            values, weights = [], []
            both = jnp.exp(s_scr[step, j] - m_scr[j, 0:1, :]).astype(BF)
            for half in range(2):
                cols = pl.ds(pl.multiple_of(start + half * TILE, TILE), TILE)
                p = both[half * TILE : (half + 1) * TILE]
                values.append(
                    jnp.concatenate([split_lanes(vt_ref[j * TILE : (j + 1) * TILE, cols]), ones], 0)
                )
                weights.append(lanes_to_rows(p))
            o_scr[j] += dot(jnp.concatenate(values, 1), jnp.concatenate(weights, 0))
        return carry

    lax.fori_loop(0, count, weigh, 0)
    half = TILE // 2
    for j in range(pairs):
        cols = slice(j * TILE, (j + 1) * TILE)
        total = o_scr[j, TILE : TILE + 2, :]
        inverse = 1.0 / total
        ct = jnp.concatenate(
            [o_scr[j, :half, :] * inverse[0:1], o_scr[j, half:TILE, :] * inverse[1:2]], 0
        )
        ct_ref[cols, :] = ct
        low = ct.astype(BF)
        ctb_ref[cols, :] = low
        c_ref[:, cols] = low.T
        top = jnp.concatenate([m_scr[j, 0:1, :TILE], m_scr[j, 0:1, TILE:]], 0)
        lse_ref[2 * j : 2 * j + 2, :] = top + jnp.log(total)


def attend(queries_t, one_t, keys, values_t, aux, lo, hi):
    features, length = queries_t.shape
    window = keys.shape[0]
    pairs = features // TILE
    row = lambda i, *_: (i, 0)
    col = lambda i, *_: (0, i)
    whole = lambda i, *_: (0, 0)
    return pl.pallas_call(
        attend_kernel,
        grid_spec=pltpu.PrefetchScalarGridSpec(
            num_scalar_prefetch=2,
            grid=(length // TILE,),
            in_specs=[
                pl.BlockSpec((features, TILE), col),
                pl.BlockSpec((TILE, TILE), col),
                pl.BlockSpec((window, features), whole),
                pl.BlockSpec((features, window), whole),
                pl.BlockSpec((window, TILE), whole),
            ],
            out_specs=[
                pl.BlockSpec((TILE, features), row),
                pl.BlockSpec((features, TILE), col),
                pl.BlockSpec((features, TILE), col),
                pl.BlockSpec((2 * pairs, TILE), col),
            ],
            scratch_shapes=[
                pltpu.VMEM((window // TILE // 2, pairs, 2 * TILE, 2 * TILE), F32),
                pltpu.VMEM((pairs, 2 * TILE, 2 * TILE), BF),
                pltpu.VMEM((pairs, 8, 2 * TILE), F32),
                pltpu.VMEM((pairs, TILE + 16, TILE), F32),
            ],
        ),
        out_shape=[
            jax.ShapeDtypeStruct((length, features), BF),
            jax.ShapeDtypeStruct((features, length), F32),
            jax.ShapeDtypeStruct((features, length), BF),
            jax.ShapeDtypeStruct((2 * pairs, length), F32),
        ],
        compiler_params=pltpu.CompilerParams(vmem_limit_bytes=60 * VMEM_MIB),
        name="attend",
    )(lo, hi, queries_t, one_t, keys, values_t, aux)


def attend_back_kernel(
    kt_ref, qt_list_ref, count_ref, place_ref, q_ref, qt_ref, dc_ref, dct_ref, onet_ref, lse_ref, delta_ref, k_ref, keys_t_ref,
    v_ref, aux_ref, grads_ref, far_ref, sums_ref, dqt_scr, dk_scr, dv_scr,
):
    pairs = q_ref.shape[1] // TILE
    dqt_scr[...] = jnp.zeros(dqt_scr.shape, F32)
    dk_scr[...] = jnp.zeros(dk_scr.shape, F32)
    dv_scr[...] = jnp.zeros(dv_scr.shape, F32)

    def tile(n):
        krows = pl.ds(pl.multiple_of(kt_ref[n] * TILE, TILE), TILE)
        rows = pl.ds(pl.multiple_of(qt_list_ref[n] * TILE, TILE), TILE)
        one = onet_ref[:, rows]
        ones = jnp.concatenate([one, one], 1)
        aux = aux_ref[krows, :]
        for j in range(pairs):
            cols = slice(j * TILE, (j + 1) * TILE)
            keys = jnp.concatenate([k_ref[krows, cols], aux], 1)
            queries_t = jnp.concatenate([split_lanes(qt_ref[cols, rows]), ones], 0)
            lse = jnp.concatenate([lse_ref[2 * j : 2 * j + 1, rows], lse_ref[2 * j + 1 : 2 * j + 2, rows]], 1)
            p = jnp.exp(dot(keys, queries_t) - lse)
            delta = jnp.concatenate([delta_ref[2 * j : 2 * j + 1, rows], delta_ref[2 * j + 1 : 2 * j + 2, rows]], 1)
            ds = (p * (dot(v_ref[krows, cols], split_lanes(dct_ref[cols, rows])) - delta)).astype(BF)
            dv_scr[krows, cols] += dot(p.astype(BF), split_rows(dc_ref[rows, cols]))
            dk_scr[krows, cols] += dot(ds, split_rows(q_ref[rows, cols]))
            dqt_scr[cols, rows] += dot(split_lanes(keys_t_ref[cols, krows]), lanes_to_rows(ds))

    count = count_ref[0]

    def two(step, carry):
        tile(2 * step)
        tile(2 * step + 1)
        return carry

    lax.fori_loop(0, count // 2, two, 0)

    @pl.when(count % 2 == 1)
    def _():
        tile(count - 1)

    length, own = q_ref.shape
    far = k_ref.shape[0] - length
    near_start = place_ref[0] * far
    far_rows = pl.ds(pl.multiple_of((1 - place_ref[0]) * length, TILE), far)
    grads_ref[far_rows, :own] = jnp.zeros((far, own), BF)
    grads_ref[:, own : 2 * own] = dk_scr[...].astype(BF)
    grads_ref[:, 2 * own :] = dv_scr[...].astype(BF)
    for i in range(length // TILE):
        rows = pl.ds(pl.multiple_of(near_start + i * TILE, TILE), TILE)
        for j in range(pairs):
            block = dqt_scr[j * TILE : (j + 1) * TILE, i * TILE : (i + 1) * TILE] * 0.125
            grads_ref[rows, j * TILE : (j + 1) * TILE] = block.T.astype(BF)
    far_ref[...] = grads_ref[far_rows, own:]
    sums_ref[...] = jnp.broadcast_to(jnp.sum(grads_ref[...].astype(F32), 0, keepdims=True), sums_ref.shape)


def attend_back(part, parts, seq, pair_list, queries, queries_t, grads, grads_t, one_t, lse, delta, keys, keys_t, values, aux):
    length, features = queries.shape
    window = keys.shape[0]
    own = features // parts
    heads = lse.shape[0] // parts
    tall = pl.BlockSpec((length, own), lambda i, *_: (0, part))
    flat = pl.BlockSpec((own, length), lambda i, *_: (part, 0))
    tall_window = pl.BlockSpec((window, own), lambda i, *_: (0, part))
    rows = pl.BlockSpec((None, heads, length), lambda i, *_: (part, 0, 0))
    first = lambda i, *_: (0, 0)
    return pl.pallas_call(
        attend_back_kernel,
        grid_spec=pltpu.PrefetchScalarGridSpec(
            num_scalar_prefetch=4,
            grid=(1,),
            in_specs=[
                tall,
                flat,
                tall,
                flat,
                pl.BlockSpec((TILE, length), first),
                rows,
                rows,
                tall_window,
                pl.BlockSpec((own, window), lambda i, *_: (part, 0)),
                tall_window,
                pl.BlockSpec((window, TILE), first),
            ],
            out_specs=[
                pl.BlockSpec((window, 3 * own), first),
                pl.BlockSpec((window - length, 2 * own), first),
                pl.BlockSpec((8, 3 * own), first),
            ],
            scratch_shapes=[
                pltpu.VMEM((own, length), F32),
                pltpu.VMEM((window, own), F32),
                pltpu.VMEM((window, own), F32),
            ],
        ),
        out_shape=[
            jax.ShapeDtypeStruct((window, 3 * own), BF),
            jax.ShapeDtypeStruct((window - length, 2 * own), BF),
            jax.ShapeDtypeStruct((8, 3 * own), F32),
        ],
        compiler_params=pltpu.CompilerParams(vmem_limit_bytes=60 * VMEM_MIB),
        name="attend_back",
    )(
        *pair_list, seq.reshape(1).astype(jnp.int32), queries, queries_t, grads, grads_t, one_t, lse.reshape(parts, heads, length),
        delta.reshape(parts, heads, length), keys, keys_t, values, aux,
    )


def setup_kernel(
    lengths_ref, seq_ref, *refs
):
    biases, (vec_ref, aux_ref, onet_ref, spread_ref, lo_ref, hi_ref, kt_ref, qt_ref, count_ref) = refs[:-9], refs[-9:]
    for row, bias in enumerate(biases):
        vec_ref[row : row + 1, :] = bias[...].reshape(1, -1)
    window, length = aux_ref.shape[0], spread_ref.shape[0]
    far = window - length
    seq = seq_ref[0]
    passages = lengths_ref.shape[1]
    ends, total = [], jnp.int32(0)
    for p in range(passages):
        total = total + lengths_ref[0, p]
        ends.append(total)
    window_start, own_start = seq * far, seq * length

    def segments(positions):
        found = jnp.zeros(positions.shape, jnp.int32)
        for end in ends:
            found = found + jnp.where(positions >= end, 1, 0)
        return found

    lane = lax.broadcasted_iota(jnp.int32, (TILE, TILE), 1)
    row = lax.broadcasted_iota(jnp.int32, (TILE, TILE), 0)

    def window_tile(i, carry):
        found = segments(window_start + i * TILE + row)
        apart = jnp.where((found != lane) & (lane <= passages), MASKED, 0.0)
        aux_ref[pl.ds(pl.multiple_of(i * TILE, TILE), TILE), :] = apart.astype(BF)
        own = i - seq * (far // TILE)

        @pl.when((own >= 0) & (own < length // TILE))
        def _():
            rows = pl.ds(pl.multiple_of(own * TILE, TILE), TILE)
            same = (found == lane % 32) & (lane < 96) & (found < passages)
            spread_ref[rows, :] = jnp.where(same, 1.0, 0.0).astype(BF)
            across = segments(own_start + own * TILE + lane[:8])
            one = jnp.where(jnp.broadcast_to(across[:1], (TILE, TILE)) == row, 1.0, 0.0)
            onet_ref[:, rows] = one.astype(BF)

        return carry

    lax.fori_loop(0, window // TILE, window_tile, 0)

    def reach(first, low, high):
        begin, end = jnp.int32(0), jnp.int32(2 * length)
        for stop in ends:
            begin = jnp.where(stop <= first, stop, begin)
        for stop in reversed(ends):
            end = jnp.where(stop > first + TILE - 1, stop, end)
        begin = jnp.clip(begin, low, high) - low
        end = jnp.clip(end, low, high) - low
        return begin // TILE, (end + TILE - 1) // TILE

    for i in range(length // TILE):
        lo_ref[i], hi_ref[i] = reach(own_start + i * TILE, window_start, window_start + window)
    count = jnp.int32(0)
    for t in range(window // TILE):
        low, high = reach(window_start + t * TILE, own_start, own_start + length)

        def put(i, count):
            kt_ref[count] = t
            qt_ref[count] = i
            return count + 1

        count = lax.fori_loop(low, high, put, count)
    count_ref[0] = count


def setup(lengths, seq, length, window, vectors):
    tiles, window_tiles = length // TILE, window // TILE
    smem = pl.BlockSpec(memory_space=pltpu.SMEM)
    vmem = pl.BlockSpec(memory_space=pltpu.VMEM)
    number = lambda n: jax.ShapeDtypeStruct((n,), jnp.int32)
    return pl.pallas_call(
        setup_kernel,
        in_specs=[smem, smem] + [vmem] * len(vectors),
        out_specs=[vmem] * 4 + [smem] * 5,
        out_shape=[
            jax.ShapeDtypeStruct((len(vectors), vectors[0].shape[0]), F32),
            jax.ShapeDtypeStruct((window, TILE), BF),
            jax.ShapeDtypeStruct((TILE, length), BF),
            jax.ShapeDtypeStruct((length, TILE), BF),
            number(tiles),
            number(tiles),
            number(tiles * window_tiles),
            number(tiles * window_tiles),
            number(1),
        ],
        compiler_params=pltpu.CompilerParams(vmem_limit_bytes=60 * VMEM_MIB),
        name="setup",
    )(lengths, seq.reshape(1).astype(jnp.int32), *vectors)


def project_kernel(
    place_ref, x_ref, far_ref, wq_ref, wk_ref, wv_ref, vec_ref, q_ref, qt_ref, k_ref, kt_ref, v_ref, vt_ref, xt_ref, x_scr
):
    own = pl.program_id(0) < place_ref[2]

    @pl.when(own)
    def _():
        x = x_ref[...]
        x_scr[...] = x
        q = (dot(x, wq_ref[...]) + vec_ref[BIAS_Q : BIAS_Q + 1, :]).astype(BF).astype(F32)
        q = (q * 0.125).astype(BF)
        q_ref[...] = q
        qt_ref[...] = q.T

    @pl.when(jnp.logical_not(own))
    def _():
        x_scr[...] = far_ref[...]

    x = x_scr[...]
    k = dot(x, wk_ref[...]).astype(BF)
    k_ref[...] = k
    kt_ref[...] = k.T
    v = (dot(x, wv_ref[...]) + vec_ref[BIAS_V : BIAS_V + 1, :]).astype(BF)
    v_ref[...] = v
    vt_ref[...] = v.T
    xt_ref[...] = x.T


def project(x, x_far, wq, wk, wv, vectors, seq):
    length, features = x.shape
    rows = 256
    near, far = length // rows, x_far.shape[0] // rows
    window = length + x_far.shape[0]
    place = jnp.stack([seq * far, (1 - seq) * near, jnp.int32(near)]).astype(jnp.int32)
    whole = lambda i, place: (0, 0)
    weight = pl.BlockSpec((features, features), whole, pipeline_mode=pl.Buffered(1))

    def window_block(i, place):
        return jnp.where(i < near, place[0] + i, place[1] + i - near)

    first = lambda i: jnp.minimum(i, near - 1)
    down = pl.BlockSpec((rows, features), lambda i, place: (window_block(i, place), 0))
    across = pl.BlockSpec((features, rows), lambda i, place: (0, window_block(i, place)))
    tall, flat = (jax.ShapeDtypeStruct(shape, BF) for shape in ((window, features), (features, window)))
    return pl.pallas_call(
        project_kernel,
        grid_spec=pltpu.PrefetchScalarGridSpec(
            num_scalar_prefetch=1,
            grid=(near + far,),
            in_specs=[
                pl.BlockSpec((rows, features), lambda i, place: (first(i), 0)),
                pl.BlockSpec((rows, features), lambda i, place: (jnp.maximum(i - near, 0), 0)),
                weight,
                weight,
                weight,
                pl.BlockSpec(vectors.shape, whole, pipeline_mode=pl.Buffered(1)),
            ],
            out_specs=[
                pl.BlockSpec((rows, features), lambda i, place: (first(i), 0)),
                pl.BlockSpec((features, rows), lambda i, place: (0, first(i))),
                down,
                across,
                down,
                across,
                across,
            ],
            scratch_shapes=[pltpu.VMEM((rows, features), BF)],
        ),
        out_shape=[
            jax.ShapeDtypeStruct((length, features), BF),
            jax.ShapeDtypeStruct((features, length), BF),
            tall,
            flat,
            tall,
            flat,
            flat,
        ],
        compiler_params=pltpu.CompilerParams(vmem_limit_bytes=60 * VMEM_MIB),
        name="project",
    )(place, x, x_far, wq, wk, wv, vectors)


def loss_kernel(partners_ref, lengths_ref, place_ref, given_ref, pooled_ref, loss_ref, parts_ref, every_ref):
    own, _ = pooled_ref.shape
    for n in range(given_ref.shape[0] // own):
        every_ref[n * own : (n + 1) * own, :] = given_ref[
            pl.ds(pl.multiple_of((place_ref[0] ^ n) * own, own), own), :
        ]
    every = every_ref[...]
    count, features = every.shape
    first = place_ref[0] * own
    scores = 100.0 * dot(every, every, ((1,), (1,)))
    row = lax.broadcasted_iota(jnp.int32, (count, count), 0)
    lane = lax.broadcasted_iota(jnp.int32, (count, count), 1)
    scores = jnp.where(row == lane, BIG_NEG, scores)
    top = jnp.max(scores, 0, keepdims=True)
    log_sums = top + jnp.log(jnp.sum(jnp.exp(scores - top), 0, keepdims=True))
    mine = every_ref[pl.ds(pl.multiple_of(first, own), own), :]
    near = 100.0 * dot(mine, every, ((1,), (1,)))
    own_row = lax.broadcasted_iota(jnp.int32, (own, count), 0)
    own_lane = lax.broadcasted_iota(jnp.int32, (own, count), 1)
    near = jnp.where(own_row + first == own_lane, BIG_NEG, near)
    top = jnp.max(near, 1, keepdims=True)
    own_sums = top + jnp.log(jnp.sum(jnp.exp(near - top), 1, keepdims=True))
    target = jnp.concatenate(
        [jnp.where(own_lane[:1] == partners_ref[first + i], 1.0, 0.0) for i in range(own)], 0
    )
    picked = jnp.sum(jnp.where(target > 0.0, near, 0.0), 1, keepdims=True)
    loss_ref[...] = jnp.broadcast_to(own_sums - picked, loss_ref.shape)
    lane_row = own_lane[:1]

    def aim(n, held):
        return jnp.where(lane_row == n, partners_ref[n], held)

    aims = lax.fori_loop(0, count, aim, jnp.full((1, count), -1, jnp.int32))
    targeted = jnp.where(aims == own_row + first, 1.0, 0.0)
    both = jnp.exp(near - own_sums) - target + (jnp.exp(near - log_sums) - targeted)
    high, middle, low = split3(both)
    grad = 100.0 * (dot(high, every) + dot(middle, every) + dot(low, every))
    pooled = pooled_ref[...]
    inverse = lax.rsqrt(jnp.sum(pooled * pooled, 1, keepdims=True) + 1e-06)
    grad = inverse * grad - pooled * (inverse * inverse * inverse * jnp.sum(pooled * grad, 1, keepdims=True))
    sizes = jnp.concatenate(
        [jnp.full((1, features), lengths_ref[0, i].astype(F32), F32) for i in range(own)], 0
    )
    high, middle, low = split3(grad / sizes)
    parts_ref[...] = jnp.zeros(parts_ref.shape, BF)
    parts_ref[0:own, :] = high
    parts_ref[32 : 32 + own, :] = middle
    parts_ref[64 : 64 + own, :] = low


def contrast(partners, lengths, place, every, pooled):
    own, features = pooled.shape
    smem = pl.BlockSpec(memory_space=pltpu.SMEM)
    vmem = pl.BlockSpec(memory_space=pltpu.VMEM)
    return pl.pallas_call(
        loss_kernel,
        in_specs=[smem, smem, smem, vmem, vmem],
        out_specs=[vmem, vmem],
        out_shape=[jax.ShapeDtypeStruct((own, TILE), F32), jax.ShapeDtypeStruct((TILE, features), BF)],
        scratch_shapes=[pltpu.VMEM(every.shape, BF)],
        compiler_params=pltpu.CompilerParams(vmem_limit_bytes=60 * VMEM_MIB),
        name="contrast",
    )(partners, lengths, place.reshape(1).astype(jnp.int32), every, pooled)


def gelu_parts(u):
    size = jnp.abs(u)
    base = 1.0 + (0.3275911 * math.sqrt(0.5)) * size
    t = pl.reciprocal(base, approx=True)
    t = t * (2.0 - base * t)
    bell = jnp.exp2((-0.5 * math.log2(math.e)) * (u * u))
    poly = t * (0.127414796 + t * (-0.142248368 + t * (0.7107068705 + t * (-0.7265760135 + t * 0.5307027145))))
    tail = poly * bell
    below = jnp.where(u < 0.0, tail, 1.0 - tail)
    return u * below, below + u * bell * (1.0 / math.sqrt(2.0 * math.pi))


def normalized(resid):
    center = resid - jnp.mean(resid, -1, keepdims=True)
    scale = lax.rsqrt(jnp.mean(center * center, -1, keepdims=True) + EPS_NORM)
    return center * scale, scale


def feed_kernel(
    cb_ref, x_ref, member_ref, wo_ref, vec_ref, be_ref, w1_ref, w2_ref,
    n1_ref, r1_ref, h_ref, n2_ref, r2_ref, pool_ref, f_ref, gp_ref, low_scr, resid_scr,
):
    vector = lambda which: vec_ref[which : which + 1, :]
    length = cb_ref.shape[0]
    rows = 256

    @pl.when(pl.program_id(0) == 0)
    def _():
        for start in range(0, length, rows):
            at = slice(start, start + rows)
            attended = dot(cb_ref[at, :], wo_ref[...]) + vector(BIAS_O)
            unit, scale = normalized(x_ref[at, :].astype(F32) + attended)
            n1_ref[at, :] = unit.astype(BF)
            r1_ref[at, :] = scale
            hidden = unit * vector(GAIN_1) + vector(SHIFT_1)
            low = hidden.astype(BF)
            low_scr[at, :] = low
            h_ref[:, at] = low.T
            resid_scr[at, :] = hidden + vector(BIAS_S)

    for start in range(0, length, rows):
        at = slice(start, start + rows)
        active, slope = gelu_parts(dot(low_scr[at, :], w1_ref[...]) + be_ref[...])
        active = active.astype(BF)
        f_ref[:, at] = active.T
        gp_ref[at, :] = slope.astype(BF)
        resid_scr[at, :] += dot(active, w2_ref[...])

    @pl.when(pl.program_id(0) == pl.num_programs(0) - 1)
    def _():
        part = jnp.zeros(pool_ref.shape, F32)
        for start in range(0, length, rows):
            at = slice(start, start + rows)
            unit, scale = normalized(resid_scr[at, :])
            n2_ref[at, :] = unit.astype(BF)
            r2_ref[at, :] = scale
            high, middle, _ = split3(unit * vector(GAIN_2) + vector(SHIFT_2))
            members = member_ref[:, at]
            part = part + dot(members, high) + dot(members, middle)
        pool_ref[...] = part


def feed(cb, x, one_t, pass_count, wo, w1, w2, vectors, expand_bias):
    length, features = x.shape
    hidden = w1.shape[1]
    chunk = 512
    row = lambda i: (i, 0)
    col = lambda i: (0, i)
    whole = lambda i: (0, 0)

    def full(array, shape=None):
        return pl.BlockSpec(shape or array.shape, whole, pipeline_mode=pl.Buffered(1))

    return pl.pallas_call(
        feed_kernel,
        grid=(hidden // chunk,),
        in_specs=[full(cb), full(x), full(one_t, (pass_count, length)), full(wo), full(vectors)]
        + [
            pl.BlockSpec((1, chunk), col),
            pl.BlockSpec((features, chunk), col),
            pl.BlockSpec((chunk, features), row),
        ],
        out_specs=[
            pl.BlockSpec((length, features), whole),
            pl.BlockSpec((length, 1), whole),
            pl.BlockSpec((features, length), whole),
            pl.BlockSpec((length, features), whole),
            pl.BlockSpec((length, 1), whole),
            pl.BlockSpec((pass_count, features), whole),
            pl.BlockSpec((chunk, length), row),
            pl.BlockSpec((length, chunk), col),
        ],
        out_shape=[
            jax.ShapeDtypeStruct((length, features), BF),
            jax.ShapeDtypeStruct((length, 1), F32),
            jax.ShapeDtypeStruct((features, length), BF),
            jax.ShapeDtypeStruct((length, features), BF),
            jax.ShapeDtypeStruct((length, 1), F32),
            jax.ShapeDtypeStruct((pass_count, features), F32),
            jax.ShapeDtypeStruct((hidden, length), BF),
            jax.ShapeDtypeStruct((length, hidden), BF),
        ],
        scratch_shapes=[pltpu.VMEM((length, features), BF), pltpu.VMEM((length, features), F32)],
        compiler_params=pltpu.CompilerParams(vmem_limit_bytes=60 * VMEM_MIB),
        name="feed",
    )(cb, x, one_t, wo, vectors, expand_bias.reshape(1, -1), w1, w2)


def norm_back(grad, unit, scale, gain):
    wide = grad * gain
    return scale * (
        wide - jnp.mean(wide, -1, keepdims=True) - unit * jnp.mean(wide * unit, -1, keepdims=True)
    )


def add_rows(ref, row, value):
    ref[row : row + 1, :] += jnp.sum(value, 0, keepdims=True)


def feed_grads_kernel(
    spread_ref, pooled_ref, n2_ref, r2_ref, vec_ref, ht_ref, w2_ref, gp_ref, ft_ref,
    dy_ref, sums_ref, shrink_ref, expand_ref, du_ref, wide_sums_ref,
):
    rows = 256
    tiles = dy_ref.shape[0] // rows

    @pl.when(pl.program_id(0) == 0)
    def _():
        sums_ref[...] = jnp.zeros(sums_ref.shape, F32)
        for i in range(tiles):
            at = slice(i * rows, (i + 1) * rows)
            grad = dot(spread_ref[at, :], pooled_ref[...])
            unit = n2_ref[at, :].astype(F32)
            add_rows(sums_ref, 0, grad * unit)
            add_rows(sums_ref, 1, grad)
            dy = norm_back(grad, unit, r2_ref[at, :], vec_ref[GAIN_2 : GAIN_2 + 1, :]).astype(BF)
            dy_ref[at, :] = dy
            add_rows(sums_ref, 2, dy.astype(F32))

    total = jnp.zeros((1, du_ref.shape[1]), F32)
    for i in range(0, tiles, 2):
        at = slice(i * rows, (i + 2) * rows)
        du = (gp_ref[at, :].astype(F32) * dot(dy_ref[at, :], w2_ref[...], ((1,), (1,)))).astype(BF)
        du_ref[at, :] = du
        total = total + jnp.sum(du.astype(F32), 0, keepdims=True)
    wide_sums_ref[...] = jnp.broadcast_to(total, wide_sums_ref.shape)
    expand_ref[...] = dot(ht_ref[...], du_ref[...]).astype(BF)
    shrink_ref[...] = dot(ft_ref[...], dy_ref[...]).astype(BF)


def feed_grads(spread, pooled_parts, n2, r2, vectors, ht, w2, gp, ft):
    length, features = n2.shape
    hidden = gp.shape[1]
    chunk = 512
    row = lambda i: (i, 0)
    col = lambda i: (0, i)
    whole = lambda i: (0, 0)

    def full(array):
        return pl.BlockSpec(array.shape, whole, pipeline_mode=pl.Buffered(1))

    return pl.pallas_call(
        feed_grads_kernel,
        grid=(hidden // chunk,),
        in_specs=[full(a) for a in (spread, pooled_parts, n2, r2, vectors, ht)]
        + [
            pl.BlockSpec((chunk, features), row),
            pl.BlockSpec((length, chunk), col),
            pl.BlockSpec((chunk, length), row),
        ],
        out_specs=[
            pl.BlockSpec((length, features), whole),
            pl.BlockSpec((8, features), whole),
            pl.BlockSpec((chunk, features), row),
            pl.BlockSpec((features, chunk), col),
            pl.BlockSpec((length, chunk), col),
            pl.BlockSpec((8, chunk), col),
        ],
        out_shape=[
            jax.ShapeDtypeStruct((length, features), BF),
            jax.ShapeDtypeStruct((8, features), F32),
            jax.ShapeDtypeStruct((hidden, features), BF),
            jax.ShapeDtypeStruct((features, hidden), BF),
            jax.ShapeDtypeStruct((length, hidden), BF),
            jax.ShapeDtypeStruct((8, hidden), F32),
        ],
        compiler_params=pltpu.CompilerParams(vmem_limit_bytes=60 * VMEM_MIB),
        name="feed_grads",
    )(spread, pooled_parts, n2, r2, vectors, ht, w2, gp, ft)


def hidden_back_kernel(
    dy_ref, du_ref, n1_ref, r1_ref, w1_ref, wo_ref, g1_ref, ct_ref, da_ref, dc_ref, dct_ref, delta_ref, sums_ref
):
    @pl.when(pl.program_id(0) == 0)
    def _():
        sums_ref[...] = jnp.zeros(sums_ref.shape, F32)

    dh = dy_ref[...].astype(F32) + dot(du_ref[...], w1_ref[...], ((1,), (1,)))
    unit = n1_ref[...].astype(F32)
    add_rows(sums_ref, 0, dh * unit)
    add_rows(sums_ref, 1, dh)
    dr = norm_back(dh, unit, r1_ref[...], g1_ref[GAIN_1 : GAIN_1 + 1, :])
    da = dr.astype(BF)
    da_ref[...] = da
    add_rows(sums_ref, 2, da.astype(F32))
    dc_ref[...] = dot(da, wo_ref[...], ((1,), (1,))).astype(BF)
    dct = dot(wo_ref[...], da, ((1,), (1,))).astype(BF)
    dct_ref[...] = dct
    product = dct.astype(F32) * ct_ref[...]
    size = product.shape[0] // HEADS
    delta_ref[...] = jnp.concatenate(
        [jnp.sum(product[head * size : (head + 1) * size], 0, keepdims=True) for head in range(HEADS)], 0
    )


def hidden_back(dy, du, n1, r1, w1, wo, g1, ct):
    length, features = dy.shape
    hidden = du.shape[1]
    rows = 256
    row = lambda i: (i, 0)
    whole = lambda i: (0, 0)
    once = pl.Buffered(1)

    def full(array):
        return pl.BlockSpec(array.shape, whole, pipeline_mode=once)

    return pl.pallas_call(
        hidden_back_kernel,
        grid=(length // rows,),
        in_specs=[
            pl.BlockSpec((rows, features), row),
            pl.BlockSpec((rows, hidden), row),
            pl.BlockSpec((rows, features), row),
            pl.BlockSpec((rows, 1), row),
            full(w1),
            full(wo),
            full(g1),
            pl.BlockSpec((features, rows), lambda i: (0, i)),
        ],
        out_specs=[
            pl.BlockSpec((rows, features), row),
            pl.BlockSpec((rows, features), row),
            pl.BlockSpec((features, rows), lambda i: (0, i)),
            pl.BlockSpec((HEADS, rows), lambda i: (0, i)),
            pl.BlockSpec((8, features), whole),
        ],
        out_shape=[
            jax.ShapeDtypeStruct((length, features), BF),
            jax.ShapeDtypeStruct((length, features), BF),
            jax.ShapeDtypeStruct((features, length), BF),
            jax.ShapeDtypeStruct((HEADS, length), F32),
            jax.ShapeDtypeStruct((8, features), F32),
        ],
        compiler_params=pltpu.CompilerParams(vmem_limit_bytes=60 * VMEM_MIB),
        name="hidden_back",
    )(dy, du, n1, r1, w1, wo, g1, ct)


def swap_seq(array):
    return lax.ppermute(array, "seq", [(0, 1), (1, 0)])


def swap_dp(array, bit):
    count = lax.axis_size("dp")
    return lax.ppermute(array, "dp", [(i, i ^ (1 << bit)) for i in range(count)])


def swap_crossed(array, bits):
    count = lax.axis_size("dp")
    pairs = [(2 * i + s, 2 * (i ^ (1 << bits[s])) + s) for i in range(count) for s in range(2)]
    return lax.ppermute(array, ("dp", "seq"), pairs)


def pick_half(array, axis, which):
    half = array.shape[axis] // 2
    return lax.dynamic_slice_in_dim(array, which * half, half, axis)


def join(mine, other, axis, place):
    return jnp.where(
        place == 0, jnp.concatenate([mine, other], axis), jnp.concatenate([other, mine], axis)
    )


def halving_axis(shape):
    rows, cols = shape
    if rows % 32 == 0:
        return 0
    if cols % 256 == 0:
        return 1
    return 0


def pack_kernel(sums2_ref, sums1_ref, wide_ref, *refs):
    biases, out_ref = refs[:-1], refs[-1]
    features = out_ref.shape[1]
    out_ref[...] = jnp.zeros(out_ref.shape, F32)
    out_ref[0:3, :] = sums2_ref[0:3, :]
    out_ref[3:6, :] = sums1_ref[0:3, :]
    for part, bias in enumerate(biases):
        own = bias.shape[1] // 3
        cols = slice(part * own, (part + 1) * own)
        out_ref[6:7, cols] = bias[0:1, :own]
        out_ref[7:8, cols] = bias[0:1, 2 * own :]
    for row in range(wide_ref.shape[1] // features):
        out_ref[8 + row : 9 + row, :] = wide_ref[0:1, row * features : (row + 1) * features]


def pack_sums(sums2, sums1, wide_sums, bias_sums):
    rows = -(-(8 + wide_sums.shape[1] // sums2.shape[1]) // 8) * 8
    return pl.pallas_call(
        pack_kernel,
        out_shape=jax.ShapeDtypeStruct((rows, sums2.shape[1]), F32),
        compiler_params=pltpu.CompilerParams(vmem_limit_bytes=60 * VMEM_MIB),
        name="pack_sums",
    )(sums2, sums1, wide_sums, *bias_sums)


def tokens_kernel(parts, place_ref, *refs):
    grads, fars, weights = refs[:parts], refs[parts : 2 * parts], refs[2 * parts : 2 * parts + 3]
    first_ref, out_ref = refs[2 * parts + 3 :]

    def back(source, part, which, at):
        own = grads[part].shape[1] // 3
        weight = weights[which][:, part * own : (part + 1) * own]
        return dot(source[:, at * own : (at + 1) * own], weight, ((1,), (1,)))

    total = first_ref[...].astype(F32)
    for part in range(parts):
        for which in range(3):
            total = total + back(grads[part], part, which, which)
    out_ref[...] = total
    tile = pl.program_id(0) - (1 - place_ref[0]) * 2

    @pl.when((tile >= 0) & (tile < 2))
    def _():
        total = out_ref[...]
        for part in range(parts):
            for which in (1, 2):
                total = total + back(fars[part], part, which, which - 1)
        out_ref[...] = total


def tokens_back(seq, grads, fars, weights, first):
    length, features = first.shape
    rows = fars[0].shape[0] // 2
    row = lambda i, place: (i, 0)
    whole = lambda i, place: (0, 0)
    return pl.pallas_call(
        functools.partial(tokens_kernel, len(grads)),
        grid_spec=pltpu.PrefetchScalarGridSpec(
            num_scalar_prefetch=1,
            grid=(length // rows,),
            in_specs=[pl.BlockSpec((rows, grad.shape[1]), lambda i, place: (place[0] * 2 + i, 0)) for grad in grads]
            + [
                pl.BlockSpec((rows, far.shape[1]), lambda i, place: (jnp.clip(i - (1 - place[0]) * 2, 0, 1), 0))
                for far in fars
            ]
            + [pl.BlockSpec(weight.shape, whole, pipeline_mode=pl.Buffered(1)) for weight in weights]
            + [pl.BlockSpec((rows, features), row)],
            out_specs=pl.BlockSpec((rows, features), row),
        ),
        out_shape=jax.ShapeDtypeStruct((length, features), F32),
        compiler_params=pltpu.CompilerParams(vmem_limit_bytes=60 * VMEM_MIB),
        name="tokens_back",
    )(seq.reshape(1).astype(jnp.int32), *grads, *fars, *weights, first)


WIDE = 768


def products_kernel(kinds, place_ref, *refs):
    half = len(kinds) // 2
    out_ref = refs[-1]
    block = place_ref[0] * half + pl.program_id(0)
    for left, right in sorted(set(kinds)):
        mine = functools.reduce(
            jnp.logical_or, [block == n for n in range(len(kinds)) if kinds[n] == (left, right)]
        )

        @pl.when(mine)
        def _(left=left, right=right):
            out_ref[...] = dot(refs[left][...], refs[right][...]).astype(BF)


def products(blocks, which):
    count, half = len(blocks), len(blocks) // 2
    operands, specs, kinds = [], [], []

    def place_operand(side, array, split):
        for n, held in enumerate(operands):
            if held is array:
                return n
        cuts = [pair[side][1] if pair[side][0] is array else 0 for pair in blocks]
        if split:
            shape = (WIDE, array.shape[1]) if side == 0 else (array.shape[0], WIDE)

            def index(step, place):
                block = place[0] * half + step
                cut = functools.reduce(lambda held, n: jnp.where(block == n, cuts[n], held), range(count), 0)
                return (cut, 0) if side == 0 else (0, cut)

            specs.append(pl.BlockSpec(shape, index))
        else:
            specs.append(pl.BlockSpec(array.shape, lambda step, place: (0, 0), pipeline_mode=pl.Buffered(1)))
        operands.append(array)
        return len(operands) - 1

    for (left, row), (right, col) in blocks:
        kinds.append((place_operand(0, left, row is not None), place_operand(1, right, col is not None)))
    height = blocks[0][0][0].shape[0]
    return pl.pallas_call(
        functools.partial(products_kernel, kinds),
        grid_spec=pltpu.PrefetchScalarGridSpec(
            num_scalar_prefetch=1,
            grid=(half,),
            in_specs=specs,
            out_specs=pl.BlockSpec((height, WIDE), lambda g, place: (g, 0)),
        ),
        out_shape=jax.ShapeDtypeStruct((half * height, WIDE), BF),
        compiler_params=pltpu.CompilerParams(vmem_limit_bytes=60 * VMEM_MIB),
        name="products",
    )(which.reshape(1).astype(jnp.int32), *operands)


def fold_kernel(place_ref, keep_ref, other_ref, *out_refs):
    total = (keep_ref[...].astype(F32) + other_ref[...].astype(F32)).astype(BF)
    for m, out_ref in enumerate(out_refs):

        @pl.when(pl.program_id(0) == m)
        def _(out_ref=out_ref):
            out_ref[...] = total


def fold(keep, other, place, parts, first, count):
    rows, cols = keep.shape[0] // parts, keep.shape[1]
    picked = pl.BlockSpec((rows, cols), lambda m, place: (place[0] ^ (m + first), 0))
    return pl.pallas_call(
        fold_kernel,
        grid_spec=pltpu.PrefetchScalarGridSpec(
            num_scalar_prefetch=1,
            grid=(count,),
            in_specs=[picked, picked],
            out_specs=[pl.BlockSpec((rows, cols), lambda m, place: (0, 0))] * count,
        ),
        out_shape=[jax.ShapeDtypeStruct((rows, cols), BF)] * count,
        compiler_params=pltpu.CompilerParams(vmem_limit_bytes=60 * VMEM_MIB),
        name="fold",
    )(place.reshape(1).astype(jnp.int32), keep, other)


def assemble_kernel(targets, place_ref, own_ref, other_ref, *out_refs):
    shards, rows = own_ref.shape[0], own_ref.shape[1]
    step = pl.program_id(0)
    mine = step // (len(targets) // 2) == place_ref[0]
    for ref, offset, here in ((own_ref, place_ref[1], mine), (other_ref, place_ref[2], jnp.logical_not(mine))):
        for outs in sorted(set(targets)):
            ours = functools.reduce(jnp.logical_or, [step == n for n in range(len(targets)) if targets[n] == outs])

            @pl.when(here & ours)
            def _(ref=ref, offset=offset, outs=outs):
                for shard in range(shards):
                    value = ref[shard ^ (offset & (shards - 1))].astype(F32)
                    at = 0
                    for out in outs:
                        width = out_refs[out].shape[1]
                        out_refs[out][shard * rows : (shard + 1) * rows, :] = value[:, at : at + width]
                        at += width


def assemble(own, other, places, shapes, targets):
    shards, rows, _ = own.shape
    count = len(targets)
    half = count // 2
    group = shards // half

    def shard_block(which):
        def index(step, place):
            here = (step // half == place[0]) == (which == 1)
            return (jnp.where(here, (step % half) ^ (place[which] // group), 0), 0, 0)

        return pl.BlockSpec((group, rows, WIDE), index)

    out_specs = []
    for out, shape in enumerate(shapes):
        steps = [n for n in range(count) if out in targets[n]]

        def index(step, place, steps=steps):
            return (0, sum((jnp.where(step >= n, 1, 0) for n in steps[1:]), jnp.int32(0)))

        out_specs.append(pl.BlockSpec((shape[0], shape[1] // len(steps)), index))
    return pl.pallas_call(
        functools.partial(assemble_kernel, targets),
        grid_spec=pltpu.PrefetchScalarGridSpec(
            num_scalar_prefetch=1,
            grid=(count,),
            in_specs=[shard_block(1), shard_block(2)],
            out_specs=out_specs,
        ),
        out_shape=[jax.ShapeDtypeStruct(shape, F32) for shape in shapes],
        compiler_params=pltpu.CompilerParams(vmem_limit_bytes=60 * VMEM_MIB),
        name="assemble",
    )(jnp.stack(places).astype(jnp.int32), own, other)


class GradTotal:
    steps = 8

    def __init__(self, blocks):
        self.place(0)
        self.out = [products(blocks, 1 - self.seq)]
        self.keep = products(blocks, self.seq)

    def place(self, step):
        seq, dp = lax.axis_index("seq"), lax.axis_index("dp")
        self.step, self.seq, self.far = step, seq, (dp >> 2) & 3
        self.near = ((dp >> seq) & 1, (dp >> (1 - seq)) & 1)

    @classmethod
    def resumed(cls, step, out):
        total = cls.__new__(cls)
        total.place(step)
        total.out, total.got = [out], None
        return total

    def offset(self, seq):
        dp = lax.axis_index("dp")
        return ((dp >> seq) & 1) * 8 + ((dp >> (1 - seq)) & 1) * 4 + ((dp >> 2) & 3)

    def cut(self, place, parts):
        self.out = fold(self.keep, self.got[0], place, parts, 1, parts - 1)
        (self.keep,) = fold(self.keep, self.got[0], place, parts, 0, 1)

    def prepare(self):
        step = self.step
        if step in (1, 2):
            self.cut(self.near[step - 1], 2)
        elif step == 3:
            self.cut(self.far, 4)
        elif step == 4:
            total = self.keep.astype(F32)
            for other in self.got:
                total = total + other.astype(F32)
            self.out = [total.astype(BF)]
        elif step == 5:
            self.out = [jnp.stack(self.out + self.got)]
        elif step > 5 and self.got:
            self.out, self.got = [jnp.concatenate(self.out + self.got)], None

    def exchange(self):
        step, count = self.step, lax.axis_size("dp")
        if step in (0, 7):
            self.got = [swap_seq(self.out[0])]
        elif step in (1, 6):
            self.got = [swap_crossed(self.out[0], (0, 1))]
        elif step in (2, 5):
            self.got = [swap_crossed(self.out[0], (1, 0))]
        else:
            sends = self.out if step == 3 else self.out * 3
            self.got = [
                lax.ppermute(send, "dp", [(i, i ^ (m << 2)) for i in range(count)])
                for m, send in zip((1, 2, 3), sends)
            ]
        self.step += 1

    def done(self):
        return self.step == self.steps

    def whole(self, shapes, targets):
        places = [self.seq, self.offset(self.seq), self.offset(1 - self.seq)]
        return assemble(self.out[0], self.got[0], places, shapes, targets)


def plain_total(partial):
    seq, index = lax.axis_index("seq"), lax.axis_index("dp")
    block = (pick_half(partial, 0, seq).astype(F32) + swap_seq(pick_half(partial, 0, 1 - seq)).astype(F32)).astype(BF)
    steps = []
    for bit in range(int(math.log2(lax.axis_size("dp")))):
        place, axis = (index >> bit) & 1, halving_axis(block.shape)
        steps.append((bit, place, axis))
        other = swap_dp(pick_half(block, axis, 1 - place), bit)
        block = (pick_half(block, axis, place).astype(F32) + other.astype(F32)).astype(BF)
    for bit, place, axis in reversed(steps):
        block = join(block, swap_dp(block, bit), axis, place)
    return join(block, swap_seq(block), 0, seq).astype(F32)


class Swap:
    def __init__(self, array):
        self.out, self.step = [array], 0

    def prepare(self):
        pass

    def exchange(self):
        self.got = [swap_seq(self.out[0])]
        self.step = 1

    def done(self):
        return self.step == 1


class Small:
    def __init__(self, partial):
        self.block, self.step = partial, 0
        self.steps = 1 + int(math.log2(lax.axis_size("dp")))

    def prepare(self):
        if self.step:
            self.block = self.block + self.got[0]
        self.out = [self.block]

    def exchange(self):
        block = self.out[0]
        self.block = block
        self.got = [swap_seq(block) if self.step == 0 else swap_dp(block, self.step - 1)]
        self.step += 1

    def done(self):
        return self.step == self.steps

    def whole(self):
        return self.block + self.got[0]


def fence(*values):
    return lax.optimization_barrier(values)


def beside(sums, work, *inputs):
    live = [total for total in sums if not total.done()]
    for total in live:
        total.prepare()
    inputs, sends = fence(inputs, [total.out for total in live])
    for total, send in zip(live, sends):
        total.out = send
        total.exchange()
    result, received = fence(work(*inputs), [total.got for total in live])
    for total, got in zip(live, received):
        total.got = got
    return result


def body(
    tokens, lengths, partners, query_proj, query_bias, key_proj, value_proj, value_bias, output_proj, output_bias,
    first_gain, first_shift, expand_proj, expand_bias, shrink_proj, shrink_bias, second_gain, second_shift,
):
    _, length, features = tokens.shape
    pass_count = lengths.shape[1]
    seq = lax.axis_index("seq")
    dp = lax.axis_index("dp")
    far = length // 2
    window = length + far
    x = tokens[0]

    x_far = swap_seq(lax.dynamic_slice_in_dim(x, (1 - seq) * far, far, 0))
    vectors, aux, one_t, spread, key_lo, key_hi, *pair_list = setup(
        lengths,
        seq,
        length,
        window,
        (output_bias, first_gain, first_shift, shrink_bias, second_gain, second_shift, query_bias, value_bias),
    )
    queries, queries_t, keys, keys_t, values, values_t, x_t = project(
        x, x_far, query_proj, key_proj, value_proj, vectors, seq
    )
    context_low, context_t, context_low_t, lse = attend(queries_t, one_t, keys, values_t, aux, key_lo, key_hi)
    unit1, scale1, hidden_t, unit2, scale2, pooled_part, active_t, slope = feed(
        context_low, x, one_t, pass_count, output_proj, expand_proj, shrink_proj, vectors, expand_bias
    )

    lengths_wide = lengths.reshape(pass_count, 1).astype(F32)
    pooled = (pooled_part + swap_seq(pooled_part)) / lengths_wide
    inverse = lax.rsqrt(jnp.sum(pooled * pooled, -1, keepdims=True) + 1e-06)
    every = (pooled * inverse).astype(BF)
    bits = int(math.log2(lax.axis_size("dp")))
    for low in range(0, bits, 2):
        others = [
            lax.ppermute(every, "dp", [(i, i ^ (m << low)) for i in range(1 << bits)])
            for m in range(1, 1 << min(2, bits - low))
        ]
        every = jnp.concatenate([every, *others])
    passage_loss, pooled_parts = contrast(partners, lengths, dp, every, pooled)
    passage_loss = passage_loss[:, 0]

    fast = lax.axis_size("dp") == 16
    grad_shrunk, sums2, grad_shrink, grad_expand, grad_expanded, wide_sums = feed_grads(
        spread, pooled_parts, unit2, scale2, vectors, hidden_t, shrink_proj, slope, active_t
    )
    grad_shrunk, grad_expanded, grad_shrink, grad_expand = fence(
        grad_shrunk, grad_expanded, grad_shrink, grad_expand
    )
    shrink_total, expand_total = lax.psum((grad_shrink, grad_expand), ("dp", "seq"))
    grad_attended, grad_context, grad_context_t, delta, sums1 = hidden_back(
        grad_shrunk, grad_expanded, unit1, scale1, expand_proj, output_proj, vectors, context_t
    )
    parts, swaps, grads, bias_sums = 1, [], [], []
    for part in range(parts):

        def attention_work(grad_context):
            return attend_back(
                part, parts, seq, pair_list, queries, queries_t, grad_context, grad_context_t, one_t, lse, delta, keys,
                keys_t, values, aux,
            )

        grad, far_part, bias_sum = beside(swaps[-1:], attention_work, grad_context)
        grads.append(grad)
        bias_sums.append(bias_sum)
        swaps.append(Swap(far_part))
    square = query_proj.shape
    own = features // parts

    def near_rounds(context_low_t, grad_attended, x_t, far_part, *grads):
        sums, rest = [], ()
        if fast:
            late_sum = GradTotal(
                [((context_low_t, None), (grad_attended, None))]
                + [((x_t, None), (grads[0], n)) for n in range(3)]
            )
            sums.append(late_sum)
        last = Swap(far_part)
        small_sum = Small(beside(sums + [last], lambda *bias: pack_sums(sums2, sums1, wide_sums, bias), *bias_sums))
        sums.append(small_sum)
        tokens_grad = beside(
            sums,
            lambda far_part, *grads: tokens_back(
                seq, grads, (far_part,), (query_proj, key_proj, value_proj), grad_attended
            ),
            last.got[0],
            *grads,
        )
        while not small_sum.done() or fast and late_sum.step < 7:
            beside(sums, lambda _: (), far_part)
        if fast:
            late_sum.prepare()
            rest = late_sum.out[0]
        else:
            cut = lambda which: jnp.concatenate([grad[:, which * own : (which + 1) * own] for grad in grads], 1)
            rest = [
                plain_total(dot(left, right).astype(BF))
                for left, right in ((context_low_t, grad_attended), *((x_t, cut(n)) for n in range(3)))
            ]
        return small_sum.whole(), tokens_grad, rest

    def nothing(context_low_t, grad_attended, x_t, far_part, *grads):
        small = jnp.zeros((-(-(8 + expand_bias.shape[0] // features) // 8) * 8, features), F32)
        if fast:
            shards = jnp.zeros((16, 2 * features // 16, features), BF)
            return small, jnp.zeros((length, features), F32), shards
        return small, jnp.zeros((length, features), F32), [jnp.zeros(square, F32)] * 4

    small, tokens_grad, rest = lax.cond(
        lengths[0, 0] > 0, near_rounds, nothing, context_low_t, grad_attended, x_t, swaps[0].out[0],
        *grads,
    )
    tokens_grad = tokens_grad[None]
    if fast:
        late_sum = GradTotal.resumed(7, rest)
        shrink_total, expand_total = beside(
            [late_sum], lambda *totals: [total.astype(F32) for total in totals], shrink_total, expand_total
        )
        output_total, query_total, key_total, value_total = late_sum.whole(
            [square] * 4, [(0,), (1,), (2,), (3,)]
        )
    else:
        shrink_total, expand_total = shrink_total.astype(F32), expand_total.astype(F32)
        output_total, query_total, key_total, value_total = rest
    return (
        passage_loss,
        tokens_grad,
        query_total,
        small[6],
        key_total,
        value_total,
        small[7],
        output_total,
        small[5],
        small[3],
        small[4],
        expand_total,
        small[8 : 8 + expand_bias.shape[0] // features].reshape(-1),
        shrink_total,
        small[2],
        small[0],
        small[1],
    )


def solution(mesh):
    placed = (P("dp", "seq", None), P("dp", None)) + (P(),) * 16
    return jax.shard_map(
        body,
        mesh=mesh,
        in_specs=placed,
        out_specs=(P("dp"), P("dp", "seq", None)) + (P(),) * 15,
        check_vma=False,
    )
```

```python
import functools
import math

import jax
import jax.numpy as jnp
from jax import lax
from jax.experimental import pallas as pl
from jax.experimental.pallas import tpu as pltpu
from jax.sharding import PartitionSpec as P

HEADS = 12
EPS_NORM = 1e-12
BIG_NEG = -1000000000.0
HIGH = lax.Precision.HIGHEST
BF = jnp.bfloat16
F32 = jnp.float32
TILE = 128
MASKED = -float(2**30)
BIAS_O, GAIN_1, SHIFT_1, BIAS_S, GAIN_2, SHIFT_2, BIAS_Q, BIAS_V = range(8)
VMEM_MIB = 1 << 20


def dot(left, right, over=((1,), (0,))):
    return lax.dot_general(left, right, (over, ((), ())), preferred_element_type=F32)


def split3(value):
    high = value.astype(BF)
    rest = value - high.astype(F32)
    middle = rest.astype(BF)
    low = (rest - middle.astype(F32)).astype(BF)
    return high, middle, low


def split_lanes(pair):
    row = lax.broadcasted_iota(jnp.int32, (TILE, 1), 0)
    first = jnp.where(row < TILE // 2, 1.0, 0.0).astype(BF)
    second = jnp.where(row < TILE // 2, 0.0, 1.0).astype(BF)
    return jnp.concatenate([pair * first, pair * second], 1)


def split_rows(pair):
    lane = lax.broadcasted_iota(jnp.int32, (1, TILE), 1)
    first = jnp.where(lane < TILE // 2, 1.0, 0.0).astype(BF)
    second = jnp.where(lane < TILE // 2, 0.0, 1.0).astype(BF)
    return jnp.concatenate([pair * first, pair * second], 0)


def lanes_to_rows(both):
    return jnp.concatenate([both[:, :TILE], both[:, TILE:]], 0)


def attend_kernel(
    lo_ref, hi_ref, qt_ref, onet_ref, k_ref, vt_ref, aux_ref, c_ref, ct_ref, ctb_ref, lse_ref, s_scr, q_scr, m_scr, o_scr
):
    lo, hi = lo_ref[pl.program_id(0)], hi_ref[pl.program_id(0)]
    pairs = k_ref.shape[1] // TILE
    m_scr[...] = jnp.full(m_scr.shape, 2.0 * MASKED, F32)
    o_scr[...] = jnp.zeros(o_scr.shape, F32)
    one = onet_ref[...]
    for j in range(pairs):
        q_scr[j, :TILE, :] = split_lanes(qt_ref[j * TILE : (j + 1) * TILE, :])
        q_scr[j, TILE:, :] = jnp.concatenate([one, one], 1)
    extra = o_scr.shape[1] - TILE
    row = lax.broadcasted_iota(jnp.int32, (extra, 2 * TILE), 0)
    lane = lax.broadcasted_iota(jnp.int32, (extra, 2 * TILE), 1)
    ones = jnp.where(row == lane // TILE, 1.0, 0.0).astype(BF)

    count = (hi - lo + 1) // 2
    lo = jnp.minimum(lo, k_ref.shape[0] // TILE - 2 * count)

    def scores(step, carry):
        rows = pl.ds(pl.multiple_of((lo + 2 * step) * TILE, TILE), 2 * TILE)
        aux = aux_ref[rows, :]
        for j in range(pairs):
            keys = jnp.concatenate([k_ref[rows, j * TILE : (j + 1) * TILE], aux], 1)
            s = dot(keys, q_scr[j])
            s_scr[step, j] = s
            m_scr[j] = jnp.maximum(m_scr[j], jnp.max(s.reshape(TILE // 4, 8, 2 * TILE), 0))
        return carry

    lax.fori_loop(0, count, scores, 0)
    for j in range(pairs):
        m_scr[j] = jnp.broadcast_to(jnp.max(m_scr[j], 0, keepdims=True), (8, 2 * TILE))

    def weigh(step, carry):
        start = pl.multiple_of((lo + 2 * step) * TILE, TILE)
        for j in range(pairs):
            values, weights = [], []
            both = jnp.exp(s_scr[step, j] - m_scr[j, 0:1, :]).astype(BF)
            for half in range(2):
                cols = pl.ds(pl.multiple_of(start + half * TILE, TILE), TILE)
                p = both[half * TILE : (half + 1) * TILE]
                values.append(
                    jnp.concatenate([split_lanes(vt_ref[j * TILE : (j + 1) * TILE, cols]), ones], 0)
                )
                weights.append(lanes_to_rows(p))
            o_scr[j] += dot(jnp.concatenate(values, 1), jnp.concatenate(weights, 0))
        return carry

    lax.fori_loop(0, count, weigh, 0)
    half = TILE // 2
    for j in range(pairs):
        cols = slice(j * TILE, (j + 1) * TILE)
        total = o_scr[j, TILE : TILE + 2, :]
        inverse = 1.0 / total
        ct = jnp.concatenate(
            [o_scr[j, :half, :] * inverse[0:1], o_scr[j, half:TILE, :] * inverse[1:2]], 0
        )
        ct_ref[cols, :] = ct
        low = ct.astype(BF)
        ctb_ref[cols, :] = low
        c_ref[:, cols] = low.T
        top = jnp.concatenate([m_scr[j, 0:1, :TILE], m_scr[j, 0:1, TILE:]], 0)
        lse_ref[2 * j : 2 * j + 2, :] = top + jnp.log(total)


def attend(queries_t, one_t, keys, values_t, aux, lo, hi):
    features, length = queries_t.shape
    window = keys.shape[0]
    pairs = features // TILE
    row = lambda i, *_: (i, 0)
    col = lambda i, *_: (0, i)
    whole = lambda i, *_: (0, 0)
    return pl.pallas_call(
        attend_kernel,
        grid_spec=pltpu.PrefetchScalarGridSpec(
            num_scalar_prefetch=2,
            grid=(length // TILE,),
            in_specs=[
                pl.BlockSpec((features, TILE), col),
                pl.BlockSpec((TILE, TILE), col),
                pl.BlockSpec((window, features), whole),
                pl.BlockSpec((features, window), whole),
                pl.BlockSpec((window, TILE), whole),
            ],
            out_specs=[
                pl.BlockSpec((TILE, features), row),
                pl.BlockSpec((features, TILE), col),
                pl.BlockSpec((features, TILE), col),
                pl.BlockSpec((2 * pairs, TILE), col),
            ],
            scratch_shapes=[
                pltpu.VMEM((window // TILE // 2, pairs, 2 * TILE, 2 * TILE), F32),
                pltpu.VMEM((pairs, 2 * TILE, 2 * TILE), BF),
                pltpu.VMEM((pairs, 8, 2 * TILE), F32),
                pltpu.VMEM((pairs, TILE + 16, TILE), F32),
            ],
        ),
        out_shape=[
            jax.ShapeDtypeStruct((length, features), BF),
            jax.ShapeDtypeStruct((features, length), F32),
            jax.ShapeDtypeStruct((features, length), BF),
            jax.ShapeDtypeStruct((2 * pairs, length), F32),
        ],
        compiler_params=pltpu.CompilerParams(vmem_limit_bytes=60 * VMEM_MIB),
        name="attend",
    )(lo, hi, queries_t, one_t, keys, values_t, aux)


def attend_back_kernel(
    kt_ref, qt_list_ref, count_ref, place_ref, q_ref, qt_ref, dc_ref, dct_ref, onet_ref, lse_ref, delta_ref, k_ref, keys_t_ref,
    v_ref, aux_ref, grads_ref, far_ref, sums_ref, dqt_scr, dk_scr, dv_scr,
):
    pairs = q_ref.shape[1] // TILE
    dqt_scr[...] = jnp.zeros(dqt_scr.shape, F32)
    dk_scr[...] = jnp.zeros(dk_scr.shape, F32)
    dv_scr[...] = jnp.zeros(dv_scr.shape, F32)

    def tile(n):
        krows = pl.ds(pl.multiple_of(kt_ref[n] * TILE, TILE), TILE)
        rows = pl.ds(pl.multiple_of(qt_list_ref[n] * TILE, TILE), TILE)
        one = onet_ref[:, rows]
        ones = jnp.concatenate([one, one], 1)
        aux = aux_ref[krows, :]
        for j in range(pairs):
            cols = slice(j * TILE, (j + 1) * TILE)
            keys = jnp.concatenate([k_ref[krows, cols], aux], 1)
            queries_t = jnp.concatenate([split_lanes(qt_ref[cols, rows]), ones], 0)
            lse = jnp.concatenate([lse_ref[2 * j : 2 * j + 1, rows], lse_ref[2 * j + 1 : 2 * j + 2, rows]], 1)
            p = jnp.exp(dot(keys, queries_t) - lse)
            delta = jnp.concatenate([delta_ref[2 * j : 2 * j + 1, rows], delta_ref[2 * j + 1 : 2 * j + 2, rows]], 1)
            ds = (p * (dot(v_ref[krows, cols], split_lanes(dct_ref[cols, rows])) - delta)).astype(BF)
            dv_scr[krows, cols] += dot(p.astype(BF), split_rows(dc_ref[rows, cols]))
            dk_scr[krows, cols] += dot(ds, split_rows(q_ref[rows, cols]))
            dqt_scr[cols, rows] += dot(split_lanes(keys_t_ref[cols, krows]), lanes_to_rows(ds))

    count = count_ref[0]

    def two(step, carry):
        tile(2 * step)
        tile(2 * step + 1)
        return carry

    lax.fori_loop(0, count // 2, two, 0)

    @pl.when(count % 2 == 1)
    def _():
        tile(count - 1)

    length, own = q_ref.shape
    far = k_ref.shape[0] - length
    near_start = place_ref[0] * far
    far_rows = pl.ds(pl.multiple_of((1 - place_ref[0]) * length, TILE), far)
    grads_ref[far_rows, :own] = jnp.zeros((far, own), BF)
    grads_ref[:, own : 2 * own] = dk_scr[...].astype(BF)
    grads_ref[:, 2 * own :] = dv_scr[...].astype(BF)
    for i in range(length // TILE):
        rows = pl.ds(pl.multiple_of(near_start + i * TILE, TILE), TILE)
        for j in range(pairs):
            block = dqt_scr[j * TILE : (j + 1) * TILE, i * TILE : (i + 1) * TILE] * 0.125
            grads_ref[rows, j * TILE : (j + 1) * TILE] = block.T.astype(BF)
    far_ref[...] = grads_ref[far_rows, own:]
    sums_ref[...] = jnp.broadcast_to(jnp.sum(grads_ref[...].astype(F32), 0, keepdims=True), sums_ref.shape)


def attend_back(part, parts, seq, pair_list, queries, queries_t, grads, grads_t, one_t, lse, delta, keys, keys_t, values, aux):
    length, features = queries.shape
    window = keys.shape[0]
    own = features // parts
    heads = lse.shape[0] // parts
    tall = pl.BlockSpec((length, own), lambda i, *_: (0, part))
    flat = pl.BlockSpec((own, length), lambda i, *_: (part, 0))
    tall_window = pl.BlockSpec((window, own), lambda i, *_: (0, part))
    rows = pl.BlockSpec((None, heads, length), lambda i, *_: (part, 0, 0))
    first = lambda i, *_: (0, 0)
    return pl.pallas_call(
        attend_back_kernel,
        grid_spec=pltpu.PrefetchScalarGridSpec(
            num_scalar_prefetch=4,
            grid=(1,),
            in_specs=[
                tall,
                flat,
                tall,
                flat,
                pl.BlockSpec((TILE, length), first),
                rows,
                rows,
                tall_window,
                pl.BlockSpec((own, window), lambda i, *_: (part, 0)),
                tall_window,
                pl.BlockSpec((window, TILE), first),
            ],
            out_specs=[
                pl.BlockSpec((window, 3 * own), first),
                pl.BlockSpec((window - length, 2 * own), first),
                pl.BlockSpec((8, 3 * own), first),
            ],
            scratch_shapes=[
                pltpu.VMEM((own, length), F32),
                pltpu.VMEM((window, own), F32),
                pltpu.VMEM((window, own), F32),
            ],
        ),
        out_shape=[
            jax.ShapeDtypeStruct((window, 3 * own), BF),
            jax.ShapeDtypeStruct((window - length, 2 * own), BF),
            jax.ShapeDtypeStruct((8, 3 * own), F32),
        ],
        compiler_params=pltpu.CompilerParams(vmem_limit_bytes=60 * VMEM_MIB),
        name="attend_back",
    )(
        *pair_list, seq.reshape(1).astype(jnp.int32), queries, queries_t, grads, grads_t, one_t, lse.reshape(parts, heads, length),
        delta.reshape(parts, heads, length), keys, keys_t, values, aux,
    )


def setup_kernel(
    lengths_ref, seq_ref, *refs
):
    biases, (vec_ref, aux_ref, onet_ref, spread_ref, lo_ref, hi_ref, kt_ref, qt_ref, count_ref) = refs[:-9], refs[-9:]
    for row, bias in enumerate(biases):
        vec_ref[row : row + 1, :] = bias[...].reshape(1, -1)
    window, length = aux_ref.shape[0], spread_ref.shape[0]
    far = window - length
    seq = seq_ref[0]
    passages = lengths_ref.shape[1]
    ends, total = [], jnp.int32(0)
    for p in range(passages):
        total = total + lengths_ref[0, p]
        ends.append(total)
    window_start, own_start = seq * far, seq * length

    def segments(positions):
        found = jnp.zeros(positions.shape, jnp.int32)
        for end in ends:
            found = found + jnp.where(positions >= end, 1, 0)
        return found

    lane = lax.broadcasted_iota(jnp.int32, (TILE, TILE), 1)
    row = lax.broadcasted_iota(jnp.int32, (TILE, TILE), 0)

    def window_tile(i, carry):
        found = segments(window_start + i * TILE + row)
        apart = jnp.where((found != lane) & (lane <= passages), MASKED, 0.0)
        aux_ref[pl.ds(pl.multiple_of(i * TILE, TILE), TILE), :] = apart.astype(BF)
        own = i - seq * (far // TILE)

        @pl.when((own >= 0) & (own < length // TILE))
        def _():
            rows = pl.ds(pl.multiple_of(own * TILE, TILE), TILE)
            same = (found == lane % 32) & (lane < 96) & (found < passages)
            spread_ref[rows, :] = jnp.where(same, 1.0, 0.0).astype(BF)
            across = segments(own_start + own * TILE + lane[:8])
            one = jnp.where(jnp.broadcast_to(across[:1], (TILE, TILE)) == row, 1.0, 0.0)
            onet_ref[:, rows] = one.astype(BF)

        return carry

    lax.fori_loop(0, window // TILE, window_tile, 0)

    def reach(first, low, high):
        begin, end = jnp.int32(0), jnp.int32(2 * length)
        for stop in ends:
            begin = jnp.where(stop <= first, stop, begin)
        for stop in reversed(ends):
            end = jnp.where(stop > first + TILE - 1, stop, end)
        begin = jnp.clip(begin, low, high) - low
        end = jnp.clip(end, low, high) - low
        return begin // TILE, (end + TILE - 1) // TILE

    for i in range(length // TILE):
        lo_ref[i], hi_ref[i] = reach(own_start + i * TILE, window_start, window_start + window)
    count = jnp.int32(0)
    for t in range(window // TILE):
        low, high = reach(window_start + t * TILE, own_start, own_start + length)

        def put(i, count):
            kt_ref[count] = t
            qt_ref[count] = i
            return count + 1

        count = lax.fori_loop(low, high, put, count)
    count_ref[0] = count


def setup(lengths, seq, length, window, vectors):
    tiles, window_tiles = length // TILE, window // TILE
    smem = pl.BlockSpec(memory_space=pltpu.SMEM)
    vmem = pl.BlockSpec(memory_space=pltpu.VMEM)
    number = lambda n: jax.ShapeDtypeStruct((n,), jnp.int32)
    return pl.pallas_call(
        setup_kernel,
        in_specs=[smem, smem] + [vmem] * len(vectors),
        out_specs=[vmem] * 4 + [smem] * 5,
        out_shape=[
            jax.ShapeDtypeStruct((len(vectors), vectors[0].shape[0]), F32),
            jax.ShapeDtypeStruct((window, TILE), BF),
            jax.ShapeDtypeStruct((TILE, length), BF),
            jax.ShapeDtypeStruct((length, TILE), BF),
            number(tiles),
            number(tiles),
            number(tiles * window_tiles),
            number(tiles * window_tiles),
            number(1),
        ],
        compiler_params=pltpu.CompilerParams(vmem_limit_bytes=60 * VMEM_MIB),
        name="setup",
    )(lengths, seq.reshape(1).astype(jnp.int32), *vectors)


def project_kernel(
    place_ref, x_ref, far_ref, wq_ref, wk_ref, wv_ref, vec_ref, q_ref, qt_ref, k_ref, kt_ref, v_ref, vt_ref, xt_ref, x_scr
):
    own = pl.program_id(0) < place_ref[2]

    @pl.when(own)
    def _():
        x = x_ref[...]
        x_scr[...] = x
        q = (dot(x, wq_ref[...]) + vec_ref[BIAS_Q : BIAS_Q + 1, :]).astype(BF).astype(F32)
        q = (q * 0.125).astype(BF)
        q_ref[...] = q
        qt_ref[...] = q.T

    @pl.when(jnp.logical_not(own))
    def _():
        x_scr[...] = far_ref[...]

    x = x_scr[...]
    k = dot(x, wk_ref[...]).astype(BF)
    k_ref[...] = k
    kt_ref[...] = k.T
    v = (dot(x, wv_ref[...]) + vec_ref[BIAS_V : BIAS_V + 1, :]).astype(BF)
    v_ref[...] = v
    vt_ref[...] = v.T
    xt_ref[...] = x.T


def project(x, x_far, wq, wk, wv, vectors, seq):
    length, features = x.shape
    rows = 512
    near, far = length // rows, x_far.shape[0] // rows
    window = length + x_far.shape[0]
    place = jnp.stack([seq * far, (1 - seq) * near, jnp.int32(near)]).astype(jnp.int32)
    whole = lambda i, place: (0, 0)
    weight = pl.BlockSpec((features, features), whole, pipeline_mode=pl.Buffered(1))

    def window_block(i, place):
        return jnp.where(i < near, place[0] + i, place[1] + i - near)

    first = lambda i: jnp.minimum(i, near - 1)
    down = pl.BlockSpec((rows, features), lambda i, place: (window_block(i, place), 0))
    across = pl.BlockSpec((features, rows), lambda i, place: (0, window_block(i, place)))
    tall, flat = (jax.ShapeDtypeStruct(shape, BF) for shape in ((window, features), (features, window)))
    return pl.pallas_call(
        project_kernel,
        grid_spec=pltpu.PrefetchScalarGridSpec(
            num_scalar_prefetch=1,
            grid=(near + far,),
            in_specs=[
                pl.BlockSpec((rows, features), lambda i, place: (first(i), 0)),
                pl.BlockSpec((rows, features), lambda i, place: (jnp.maximum(i - near, 0), 0)),
                weight,
                weight,
                weight,
                pl.BlockSpec(vectors.shape, whole, pipeline_mode=pl.Buffered(1)),
            ],
            out_specs=[
                pl.BlockSpec((rows, features), lambda i, place: (first(i), 0)),
                pl.BlockSpec((features, rows), lambda i, place: (0, first(i))),
                down,
                across,
                down,
                across,
                across,
            ],
            scratch_shapes=[pltpu.VMEM((rows, features), BF)],
        ),
        out_shape=[
            jax.ShapeDtypeStruct((length, features), BF),
            jax.ShapeDtypeStruct((features, length), BF),
            tall,
            flat,
            tall,
            flat,
            flat,
        ],
        compiler_params=pltpu.CompilerParams(vmem_limit_bytes=60 * VMEM_MIB),
        name="project",
    )(place, x, x_far, wq, wk, wv, vectors)


def loss_kernel(partners_ref, lengths_ref, place_ref, given_ref, pooled_ref, loss_ref, parts_ref, every_ref):
    own, _ = pooled_ref.shape
    for n in range(given_ref.shape[0] // own):
        every_ref[n * own : (n + 1) * own, :] = given_ref[
            pl.ds(pl.multiple_of((place_ref[0] ^ n) * own, own), own), :
        ]
    every = every_ref[...]
    count, features = every.shape
    first = place_ref[0] * own
    scores = 100.0 * dot(every, every, ((1,), (1,)))
    row = lax.broadcasted_iota(jnp.int32, (count, count), 0)
    lane = lax.broadcasted_iota(jnp.int32, (count, count), 1)
    scores = jnp.where(row == lane, BIG_NEG, scores)
    top = jnp.max(scores, 0, keepdims=True)
    log_sums = top + jnp.log(jnp.sum(jnp.exp(scores - top), 0, keepdims=True))
    mine = every_ref[pl.ds(pl.multiple_of(first, own), own), :]
    near = 100.0 * dot(mine, every, ((1,), (1,)))
    own_row = lax.broadcasted_iota(jnp.int32, (own, count), 0)
    own_lane = lax.broadcasted_iota(jnp.int32, (own, count), 1)
    near = jnp.where(own_row + first == own_lane, BIG_NEG, near)
    top = jnp.max(near, 1, keepdims=True)
    own_sums = top + jnp.log(jnp.sum(jnp.exp(near - top), 1, keepdims=True))
    target = jnp.concatenate(
        [jnp.where(own_lane[:1] == partners_ref[first + i], 1.0, 0.0) for i in range(own)], 0
    )
    picked = jnp.sum(jnp.where(target > 0.0, near, 0.0), 1, keepdims=True)
    loss_ref[...] = jnp.broadcast_to(own_sums - picked, loss_ref.shape)
    lane_row = own_lane[:1]

    def aim(n, held):
        return jnp.where(lane_row == n, partners_ref[n], held)

    aims = lax.fori_loop(0, count, aim, jnp.full((1, count), -1, jnp.int32))
    targeted = jnp.where(aims == own_row + first, 1.0, 0.0)
    both = jnp.exp(near - own_sums) - target + (jnp.exp(near - log_sums) - targeted)
    high, middle, low = split3(both)
    grad = 100.0 * (dot(high, every) + dot(middle, every) + dot(low, every))
    pooled = pooled_ref[...]
    inverse = lax.rsqrt(jnp.sum(pooled * pooled, 1, keepdims=True) + 1e-06)
    grad = inverse * grad - pooled * (inverse * inverse * inverse * jnp.sum(pooled * grad, 1, keepdims=True))
    sizes = jnp.concatenate(
        [jnp.full((1, features), lengths_ref[0, i].astype(F32), F32) for i in range(own)], 0
    )
    high, middle, low = split3(grad / sizes)
    parts_ref[...] = jnp.zeros(parts_ref.shape, BF)
    parts_ref[0:own, :] = high
    parts_ref[32 : 32 + own, :] = middle
    parts_ref[64 : 64 + own, :] = low


def contrast(partners, lengths, place, every, pooled):
    own, features = pooled.shape
    smem = pl.BlockSpec(memory_space=pltpu.SMEM)
    vmem = pl.BlockSpec(memory_space=pltpu.VMEM)
    return pl.pallas_call(
        loss_kernel,
        in_specs=[smem, smem, smem, vmem, vmem],
        out_specs=[vmem, vmem],
        out_shape=[jax.ShapeDtypeStruct((own, TILE), F32), jax.ShapeDtypeStruct((TILE, features), BF)],
        scratch_shapes=[pltpu.VMEM(every.shape, BF)],
        compiler_params=pltpu.CompilerParams(vmem_limit_bytes=60 * VMEM_MIB),
        name="contrast",
    )(partners, lengths, place.reshape(1).astype(jnp.int32), every, pooled)


def gelu_parts(u):
    size = jnp.abs(u)
    base = 1.0 + (0.3275911 * math.sqrt(0.5)) * size
    t = pl.reciprocal(base, approx=True)
    t = t * (2.0 - base * t)
    bell = jnp.exp2((-0.5 * math.log2(math.e)) * (u * u))
    poly = t * (0.127414796 + t * (-0.142248368 + t * (0.7107068705 + t * (-0.7265760135 + t * 0.5307027145))))
    tail = poly * bell
    below = jnp.where(u < 0.0, tail, 1.0 - tail)
    return u * below, below + u * bell * (1.0 / math.sqrt(2.0 * math.pi))


def normalized(resid):
    center = resid - jnp.mean(resid, -1, keepdims=True)
    scale = lax.rsqrt(jnp.mean(center * center, -1, keepdims=True) + EPS_NORM)
    return center * scale, scale


def feed_kernel(
    cb_ref, x_ref, member_ref, wo_ref, vec_ref, be_ref, w1_ref, w2_ref,
    n1_ref, r1_ref, h_ref, n2_ref, r2_ref, pool_ref, f_ref, gp_ref, low_scr, resid_scr,
):
    vector = lambda which: vec_ref[which : which + 1, :]
    length = cb_ref.shape[0]
    rows = 256

    @pl.when(pl.program_id(0) == 0)
    def _():
        for start in range(0, length, rows):
            at = slice(start, start + rows)
            attended = dot(cb_ref[at, :], wo_ref[...]) + vector(BIAS_O)
            unit, scale = normalized(x_ref[at, :].astype(F32) + attended)
            n1_ref[at, :] = unit.astype(BF)
            r1_ref[at, :] = scale
            hidden = unit * vector(GAIN_1) + vector(SHIFT_1)
            low = hidden.astype(BF)
            low_scr[at, :] = low
            h_ref[:, at] = low.T
            resid_scr[at, :] = hidden + vector(BIAS_S)

    for start in range(0, length, rows):
        at = slice(start, start + rows)
        active, slope = gelu_parts(dot(low_scr[at, :], w1_ref[...]) + be_ref[...])
        active = active.astype(BF)
        f_ref[:, at] = active.T
        gp_ref[at, :] = slope.astype(BF)
        resid_scr[at, :] += dot(active, w2_ref[...])

    @pl.when(pl.program_id(0) == pl.num_programs(0) - 1)
    def _():
        part = jnp.zeros(pool_ref.shape, F32)
        for start in range(0, length, rows):
            at = slice(start, start + rows)
            unit, scale = normalized(resid_scr[at, :])
            n2_ref[at, :] = unit.astype(BF)
            r2_ref[at, :] = scale
            high, middle, _ = split3(unit * vector(GAIN_2) + vector(SHIFT_2))
            members = member_ref[:, at]
            part = part + dot(members, high) + dot(members, middle)
        pool_ref[...] = part


def feed(cb, x, one_t, pass_count, wo, w1, w2, vectors, expand_bias):
    length, features = x.shape
    hidden = w1.shape[1]
    chunk = 768
    row = lambda i: (i, 0)
    col = lambda i: (0, i)
    whole = lambda i: (0, 0)

    def full(array, shape=None):
        return pl.BlockSpec(shape or array.shape, whole, pipeline_mode=pl.Buffered(1))

    return pl.pallas_call(
        feed_kernel,
        grid=(hidden // chunk,),
        in_specs=[full(cb), full(x), full(one_t, (pass_count, length)), full(wo), full(vectors)]
        + [
            pl.BlockSpec((1, chunk), col),
            pl.BlockSpec((features, chunk), col),
            pl.BlockSpec((chunk, features), row),
        ],
        out_specs=[
            pl.BlockSpec((length, features), whole),
            pl.BlockSpec((length, 1), whole),
            pl.BlockSpec((features, length), whole),
            pl.BlockSpec((length, features), whole),
            pl.BlockSpec((length, 1), whole),
            pl.BlockSpec((pass_count, features), whole),
            pl.BlockSpec((chunk, length), row),
            pl.BlockSpec((length, chunk), col),
        ],
        out_shape=[
            jax.ShapeDtypeStruct((length, features), BF),
            jax.ShapeDtypeStruct((length, 1), F32),
            jax.ShapeDtypeStruct((features, length), BF),
            jax.ShapeDtypeStruct((length, features), BF),
            jax.ShapeDtypeStruct((length, 1), F32),
            jax.ShapeDtypeStruct((pass_count, features), F32),
            jax.ShapeDtypeStruct((hidden, length), BF),
            jax.ShapeDtypeStruct((length, hidden), BF),
        ],
        scratch_shapes=[pltpu.VMEM((length, features), BF), pltpu.VMEM((length, features), F32)],
        compiler_params=pltpu.CompilerParams(vmem_limit_bytes=60 * VMEM_MIB),
        name="feed",
    )(cb, x, one_t, wo, vectors, expand_bias.reshape(1, -1), w1, w2)


def norm_back(grad, unit, scale, gain):
    wide = grad * gain
    return scale * (
        wide - jnp.mean(wide, -1, keepdims=True) - unit * jnp.mean(wide * unit, -1, keepdims=True)
    )


def add_rows(ref, row, value):
    ref[row : row + 1, :] += jnp.sum(value, 0, keepdims=True)


def feed_grads_kernel(
    spread_ref, pooled_ref, n2_ref, r2_ref, vec_ref, ht_ref, w2_ref, gp_ref, ft_ref,
    dy_ref, sums_ref, shrink_ref, expand_ref, du_ref, wide_sums_ref,
):
    rows = 256
    tiles = dy_ref.shape[0] // rows

    @pl.when(pl.program_id(0) == 0)
    def _():
        sums_ref[...] = jnp.zeros(sums_ref.shape, F32)
        for i in range(tiles):
            at = slice(i * rows, (i + 1) * rows)
            grad = dot(spread_ref[at, :], pooled_ref[...])
            unit = n2_ref[at, :].astype(F32)
            add_rows(sums_ref, 0, grad * unit)
            add_rows(sums_ref, 1, grad)
            dy = norm_back(grad, unit, r2_ref[at, :], vec_ref[GAIN_2 : GAIN_2 + 1, :]).astype(BF)
            dy_ref[at, :] = dy
            add_rows(sums_ref, 2, dy.astype(F32))

    total = jnp.zeros((1, du_ref.shape[1]), F32)
    for i in range(0, tiles, 2):
        at = slice(i * rows, (i + 2) * rows)
        du = (gp_ref[at, :].astype(F32) * dot(dy_ref[at, :], w2_ref[...], ((1,), (1,)))).astype(BF)
        du_ref[at, :] = du
        total = total + jnp.sum(du.astype(F32), 0, keepdims=True)
    wide_sums_ref[...] = jnp.broadcast_to(total, wide_sums_ref.shape)
    expand_ref[...] = dot(ht_ref[...], du_ref[...]).astype(BF)
    shrink_ref[...] = dot(ft_ref[...], dy_ref[...]).astype(BF)


def feed_grads(spread, pooled_parts, n2, r2, vectors, ht, w2, gp, ft):
    length, features = n2.shape
    hidden = gp.shape[1]
    chunk = 512
    row = lambda i: (i, 0)
    col = lambda i: (0, i)
    whole = lambda i: (0, 0)

    def full(array):
        return pl.BlockSpec(array.shape, whole, pipeline_mode=pl.Buffered(1))

    return pl.pallas_call(
        feed_grads_kernel,
        grid=(hidden // chunk,),
        in_specs=[full(a) for a in (spread, pooled_parts, n2, r2, vectors, ht)]
        + [
            pl.BlockSpec((chunk, features), row),
            pl.BlockSpec((length, chunk), col),
            pl.BlockSpec((chunk, length), row),
        ],
        out_specs=[
            pl.BlockSpec((length, features), whole),
            pl.BlockSpec((8, features), whole),
            pl.BlockSpec((chunk, features), row),
            pl.BlockSpec((features, chunk), col),
            pl.BlockSpec((length, chunk), col),
            pl.BlockSpec((8, chunk), col),
        ],
        out_shape=[
            jax.ShapeDtypeStruct((length, features), BF),
            jax.ShapeDtypeStruct((8, features), F32),
            jax.ShapeDtypeStruct((hidden, features), BF),
            jax.ShapeDtypeStruct((features, hidden), BF),
            jax.ShapeDtypeStruct((length, hidden), BF),
            jax.ShapeDtypeStruct((8, hidden), F32),
        ],
        compiler_params=pltpu.CompilerParams(vmem_limit_bytes=60 * VMEM_MIB),
        name="feed_grads",
    )(spread, pooled_parts, n2, r2, vectors, ht, w2, gp, ft)


def hidden_back_kernel(
    dy_ref, du_ref, n1_ref, r1_ref, w1_ref, wo_ref, g1_ref, ct_ref, da_ref, dc_ref, dct_ref, delta_ref, sums_ref
):
    @pl.when(pl.program_id(0) == 0)
    def _():
        sums_ref[...] = jnp.zeros(sums_ref.shape, F32)

    dh = dy_ref[...].astype(F32) + dot(du_ref[...], w1_ref[...], ((1,), (1,)))
    unit = n1_ref[...].astype(F32)
    add_rows(sums_ref, 0, dh * unit)
    add_rows(sums_ref, 1, dh)
    dr = norm_back(dh, unit, r1_ref[...], g1_ref[GAIN_1 : GAIN_1 + 1, :])
    da = dr.astype(BF)
    da_ref[...] = da
    add_rows(sums_ref, 2, da.astype(F32))
    dc_ref[...] = dot(da, wo_ref[...], ((1,), (1,))).astype(BF)
    dct = dot(wo_ref[...], da, ((1,), (1,))).astype(BF)
    dct_ref[...] = dct
    product = dct.astype(F32) * ct_ref[...]
    size = product.shape[0] // HEADS
    delta_ref[...] = jnp.concatenate(
        [jnp.sum(product[head * size : (head + 1) * size], 0, keepdims=True) for head in range(HEADS)], 0
    )


def hidden_back(dy, du, n1, r1, w1, wo, g1, ct):
    length, features = dy.shape
    hidden = du.shape[1]
    rows = 256
    row = lambda i: (i, 0)
    whole = lambda i: (0, 0)
    once = pl.Buffered(1)

    def full(array):
        return pl.BlockSpec(array.shape, whole, pipeline_mode=once)

    return pl.pallas_call(
        hidden_back_kernel,
        grid=(length // rows,),
        in_specs=[
            pl.BlockSpec((rows, features), row),
            pl.BlockSpec((rows, hidden), row),
            pl.BlockSpec((rows, features), row),
            pl.BlockSpec((rows, 1), row),
            full(w1),
            full(wo),
            full(g1),
            pl.BlockSpec((features, rows), lambda i: (0, i)),
        ],
        out_specs=[
            pl.BlockSpec((rows, features), row),
            pl.BlockSpec((rows, features), row),
            pl.BlockSpec((features, rows), lambda i: (0, i)),
            pl.BlockSpec((HEADS, rows), lambda i: (0, i)),
            pl.BlockSpec((8, features), whole),
        ],
        out_shape=[
            jax.ShapeDtypeStruct((length, features), BF),
            jax.ShapeDtypeStruct((length, features), BF),
            jax.ShapeDtypeStruct((features, length), BF),
            jax.ShapeDtypeStruct((HEADS, length), F32),
            jax.ShapeDtypeStruct((8, features), F32),
        ],
        compiler_params=pltpu.CompilerParams(vmem_limit_bytes=60 * VMEM_MIB),
        name="hidden_back",
    )(dy, du, n1, r1, w1, wo, g1, ct)


def swap_seq(array):
    return lax.ppermute(array, "seq", [(0, 1), (1, 0)])


def swap_dp(array, bit):
    count = lax.axis_size("dp")
    return lax.ppermute(array, "dp", [(i, i ^ (1 << bit)) for i in range(count)])


def swap_crossed(array, bits):
    count = lax.axis_size("dp")
    pairs = [(2 * i + s, 2 * (i ^ (1 << bits[s])) + s) for i in range(count) for s in range(2)]
    return lax.ppermute(array, ("dp", "seq"), pairs)


def pick_half(array, axis, which):
    half = array.shape[axis] // 2
    return lax.dynamic_slice_in_dim(array, which * half, half, axis)


def join(mine, other, axis, place):
    return jnp.where(
        place == 0, jnp.concatenate([mine, other], axis), jnp.concatenate([other, mine], axis)
    )


def halving_axis(shape):
    rows, cols = shape
    if rows % 32 == 0:
        return 0
    if cols % 256 == 0:
        return 1
    return 0


def pack_kernel(sums2_ref, sums1_ref, wide_ref, *refs):
    biases, out_ref = refs[:-1], refs[-1]
    features = out_ref.shape[1]
    out_ref[...] = jnp.zeros(out_ref.shape, F32)
    out_ref[0:3, :] = sums2_ref[0:3, :]
    out_ref[3:6, :] = sums1_ref[0:3, :]
    for part, bias in enumerate(biases):
        own = bias.shape[1] // 3
        cols = slice(part * own, (part + 1) * own)
        out_ref[6:7, cols] = bias[0:1, :own]
        out_ref[7:8, cols] = bias[0:1, 2 * own :]
    for row in range(wide_ref.shape[1] // features):
        out_ref[8 + row : 9 + row, :] = wide_ref[0:1, row * features : (row + 1) * features]


def pack_sums(sums2, sums1, wide_sums, bias_sums):
    rows = -(-(8 + wide_sums.shape[1] // sums2.shape[1]) // 8) * 8
    return pl.pallas_call(
        pack_kernel,
        out_shape=jax.ShapeDtypeStruct((rows, sums2.shape[1]), F32),
        compiler_params=pltpu.CompilerParams(vmem_limit_bytes=60 * VMEM_MIB),
        name="pack_sums",
    )(sums2, sums1, wide_sums, *bias_sums)


def tokens_kernel(parts, place_ref, *refs):
    grads, fars, weights = refs[:parts], refs[parts : 2 * parts], refs[2 * parts : 2 * parts + 3]
    first_ref, out_ref = refs[2 * parts + 3 :]

    def back(source, part, which, at):
        own = grads[part].shape[1] // 3
        weight = weights[which][:, part * own : (part + 1) * own]
        return dot(source[:, at * own : (at + 1) * own], weight, ((1,), (1,)))

    total = first_ref[...].astype(F32)
    for part in range(parts):
        for which in range(3):
            total = total + back(grads[part], part, which, which)
    out_ref[...] = total
    tile = pl.program_id(0) - (1 - place_ref[0]) * 2

    @pl.when((tile >= 0) & (tile < 2))
    def _():
        total = out_ref[...]
        for part in range(parts):
            for which in (1, 2):
                total = total + back(fars[part], part, which, which - 1)
        out_ref[...] = total


def tokens_back(seq, grads, fars, weights, first):
    length, features = first.shape
    rows = fars[0].shape[0] // 2
    row = lambda i, place: (i, 0)
    whole = lambda i, place: (0, 0)
    return pl.pallas_call(
        functools.partial(tokens_kernel, len(grads)),
        grid_spec=pltpu.PrefetchScalarGridSpec(
            num_scalar_prefetch=1,
            grid=(length // rows,),
            in_specs=[pl.BlockSpec((rows, grad.shape[1]), lambda i, place: (place[0] * 2 + i, 0)) for grad in grads]
            + [
                pl.BlockSpec((rows, far.shape[1]), lambda i, place: (jnp.clip(i - (1 - place[0]) * 2, 0, 1), 0))
                for far in fars
            ]
            + [pl.BlockSpec(weight.shape, whole, pipeline_mode=pl.Buffered(1)) for weight in weights]
            + [pl.BlockSpec((rows, features), row)],
            out_specs=pl.BlockSpec((rows, features), row),
        ),
        out_shape=jax.ShapeDtypeStruct((length, features), F32),
        compiler_params=pltpu.CompilerParams(vmem_limit_bytes=60 * VMEM_MIB),
        name="tokens_back",
    )(seq.reshape(1).astype(jnp.int32), *grads, *fars, *weights, first)


WIDE = 768


def products_kernel(kinds, place_ref, *refs):
    half = len(kinds) // 2
    out_ref = refs[-1]
    block = place_ref[0] * half + pl.program_id(0)
    for left, right in sorted(set(kinds)):
        mine = functools.reduce(
            jnp.logical_or, [block == n for n in range(len(kinds)) if kinds[n] == (left, right)]
        )

        @pl.when(mine)
        def _(left=left, right=right):
            out_ref[...] = dot(refs[left][...], refs[right][...]).astype(BF)


def products(blocks, which):
    count, half = len(blocks), len(blocks) // 2
    operands, specs, kinds = [], [], []

    def place_operand(side, array, split):
        for n, held in enumerate(operands):
            if held is array:
                return n
        cuts = [pair[side][1] if pair[side][0] is array else 0 for pair in blocks]
        if split:
            shape = (WIDE, array.shape[1]) if side == 0 else (array.shape[0], WIDE)

            def index(step, place):
                block = place[0] * half + step
                cut = functools.reduce(lambda held, n: jnp.where(block == n, cuts[n], held), range(count), 0)
                return (cut, 0) if side == 0 else (0, cut)

            specs.append(pl.BlockSpec(shape, index))
        else:
            specs.append(pl.BlockSpec(array.shape, lambda step, place: (0, 0), pipeline_mode=pl.Buffered(1)))
        operands.append(array)
        return len(operands) - 1

    for (left, row), (right, col) in blocks:
        kinds.append((place_operand(0, left, row is not None), place_operand(1, right, col is not None)))
    height = blocks[0][0][0].shape[0]
    return pl.pallas_call(
        functools.partial(products_kernel, kinds),
        grid_spec=pltpu.PrefetchScalarGridSpec(
            num_scalar_prefetch=1,
            grid=(half,),
            in_specs=specs,
            out_specs=pl.BlockSpec((height, WIDE), lambda g, place: (g, 0)),
        ),
        out_shape=jax.ShapeDtypeStruct((half * height, WIDE), BF),
        compiler_params=pltpu.CompilerParams(vmem_limit_bytes=60 * VMEM_MIB),
        name="products",
    )(which.reshape(1).astype(jnp.int32), *operands)


def fold_kernel(place_ref, keep_ref, other_ref, *out_refs):
    total = (keep_ref[...].astype(F32) + other_ref[...].astype(F32)).astype(BF)
    for m, out_ref in enumerate(out_refs):

        @pl.when(pl.program_id(0) == m)
        def _(out_ref=out_ref):
            out_ref[...] = total


def fold(keep, other, place, parts, first, count):
    rows, cols = keep.shape[0] // parts, keep.shape[1]
    picked = pl.BlockSpec((rows, cols), lambda m, place: (place[0] ^ (m + first), 0))
    return pl.pallas_call(
        fold_kernel,
        grid_spec=pltpu.PrefetchScalarGridSpec(
            num_scalar_prefetch=1,
            grid=(count,),
            in_specs=[picked, picked],
            out_specs=[pl.BlockSpec((rows, cols), lambda m, place: (0, 0))] * count,
        ),
        out_shape=[jax.ShapeDtypeStruct((rows, cols), BF)] * count,
        compiler_params=pltpu.CompilerParams(vmem_limit_bytes=60 * VMEM_MIB),
        name="fold",
    )(place.reshape(1).astype(jnp.int32), keep, other)


def assemble_kernel(targets, place_ref, own_ref, other_ref, *out_refs):
    shards, rows = own_ref.shape[0], own_ref.shape[1]
    step = pl.program_id(0)
    mine = step // (len(targets) // 2) == place_ref[0]
    for ref, offset, here in ((own_ref, place_ref[1], mine), (other_ref, place_ref[2], jnp.logical_not(mine))):
        for outs in sorted(set(targets)):
            ours = functools.reduce(jnp.logical_or, [step == n for n in range(len(targets)) if targets[n] == outs])

            @pl.when(here & ours)
            def _(ref=ref, offset=offset, outs=outs):
                for shard in range(shards):
                    value = ref[shard ^ (offset & (shards - 1))].astype(F32)
                    at = 0
                    for out in outs:
                        width = out_refs[out].shape[1]
                        out_refs[out][shard * rows : (shard + 1) * rows, :] = value[:, at : at + width]
                        at += width


def assemble(own, other, places, shapes, targets):
    shards, rows, _ = own.shape
    count = len(targets)
    half = count // 2
    group = shards // half

    def shard_block(which):
        def index(step, place):
            here = (step // half == place[0]) == (which == 1)
            return (jnp.where(here, (step % half) ^ (place[which] // group), 0), 0, 0)

        return pl.BlockSpec((group, rows, WIDE), index)

    out_specs = []
    for out, shape in enumerate(shapes):
        steps = [n for n in range(count) if out in targets[n]]

        def index(step, place, steps=steps):
            return (0, sum((jnp.where(step >= n, 1, 0) for n in steps[1:]), jnp.int32(0)))

        out_specs.append(pl.BlockSpec((shape[0], shape[1] // len(steps)), index))
    return pl.pallas_call(
        functools.partial(assemble_kernel, targets),
        grid_spec=pltpu.PrefetchScalarGridSpec(
            num_scalar_prefetch=1,
            grid=(count,),
            in_specs=[shard_block(1), shard_block(2)],
            out_specs=out_specs,
        ),
        out_shape=[jax.ShapeDtypeStruct(shape, F32) for shape in shapes],
        compiler_params=pltpu.CompilerParams(vmem_limit_bytes=60 * VMEM_MIB),
        name="assemble",
    )(jnp.stack(places).astype(jnp.int32), own, other)


class GradTotal:
    steps = 8

    def __init__(self, blocks):
        self.place(0)
        self.out = [products(blocks, 1 - self.seq)]
        self.keep = products(blocks, self.seq)

    def place(self, step):
        seq, dp = lax.axis_index("seq"), lax.axis_index("dp")
        self.step, self.seq, self.far = step, seq, (dp >> 2) & 3
        self.near = ((dp >> seq) & 1, (dp >> (1 - seq)) & 1)

    @classmethod
    def resumed(cls, step, out):
        total = cls.__new__(cls)
        total.place(step)
        total.out, total.got = [out], None
        return total

    def offset(self, seq):
        dp = lax.axis_index("dp")
        return ((dp >> seq) & 1) * 8 + ((dp >> (1 - seq)) & 1) * 4 + ((dp >> 2) & 3)

    def cut(self, place, parts):
        self.out = fold(self.keep, self.got[0], place, parts, 1, parts - 1)
        (self.keep,) = fold(self.keep, self.got[0], place, parts, 0, 1)

    def prepare(self):
        step = self.step
        if step in (1, 2):
            self.cut(self.near[step - 1], 2)
        elif step == 3:
            self.cut(self.far, 4)
        elif step == 4:
            total = self.keep.astype(F32)
            for other in self.got:
                total = total + other.astype(F32)
            self.out = [total.astype(BF)]
        elif step == 5:
            self.out = [jnp.stack(self.out + self.got)]
        elif step > 5 and self.got:
            self.out, self.got = [jnp.concatenate(self.out + self.got)], None

    def exchange(self):
        step, count = self.step, lax.axis_size("dp")
        if step in (0, 7):
            self.got = [swap_seq(self.out[0])]
        elif step in (1, 6):
            self.got = [swap_crossed(self.out[0], (0, 1))]
        elif step in (2, 5):
            self.got = [swap_crossed(self.out[0], (1, 0))]
        else:
            sends = self.out if step == 3 else self.out * 3
            self.got = [
                lax.ppermute(send, "dp", [(i, i ^ (m << 2)) for i in range(count)])
                for m, send in zip((1, 2, 3), sends)
            ]
        self.step += 1

    def done(self):
        return self.step == self.steps

    def whole(self, shapes, targets):
        places = [self.seq, self.offset(self.seq), self.offset(1 - self.seq)]
        return assemble(self.out[0], self.got[0], places, shapes, targets)


def plain_total(partial):
    seq, index = lax.axis_index("seq"), lax.axis_index("dp")
    block = (pick_half(partial, 0, seq).astype(F32) + swap_seq(pick_half(partial, 0, 1 - seq)).astype(F32)).astype(BF)
    steps = []
    for bit in range(int(math.log2(lax.axis_size("dp")))):
        place, axis = (index >> bit) & 1, halving_axis(block.shape)
        steps.append((bit, place, axis))
        other = swap_dp(pick_half(block, axis, 1 - place), bit)
        block = (pick_half(block, axis, place).astype(F32) + other.astype(F32)).astype(BF)
    for bit, place, axis in reversed(steps):
        block = join(block, swap_dp(block, bit), axis, place)
    return join(block, swap_seq(block), 0, seq).astype(F32)


class Swap:
    def __init__(self, array):
        self.out, self.step = [array], 0

    def prepare(self):
        pass

    def exchange(self):
        self.got = [swap_seq(self.out[0])]
        self.step = 1

    def done(self):
        return self.step == 1


class Small:
    def __init__(self, partial):
        self.block, self.step = partial, 0
        self.steps = 1 + int(math.log2(lax.axis_size("dp")))

    def prepare(self):
        if self.step:
            self.block = self.block + self.got[0]
        self.out = [self.block]

    def exchange(self):
        block = self.out[0]
        self.block = block
        self.got = [swap_seq(block) if self.step == 0 else swap_dp(block, self.step - 1)]
        self.step += 1

    def done(self):
        return self.step == self.steps

    def whole(self):
        return self.block + self.got[0]


def fence(*values):
    return lax.optimization_barrier(values)


def beside(sums, work, *inputs):
    live = [total for total in sums if not total.done()]
    for total in live:
        total.prepare()
    inputs, sends = fence(inputs, [total.out for total in live])
    for total, send in zip(live, sends):
        total.out = send
        total.exchange()
    result, received = fence(work(*inputs), [total.got for total in live])
    for total, got in zip(live, received):
        total.got = got
    return result


def body(
    tokens, lengths, partners, query_proj, query_bias, key_proj, value_proj, value_bias, output_proj, output_bias,
    first_gain, first_shift, expand_proj, expand_bias, shrink_proj, shrink_bias, second_gain, second_shift,
):
    _, length, features = tokens.shape
    pass_count = lengths.shape[1]
    seq = lax.axis_index("seq")
    dp = lax.axis_index("dp")
    far = length // 2
    window = length + far
    x = tokens[0]

    x_far = swap_seq(lax.dynamic_slice_in_dim(x, (1 - seq) * far, far, 0))
    vectors, aux, one_t, spread, key_lo, key_hi, *pair_list = setup(
        lengths,
        seq,
        length,
        window,
        (output_bias, first_gain, first_shift, shrink_bias, second_gain, second_shift, query_bias, value_bias),
    )
    queries, queries_t, keys, keys_t, values, values_t, x_t = project(
        x, x_far, query_proj, key_proj, value_proj, vectors, seq
    )
    context_low, context_t, context_low_t, lse = attend(queries_t, one_t, keys, values_t, aux, key_lo, key_hi)
    unit1, scale1, hidden_t, unit2, scale2, pooled_part, active_t, slope = feed(
        context_low, x, one_t, pass_count, output_proj, expand_proj, shrink_proj, vectors, expand_bias
    )

    lengths_wide = lengths.reshape(pass_count, 1).astype(F32)
    pooled = (pooled_part + swap_seq(pooled_part)) / lengths_wide
    inverse = lax.rsqrt(jnp.sum(pooled * pooled, -1, keepdims=True) + 1e-06)
    every = (pooled * inverse).astype(BF)
    bits = int(math.log2(lax.axis_size("dp")))
    for low in range(0, bits, 2):
        others = [
            lax.ppermute(every, "dp", [(i, i ^ (m << low)) for i in range(1 << bits)])
            for m in range(1, 1 << min(2, bits - low))
        ]
        every = jnp.concatenate([every, *others])
    passage_loss, pooled_parts = contrast(partners, lengths, dp, every, pooled)
    passage_loss = passage_loss[:, 0]

    fast = lax.axis_size("dp") == 16
    grad_shrunk, sums2, grad_shrink, grad_expand, grad_expanded, wide_sums = feed_grads(
        spread, pooled_parts, unit2, scale2, vectors, hidden_t, shrink_proj, slope, active_t
    )
    grad_shrunk, grad_expanded, grad_shrink, grad_expand = fence(
        grad_shrunk, grad_expanded, grad_shrink, grad_expand
    )
    shrink_total, expand_total = lax.psum((grad_shrink, grad_expand), ("dp", "seq"))
    grad_attended, grad_context, grad_context_t, delta, sums1 = hidden_back(
        grad_shrunk, grad_expanded, unit1, scale1, expand_proj, output_proj, vectors, context_t
    )
    parts, swaps, grads, bias_sums = 1, [], [], []
    for part in range(parts):

        def attention_work(grad_context):
            return attend_back(
                part, parts, seq, pair_list, queries, queries_t, grad_context, grad_context_t, one_t, lse, delta, keys,
                keys_t, values, aux,
            )

        grad, far_part, bias_sum = beside(swaps[-1:], attention_work, grad_context)
        grads.append(grad)
        bias_sums.append(bias_sum)
        swaps.append(Swap(far_part))
    square = query_proj.shape
    own = features // parts

    def near_rounds(context_low_t, grad_attended, x_t, far_part, *grads):
        sums, rest = [], ()
        if fast:
            late_sum = GradTotal(
                [((context_low_t, None), (grad_attended, None))]
                + [((x_t, None), (grads[0], n)) for n in range(3)]
            )
            sums.append(late_sum)
        last = Swap(far_part)
        small_sum = Small(beside(sums + [last], lambda *bias: pack_sums(sums2, sums1, wide_sums, bias), *bias_sums))
        sums.append(small_sum)
        tokens_grad = beside(
            sums,
            lambda far_part, *grads: tokens_back(
                seq, grads, (far_part,), (query_proj, key_proj, value_proj), grad_attended
            ),
            last.got[0],
            *grads,
        )
        while not small_sum.done() or fast and late_sum.step < 7:
            beside(sums, lambda _: (), far_part)
        if fast:
            late_sum.prepare()
            rest = late_sum.out[0]
        else:
            cut = lambda which: jnp.concatenate([grad[:, which * own : (which + 1) * own] for grad in grads], 1)
            rest = [
                plain_total(dot(left, right).astype(BF))
                for left, right in ((context_low_t, grad_attended), *((x_t, cut(n)) for n in range(3)))
            ]
        return small_sum.whole(), tokens_grad, rest

    def nothing(context_low_t, grad_attended, x_t, far_part, *grads):
        small = jnp.zeros((-(-(8 + expand_bias.shape[0] // features) // 8) * 8, features), F32)
        if fast:
            shards = jnp.zeros((16, 2 * features // 16, features), BF)
            return small, jnp.zeros((length, features), F32), shards
        return small, jnp.zeros((length, features), F32), [jnp.zeros(square, F32)] * 4

    small, tokens_grad, rest = lax.cond(
        lengths[0, 0] > 0, near_rounds, nothing, context_low_t, grad_attended, x_t, swaps[0].out[0],
        *grads,
    )
    tokens_grad = tokens_grad[None]
    if fast:
        late_sum = GradTotal.resumed(7, rest)
        shrink_total, expand_total = beside(
            [late_sum], lambda *totals: [total.astype(F32) for total in totals], shrink_total, expand_total
        )
        output_total, query_total, key_total, value_total = late_sum.whole(
            [square] * 4, [(0,), (1,), (2,), (3,)]
        )
    else:
        shrink_total, expand_total = shrink_total.astype(F32), expand_total.astype(F32)
        output_total, query_total, key_total, value_total = rest
    return (
        passage_loss,
        tokens_grad,
        query_total,
        small[6],
        key_total,
        value_total,
        small[7],
        output_total,
        small[5],
        small[3],
        small[4],
        expand_total,
        small[8 : 8 + expand_bias.shape[0] // features].reshape(-1),
        shrink_total,
        small[2],
        small[0],
        small[1],
    )


def solution(mesh):
    placed = (P("dp", "seq", None), P("dp", None)) + (P(),) * 16
    return jax.shard_map(
        body,
        mesh=mesh,
        in_specs=placed,
        out_specs=(P("dp"), P("dp", "seq", None)) + (P(),) * 15,
        check_vma=False,
    )
```

```python
import functools
import math

import jax
import jax.numpy as jnp
from jax import lax
from jax.experimental import pallas as pl
from jax.experimental.pallas import tpu as pltpu
from jax.sharding import PartitionSpec as P

HEADS = 12
EPS_NORM = 1e-12
BIG_NEG = -1000000000.0
HIGH = lax.Precision.HIGHEST
BF = jnp.bfloat16
F32 = jnp.float32
TILE = 128
MASKED = -float(2**30)
BIAS_O, GAIN_1, SHIFT_1, BIAS_S, GAIN_2, SHIFT_2, BIAS_Q, BIAS_V = range(8)
VMEM_MIB = 1 << 20


def dot(left, right, over=((1,), (0,))):
    return lax.dot_general(left, right, (over, ((), ())), preferred_element_type=F32)


def split3(value):
    high = value.astype(BF)
    rest = value - high.astype(F32)
    middle = rest.astype(BF)
    low = (rest - middle.astype(F32)).astype(BF)
    return high, middle, low


def split_lanes(pair):
    row = lax.broadcasted_iota(jnp.int32, (TILE, 1), 0)
    first = jnp.where(row < TILE // 2, 1.0, 0.0).astype(BF)
    second = jnp.where(row < TILE // 2, 0.0, 1.0).astype(BF)
    return jnp.concatenate([pair * first, pair * second], 1)


def split_rows(pair):
    lane = lax.broadcasted_iota(jnp.int32, (1, TILE), 1)
    first = jnp.where(lane < TILE // 2, 1.0, 0.0).astype(BF)
    second = jnp.where(lane < TILE // 2, 0.0, 1.0).astype(BF)
    return jnp.concatenate([pair * first, pair * second], 0)


def lanes_to_rows(both):
    return jnp.concatenate([both[:, :TILE], both[:, TILE:]], 0)


def attend_kernel(
    lo_ref, hi_ref, qt_ref, onet_ref, k_ref, vt_ref, aux_ref, c_ref, ct_ref, ctb_ref, lse_ref, s_scr, q_scr, m_scr, o_scr
):
    lo, hi = lo_ref[pl.program_id(0)], hi_ref[pl.program_id(0)]
    pairs = k_ref.shape[1] // TILE
    m_scr[...] = jnp.full(m_scr.shape, 2.0 * MASKED, F32)
    o_scr[...] = jnp.zeros(o_scr.shape, F32)
    one = onet_ref[...]
    for j in range(pairs):
        q_scr[j, :TILE, :] = split_lanes(qt_ref[j * TILE : (j + 1) * TILE, :])
        q_scr[j, TILE:, :] = jnp.concatenate([one, one], 1)
    extra = o_scr.shape[1] - TILE
    row = lax.broadcasted_iota(jnp.int32, (extra, 2 * TILE), 0)
    lane = lax.broadcasted_iota(jnp.int32, (extra, 2 * TILE), 1)
    ones = jnp.where(row == lane // TILE, 1.0, 0.0).astype(BF)

    count = (hi - lo + 1) // 2
    lo = jnp.minimum(lo, k_ref.shape[0] // TILE - 2 * count)

    def scores(step, carry):
        rows = pl.ds(pl.multiple_of((lo + 2 * step) * TILE, TILE), 2 * TILE)
        aux = aux_ref[rows, :]
        for j in range(pairs):
            keys = jnp.concatenate([k_ref[rows, j * TILE : (j + 1) * TILE], aux], 1)
            s = dot(keys, q_scr[j])
            s_scr[step, j] = s
            m_scr[j] = jnp.maximum(m_scr[j], jnp.max(s.reshape(TILE // 4, 8, 2 * TILE), 0))
        return carry

    lax.fori_loop(0, count, scores, 0)
    for j in range(pairs):
        m_scr[j] = jnp.broadcast_to(jnp.max(m_scr[j], 0, keepdims=True), (8, 2 * TILE))

    def weigh(step, carry):
        start = pl.multiple_of((lo + 2 * step) * TILE, TILE)
        for j in range(pairs):
            values, weights = [], []
            both = jnp.exp(s_scr[step, j] - m_scr[j, 0:1, :]).astype(BF)
            for half in range(2):
                cols = pl.ds(pl.multiple_of(start + half * TILE, TILE), TILE)
                p = both[half * TILE : (half + 1) * TILE]
                values.append(
                    jnp.concatenate([split_lanes(vt_ref[j * TILE : (j + 1) * TILE, cols]), ones], 0)
                )
                weights.append(lanes_to_rows(p))
            o_scr[j] += dot(jnp.concatenate(values, 1), jnp.concatenate(weights, 0))
        return carry

    lax.fori_loop(0, count, weigh, 0)
    half = TILE // 2
    for j in range(pairs):
        cols = slice(j * TILE, (j + 1) * TILE)
        total = o_scr[j, TILE : TILE + 2, :]
        inverse = 1.0 / total
        ct = jnp.concatenate(
            [o_scr[j, :half, :] * inverse[0:1], o_scr[j, half:TILE, :] * inverse[1:2]], 0
        )
        ct_ref[cols, :] = ct
        low = ct.astype(BF)
        ctb_ref[cols, :] = low
        c_ref[:, cols] = low.T
        top = jnp.concatenate([m_scr[j, 0:1, :TILE], m_scr[j, 0:1, TILE:]], 0)
        lse_ref[2 * j : 2 * j + 2, :] = top + jnp.log(total)


def attend(queries_t, one_t, keys, values_t, aux, lo, hi):
    features, length = queries_t.shape
    window = keys.shape[0]
    pairs = features // TILE
    row = lambda i, *_: (i, 0)
    col = lambda i, *_: (0, i)
    whole = lambda i, *_: (0, 0)
    return pl.pallas_call(
        attend_kernel,
        grid_spec=pltpu.PrefetchScalarGridSpec(
            num_scalar_prefetch=2,
            grid=(length // TILE,),
            in_specs=[
                pl.BlockSpec((features, TILE), col),
                pl.BlockSpec((TILE, TILE), col),
                pl.BlockSpec((window, features), whole),
                pl.BlockSpec((features, window), whole),
                pl.BlockSpec((window, TILE), whole),
            ],
            out_specs=[
                pl.BlockSpec((TILE, features), row),
                pl.BlockSpec((features, TILE), col),
                pl.BlockSpec((features, TILE), col),
                pl.BlockSpec((2 * pairs, TILE), col),
            ],
            scratch_shapes=[
                pltpu.VMEM((window // TILE // 2, pairs, 2 * TILE, 2 * TILE), F32),
                pltpu.VMEM((pairs, 2 * TILE, 2 * TILE), BF),
                pltpu.VMEM((pairs, 8, 2 * TILE), F32),
                pltpu.VMEM((pairs, TILE + 16, TILE), F32),
            ],
        ),
        out_shape=[
            jax.ShapeDtypeStruct((length, features), BF),
            jax.ShapeDtypeStruct((features, length), F32),
            jax.ShapeDtypeStruct((features, length), BF),
            jax.ShapeDtypeStruct((2 * pairs, length), F32),
        ],
        compiler_params=pltpu.CompilerParams(vmem_limit_bytes=60 * VMEM_MIB),
        name="attend",
    )(lo, hi, queries_t, one_t, keys, values_t, aux)


def attend_back_kernel(
    kt_ref, qt_list_ref, count_ref, place_ref, q_ref, qt_ref, dc_ref, dct_ref, onet_ref, lse_ref, delta_ref, k_ref, keys_t_ref,
    v_ref, aux_ref, grads_ref, far_ref, sums_ref, dqt_scr, dk_scr, dv_scr,
):
    pairs = q_ref.shape[1] // TILE
    dqt_scr[...] = jnp.zeros(dqt_scr.shape, F32)
    dk_scr[...] = jnp.zeros(dk_scr.shape, F32)
    dv_scr[...] = jnp.zeros(dv_scr.shape, F32)

    def tile(n):
        krows = pl.ds(pl.multiple_of(kt_ref[n] * TILE, TILE), TILE)
        rows = pl.ds(pl.multiple_of(qt_list_ref[n] * TILE, TILE), TILE)
        one = onet_ref[:, rows]
        ones = jnp.concatenate([one, one], 1)
        aux = aux_ref[krows, :]
        for j in range(pairs):
            cols = slice(j * TILE, (j + 1) * TILE)
            keys = jnp.concatenate([k_ref[krows, cols], aux], 1)
            queries_t = jnp.concatenate([split_lanes(qt_ref[cols, rows]), ones], 0)
            lse = jnp.concatenate([lse_ref[2 * j : 2 * j + 1, rows], lse_ref[2 * j + 1 : 2 * j + 2, rows]], 1)
            p = jnp.exp(dot(keys, queries_t) - lse)
            delta = jnp.concatenate([delta_ref[2 * j : 2 * j + 1, rows], delta_ref[2 * j + 1 : 2 * j + 2, rows]], 1)
            ds = (p * (dot(v_ref[krows, cols], split_lanes(dct_ref[cols, rows])) - delta)).astype(BF)
            dv_scr[krows, cols] += dot(p.astype(BF), split_rows(dc_ref[rows, cols]))
            dk_scr[krows, cols] += dot(ds, split_rows(q_ref[rows, cols]))
            dqt_scr[cols, rows] += dot(split_lanes(keys_t_ref[cols, krows]), lanes_to_rows(ds))

    count = count_ref[0]

    def two(step, carry):
        tile(2 * step)
        tile(2 * step + 1)
        return carry

    lax.fori_loop(0, count // 2, two, 0)

    @pl.when(count % 2 == 1)
    def _():
        tile(count - 1)

    length, own = q_ref.shape
    far = k_ref.shape[0] - length
    near_start = place_ref[0] * far
    far_rows = pl.ds(pl.multiple_of((1 - place_ref[0]) * length, TILE), far)
    grads_ref[far_rows, :own] = jnp.zeros((far, own), BF)
    grads_ref[:, own : 2 * own] = dk_scr[...].astype(BF)
    grads_ref[:, 2 * own :] = dv_scr[...].astype(BF)
    for i in range(length // TILE):
        rows = pl.ds(pl.multiple_of(near_start + i * TILE, TILE), TILE)
        for j in range(pairs):
            block = dqt_scr[j * TILE : (j + 1) * TILE, i * TILE : (i + 1) * TILE] * 0.125
            grads_ref[rows, j * TILE : (j + 1) * TILE] = block.T.astype(BF)
    far_ref[...] = grads_ref[far_rows, own:]
    sums_ref[...] = jnp.broadcast_to(jnp.sum(grads_ref[...].astype(F32), 0, keepdims=True), sums_ref.shape)


def attend_back(part, parts, seq, pair_list, queries, queries_t, grads, grads_t, one_t, lse, delta, keys, keys_t, values, aux):
    length, features = queries.shape
    window = keys.shape[0]
    own = features // parts
    heads = lse.shape[0] // parts
    tall = pl.BlockSpec((length, own), lambda i, *_: (0, part))
    flat = pl.BlockSpec((own, length), lambda i, *_: (part, 0))
    tall_window = pl.BlockSpec((window, own), lambda i, *_: (0, part))
    rows = pl.BlockSpec((None, heads, length), lambda i, *_: (part, 0, 0))
    first = lambda i, *_: (0, 0)
    return pl.pallas_call(
        attend_back_kernel,
        grid_spec=pltpu.PrefetchScalarGridSpec(
            num_scalar_prefetch=4,
            grid=(1,),
            in_specs=[
                tall,
                flat,
                tall,
                flat,
                pl.BlockSpec((TILE, length), first),
                rows,
                rows,
                tall_window,
                pl.BlockSpec((own, window), lambda i, *_: (part, 0)),
                tall_window,
                pl.BlockSpec((window, TILE), first),
            ],
            out_specs=[
                pl.BlockSpec((window, 3 * own), first),
                pl.BlockSpec((window - length, 2 * own), first),
                pl.BlockSpec((8, 3 * own), first),
            ],
            scratch_shapes=[
                pltpu.VMEM((own, length), F32),
                pltpu.VMEM((window, own), F32),
                pltpu.VMEM((window, own), F32),
            ],
        ),
        out_shape=[
            jax.ShapeDtypeStruct((window, 3 * own), BF),
            jax.ShapeDtypeStruct((window - length, 2 * own), BF),
            jax.ShapeDtypeStruct((8, 3 * own), F32),
        ],
        compiler_params=pltpu.CompilerParams(vmem_limit_bytes=60 * VMEM_MIB),
        name="attend_back",
    )(
        *pair_list, seq.reshape(1).astype(jnp.int32), queries, queries_t, grads, grads_t, one_t, lse.reshape(parts, heads, length),
        delta.reshape(parts, heads, length), keys, keys_t, values, aux,
    )


def setup_kernel(
    lengths_ref, seq_ref, *refs
):
    biases, (vec_ref, aux_ref, onet_ref, spread_ref, lo_ref, hi_ref, kt_ref, qt_ref, count_ref) = refs[:-9], refs[-9:]
    for row, bias in enumerate(biases):
        vec_ref[row : row + 1, :] = bias[...].reshape(1, -1)
    window, length = aux_ref.shape[0], spread_ref.shape[0]
    far = window - length
    seq = seq_ref[0]
    passages = lengths_ref.shape[1]
    ends, total = [], jnp.int32(0)
    for p in range(passages):
        total = total + lengths_ref[0, p]
        ends.append(total)
    window_start, own_start = seq * far, seq * length

    def segments(positions):
        found = jnp.zeros(positions.shape, jnp.int32)
        for end in ends:
            found = found + jnp.where(positions >= end, 1, 0)
        return found

    lane = lax.broadcasted_iota(jnp.int32, (TILE, TILE), 1)
    row = lax.broadcasted_iota(jnp.int32, (TILE, TILE), 0)

    def window_tile(i, carry):
        found = segments(window_start + i * TILE + row)
        apart = jnp.where((found != lane) & (lane <= passages), MASKED, 0.0)
        aux_ref[pl.ds(pl.multiple_of(i * TILE, TILE), TILE), :] = apart.astype(BF)
        own = i - seq * (far // TILE)

        @pl.when((own >= 0) & (own < length // TILE))
        def _():
            rows = pl.ds(pl.multiple_of(own * TILE, TILE), TILE)
            same = (found == lane % 32) & (lane < 96) & (found < passages)
            spread_ref[rows, :] = jnp.where(same, 1.0, 0.0).astype(BF)
            across = segments(own_start + own * TILE + lane[:8])
            one = jnp.where(jnp.broadcast_to(across[:1], (TILE, TILE)) == row, 1.0, 0.0)
            onet_ref[:, rows] = one.astype(BF)

        return carry

    lax.fori_loop(0, window // TILE, window_tile, 0)

    def reach(first, low, high):
        begin, end = jnp.int32(0), jnp.int32(2 * length)
        for stop in ends:
            begin = jnp.where(stop <= first, stop, begin)
        for stop in reversed(ends):
            end = jnp.where(stop > first + TILE - 1, stop, end)
        begin = jnp.clip(begin, low, high) - low
        end = jnp.clip(end, low, high) - low
        return begin // TILE, (end + TILE - 1) // TILE

    for i in range(length // TILE):
        lo_ref[i], hi_ref[i] = reach(own_start + i * TILE, window_start, window_start + window)
    count = jnp.int32(0)
    for t in range(window // TILE):
        low, high = reach(window_start + t * TILE, own_start, own_start + length)

        def put(i, count):
            kt_ref[count] = t
            qt_ref[count] = i
            return count + 1

        count = lax.fori_loop(low, high, put, count)
    count_ref[0] = count


def setup(lengths, seq, length, window, vectors):
    tiles, window_tiles = length // TILE, window // TILE
    smem = pl.BlockSpec(memory_space=pltpu.SMEM)
    vmem = pl.BlockSpec(memory_space=pltpu.VMEM)
    number = lambda n: jax.ShapeDtypeStruct((n,), jnp.int32)
    return pl.pallas_call(
        setup_kernel,
        in_specs=[smem, smem] + [vmem] * len(vectors),
        out_specs=[vmem] * 4 + [smem] * 5,
        out_shape=[
            jax.ShapeDtypeStruct((len(vectors), vectors[0].shape[0]), F32),
            jax.ShapeDtypeStruct((window, TILE), BF),
            jax.ShapeDtypeStruct((TILE, length), BF),
            jax.ShapeDtypeStruct((length, TILE), BF),
            number(tiles),
            number(tiles),
            number(tiles * window_tiles),
            number(tiles * window_tiles),
            number(1),
        ],
        compiler_params=pltpu.CompilerParams(vmem_limit_bytes=60 * VMEM_MIB),
        name="setup",
    )(lengths, seq.reshape(1).astype(jnp.int32), *vectors)


def project_kernel(
    place_ref, x_ref, far_ref, wq_ref, wk_ref, wv_ref, vec_ref, q_ref, qt_ref, k_ref, kt_ref, v_ref, vt_ref, xt_ref, x_scr
):
    own = pl.program_id(0) < place_ref[2]

    @pl.when(own)
    def _():
        x = x_ref[...]
        x_scr[...] = x
        q = (dot(x, wq_ref[...]) + vec_ref[BIAS_Q : BIAS_Q + 1, :]).astype(BF).astype(F32)
        q = (q * 0.125).astype(BF)
        q_ref[...] = q
        qt_ref[...] = q.T

    @pl.when(jnp.logical_not(own))
    def _():
        x_scr[...] = far_ref[...]

    x = x_scr[...]
    k = dot(x, wk_ref[...]).astype(BF)
    k_ref[...] = k
    kt_ref[...] = k.T
    v = (dot(x, wv_ref[...]) + vec_ref[BIAS_V : BIAS_V + 1, :]).astype(BF)
    v_ref[...] = v
    vt_ref[...] = v.T
    xt_ref[...] = x.T


def project(x, x_far, wq, wk, wv, vectors, seq):
    length, features = x.shape
    rows = 512
    near, far = length // rows, x_far.shape[0] // rows
    window = length + x_far.shape[0]
    place = jnp.stack([seq * far, (1 - seq) * near, jnp.int32(near)]).astype(jnp.int32)
    whole = lambda i, place: (0, 0)
    weight = pl.BlockSpec((features, features), whole, pipeline_mode=pl.Buffered(1))

    def window_block(i, place):
        return jnp.where(i < near, place[0] + i, place[1] + i - near)

    first = lambda i: jnp.minimum(i, near - 1)
    down = pl.BlockSpec((rows, features), lambda i, place: (window_block(i, place), 0))
    across = pl.BlockSpec((features, rows), lambda i, place: (0, window_block(i, place)))
    tall, flat = (jax.ShapeDtypeStruct(shape, BF) for shape in ((window, features), (features, window)))
    return pl.pallas_call(
        project_kernel,
        grid_spec=pltpu.PrefetchScalarGridSpec(
            num_scalar_prefetch=1,
            grid=(near + far,),
            in_specs=[
                pl.BlockSpec((rows, features), lambda i, place: (first(i), 0)),
                pl.BlockSpec((rows, features), lambda i, place: (jnp.maximum(i - near, 0), 0)),
                weight,
                weight,
                weight,
                pl.BlockSpec(vectors.shape, whole, pipeline_mode=pl.Buffered(1)),
            ],
            out_specs=[
                pl.BlockSpec((rows, features), lambda i, place: (first(i), 0)),
                pl.BlockSpec((features, rows), lambda i, place: (0, first(i))),
                down,
                across,
                down,
                across,
                across,
            ],
            scratch_shapes=[pltpu.VMEM((rows, features), BF)],
        ),
        out_shape=[
            jax.ShapeDtypeStruct((length, features), BF),
            jax.ShapeDtypeStruct((features, length), BF),
            tall,
            flat,
            tall,
            flat,
            flat,
        ],
        compiler_params=pltpu.CompilerParams(vmem_limit_bytes=60 * VMEM_MIB),
        name="project",
    )(place, x, x_far, wq, wk, wv, vectors)


def loss_kernel(partners_ref, lengths_ref, place_ref, given_ref, pooled_ref, loss_ref, parts_ref, every_ref):
    own, _ = pooled_ref.shape
    for n in range(given_ref.shape[0] // own):
        every_ref[n * own : (n + 1) * own, :] = given_ref[
            pl.ds(pl.multiple_of((place_ref[0] ^ n) * own, own), own), :
        ]
    every = every_ref[...]
    count, features = every.shape
    first = place_ref[0] * own
    scores = 100.0 * dot(every, every, ((1,), (1,)))
    row = lax.broadcasted_iota(jnp.int32, (count, count), 0)
    lane = lax.broadcasted_iota(jnp.int32, (count, count), 1)
    scores = jnp.where(row == lane, BIG_NEG, scores)
    top = jnp.max(scores, 0, keepdims=True)
    log_sums = top + jnp.log(jnp.sum(jnp.exp(scores - top), 0, keepdims=True))
    mine = every_ref[pl.ds(pl.multiple_of(first, own), own), :]
    near = 100.0 * dot(mine, every, ((1,), (1,)))
    own_row = lax.broadcasted_iota(jnp.int32, (own, count), 0)
    own_lane = lax.broadcasted_iota(jnp.int32, (own, count), 1)
    near = jnp.where(own_row + first == own_lane, BIG_NEG, near)
    top = jnp.max(near, 1, keepdims=True)
    own_sums = top + jnp.log(jnp.sum(jnp.exp(near - top), 1, keepdims=True))
    target = jnp.concatenate(
        [jnp.where(own_lane[:1] == partners_ref[first + i], 1.0, 0.0) for i in range(own)], 0
    )
    picked = jnp.sum(jnp.where(target > 0.0, near, 0.0), 1, keepdims=True)
    loss_ref[...] = jnp.broadcast_to(own_sums - picked, loss_ref.shape)
    lane_row = own_lane[:1]

    def aim(n, held):
        return jnp.where(lane_row == n, partners_ref[n], held)

    aims = lax.fori_loop(0, count, aim, jnp.full((1, count), -1, jnp.int32))
    targeted = jnp.where(aims == own_row + first, 1.0, 0.0)
    both = jnp.exp(near - own_sums) - target + (jnp.exp(near - log_sums) - targeted)
    high, middle, low = split3(both)
    grad = 100.0 * (dot(high, every) + dot(middle, every) + dot(low, every))
    pooled = pooled_ref[...]
    inverse = lax.rsqrt(jnp.sum(pooled * pooled, 1, keepdims=True) + 1e-06)
    grad = inverse * grad - pooled * (inverse * inverse * inverse * jnp.sum(pooled * grad, 1, keepdims=True))
    sizes = jnp.concatenate(
        [jnp.full((1, features), lengths_ref[0, i].astype(F32), F32) for i in range(own)], 0
    )
    high, middle, low = split3(grad / sizes)
    parts_ref[...] = jnp.zeros(parts_ref.shape, BF)
    parts_ref[0:own, :] = high
    parts_ref[32 : 32 + own, :] = middle
    parts_ref[64 : 64 + own, :] = low


def contrast(partners, lengths, place, every, pooled):
    own, features = pooled.shape
    smem = pl.BlockSpec(memory_space=pltpu.SMEM)
    vmem = pl.BlockSpec(memory_space=pltpu.VMEM)
    return pl.pallas_call(
        loss_kernel,
        in_specs=[smem, smem, smem, vmem, vmem],
        out_specs=[vmem, vmem],
        out_shape=[jax.ShapeDtypeStruct((own, TILE), F32), jax.ShapeDtypeStruct((TILE, features), BF)],
        scratch_shapes=[pltpu.VMEM(every.shape, BF)],
        compiler_params=pltpu.CompilerParams(vmem_limit_bytes=60 * VMEM_MIB),
        name="contrast",
    )(partners, lengths, place.reshape(1).astype(jnp.int32), every, pooled)


def gelu_parts(u):
    size = jnp.abs(u)
    base = 1.0 + (0.3275911 * math.sqrt(0.5)) * size
    t = pl.reciprocal(base, approx=True)
    t = t * (2.0 - base * t)
    bell = jnp.exp2((-0.5 * math.log2(math.e)) * (u * u))
    poly = t * (0.127414796 + t * (-0.142248368 + t * (0.7107068705 + t * (-0.7265760135 + t * 0.5307027145))))
    tail = poly * bell
    below = jnp.where(u < 0.0, tail, 1.0 - tail)
    return u * below, below + u * bell * (1.0 / math.sqrt(2.0 * math.pi))


def normalized(resid):
    center = resid - jnp.mean(resid, -1, keepdims=True)
    scale = lax.rsqrt(jnp.mean(center * center, -1, keepdims=True) + EPS_NORM)
    return center * scale, scale


def feed_kernel(
    cb_ref, x_ref, member_ref, wo_ref, vec_ref, be_ref, w1_ref, w2_ref,
    n1_ref, r1_ref, h_ref, n2_ref, r2_ref, pool_ref, f_ref, gp_ref, low_scr, resid_scr,
):
    vector = lambda which: vec_ref[which : which + 1, :]
    length = cb_ref.shape[0]
    rows = 256

    @pl.when(pl.program_id(0) == 0)
    def _():
        for start in range(0, length, 2 * rows):
            at = slice(start, start + 2 * rows)
            attended = dot(cb_ref[at, :], wo_ref[...]) + vector(BIAS_O)
            unit, scale = normalized(x_ref[at, :].astype(F32) + attended)
            n1_ref[at, :] = unit.astype(BF)
            r1_ref[at, :] = scale
            hidden = unit * vector(GAIN_1) + vector(SHIFT_1)
            low = hidden.astype(BF)
            low_scr[at, :] = low
            h_ref[:, at] = low.T
            resid_scr[at, :] = hidden + vector(BIAS_S)

    for start in range(0, length, rows):
        at = slice(start, start + rows)
        active, slope = gelu_parts(dot(low_scr[at, :], w1_ref[...]) + be_ref[...])
        active = active.astype(BF)
        f_ref[:, at] = active.T
        gp_ref[at, :] = slope.astype(BF)
        resid_scr[at, :] += dot(active, w2_ref[...])

    @pl.when(pl.program_id(0) == pl.num_programs(0) - 1)
    def _():
        part = jnp.zeros(pool_ref.shape, F32)
        for start in range(0, length, 2 * rows):
            at = slice(start, start + 2 * rows)
            unit, scale = normalized(resid_scr[at, :])
            n2_ref[at, :] = unit.astype(BF)
            r2_ref[at, :] = scale
            high, middle, _ = split3(unit * vector(GAIN_2) + vector(SHIFT_2))
            members = member_ref[:, at]
            part = part + dot(members, high) + dot(members, middle)
        pool_ref[...] = part


def feed(cb, x, one_t, pass_count, wo, w1, w2, vectors, expand_bias):
    length, features = x.shape
    hidden = w1.shape[1]
    chunk = 768
    row = lambda i: (i, 0)
    col = lambda i: (0, i)
    whole = lambda i: (0, 0)

    def full(array, shape=None):
        return pl.BlockSpec(shape or array.shape, whole, pipeline_mode=pl.Buffered(1))

    return pl.pallas_call(
        feed_kernel,
        grid=(hidden // chunk,),
        in_specs=[full(cb), full(x), full(one_t, (pass_count, length)), full(wo), full(vectors)]
        + [
            pl.BlockSpec((1, chunk), col),
            pl.BlockSpec((features, chunk), col),
            pl.BlockSpec((chunk, features), row),
        ],
        out_specs=[
            pl.BlockSpec((length, features), whole),
            pl.BlockSpec((length, 1), whole),
            pl.BlockSpec((features, length), whole),
            pl.BlockSpec((length, features), whole),
            pl.BlockSpec((length, 1), whole),
            pl.BlockSpec((pass_count, features), whole),
            pl.BlockSpec((chunk, length), row),
            pl.BlockSpec((length, chunk), col),
        ],
        out_shape=[
            jax.ShapeDtypeStruct((length, features), BF),
            jax.ShapeDtypeStruct((length, 1), F32),
            jax.ShapeDtypeStruct((features, length), BF),
            jax.ShapeDtypeStruct((length, features), BF),
            jax.ShapeDtypeStruct((length, 1), F32),
            jax.ShapeDtypeStruct((pass_count, features), F32),
            jax.ShapeDtypeStruct((hidden, length), BF),
            jax.ShapeDtypeStruct((length, hidden), BF),
        ],
        scratch_shapes=[pltpu.VMEM((length, features), BF), pltpu.VMEM((length, features), F32)],
        compiler_params=pltpu.CompilerParams(vmem_limit_bytes=60 * VMEM_MIB),
        name="feed",
    )(cb, x, one_t, wo, vectors, expand_bias.reshape(1, -1), w1, w2)


def norm_back(grad, unit, scale, gain):
    wide = grad * gain
    return scale * (
        wide - jnp.mean(wide, -1, keepdims=True) - unit * jnp.mean(wide * unit, -1, keepdims=True)
    )


def add_rows(ref, row, value):
    ref[row : row + 1, :] += jnp.sum(value, 0, keepdims=True)


def feed_grads_kernel(
    spread_ref, pooled_ref, n2_ref, r2_ref, vec_ref, ht_ref, w2_ref, gp_ref, ft_ref,
    dy_ref, sums_ref, shrink_ref, expand_ref, du_ref, wide_sums_ref,
):
    rows = 512
    tiles = dy_ref.shape[0] // rows

    @pl.when(pl.program_id(0) == 0)
    def _():
        sums_ref[...] = jnp.zeros(sums_ref.shape, F32)
        for i in range(tiles):
            at = slice(i * rows, (i + 1) * rows)
            grad = dot(spread_ref[at, :], pooled_ref[...])
            unit = n2_ref[at, :].astype(F32)
            add_rows(sums_ref, 0, grad * unit)
            add_rows(sums_ref, 1, grad)
            dy = norm_back(grad, unit, r2_ref[at, :], vec_ref[GAIN_2 : GAIN_2 + 1, :]).astype(BF)
            dy_ref[at, :] = dy
            add_rows(sums_ref, 2, dy.astype(F32))

    total = jnp.zeros((1, du_ref.shape[1]), F32)
    for i in range(0, tiles, 2):
        at = slice(i * rows, (i + 2) * rows)
        du = (gp_ref[at, :].astype(F32) * dot(dy_ref[at, :], w2_ref[...], ((1,), (1,)))).astype(BF)
        du_ref[at, :] = du
        total = total + jnp.sum(du.astype(F32), 0, keepdims=True)
    wide_sums_ref[...] = jnp.broadcast_to(total, wide_sums_ref.shape)
    expand_ref[...] = dot(ht_ref[...], du_ref[...]).astype(BF)
    shrink_ref[...] = dot(ft_ref[...], dy_ref[...]).astype(BF)


def feed_grads(spread, pooled_parts, n2, r2, vectors, ht, w2, gp, ft):
    length, features = n2.shape
    hidden = gp.shape[1]
    chunk = 512
    row = lambda i: (i, 0)
    col = lambda i: (0, i)
    whole = lambda i: (0, 0)

    def full(array):
        return pl.BlockSpec(array.shape, whole, pipeline_mode=pl.Buffered(1))

    return pl.pallas_call(
        feed_grads_kernel,
        grid=(hidden // chunk,),
        in_specs=[full(a) for a in (spread, pooled_parts, n2, r2, vectors, ht)]
        + [
            pl.BlockSpec((chunk, features), row),
            pl.BlockSpec((length, chunk), col),
            pl.BlockSpec((chunk, length), row),
        ],
        out_specs=[
            pl.BlockSpec((length, features), whole),
            pl.BlockSpec((8, features), whole),
            pl.BlockSpec((chunk, features), row),
            pl.BlockSpec((features, chunk), col),
            pl.BlockSpec((length, chunk), col),
            pl.BlockSpec((8, chunk), col),
        ],
        out_shape=[
            jax.ShapeDtypeStruct((length, features), BF),
            jax.ShapeDtypeStruct((8, features), F32),
            jax.ShapeDtypeStruct((hidden, features), BF),
            jax.ShapeDtypeStruct((features, hidden), BF),
            jax.ShapeDtypeStruct((length, hidden), BF),
            jax.ShapeDtypeStruct((8, hidden), F32),
        ],
        compiler_params=pltpu.CompilerParams(vmem_limit_bytes=60 * VMEM_MIB),
        name="feed_grads",
    )(spread, pooled_parts, n2, r2, vectors, ht, w2, gp, ft)


def hidden_back_kernel(
    dy_ref, du_ref, n1_ref, r1_ref, w1_ref, wo_ref, g1_ref, ct_ref, da_ref, dc_ref, dct_ref, delta_ref, sums_ref
):
    @pl.when(pl.program_id(0) == 0)
    def _():
        sums_ref[...] = jnp.zeros(sums_ref.shape, F32)

    dh = dy_ref[...].astype(F32) + dot(du_ref[...], w1_ref[...], ((1,), (1,)))
    unit = n1_ref[...].astype(F32)
    add_rows(sums_ref, 0, dh * unit)
    add_rows(sums_ref, 1, dh)
    dr = norm_back(dh, unit, r1_ref[...], g1_ref[GAIN_1 : GAIN_1 + 1, :])
    da = dr.astype(BF)
    da_ref[...] = da
    add_rows(sums_ref, 2, da.astype(F32))
    dc_ref[...] = dot(da, wo_ref[...], ((1,), (1,))).astype(BF)
    dct = dot(wo_ref[...], da, ((1,), (1,))).astype(BF)
    dct_ref[...] = dct
    product = dct.astype(F32) * ct_ref[...]
    size = product.shape[0] // HEADS
    delta_ref[...] = jnp.concatenate(
        [jnp.sum(product[head * size : (head + 1) * size], 0, keepdims=True) for head in range(HEADS)], 0
    )


def hidden_back(dy, du, n1, r1, w1, wo, g1, ct):
    length, features = dy.shape
    hidden = du.shape[1]
    rows = 256
    row = lambda i: (i, 0)
    whole = lambda i: (0, 0)
    once = pl.Buffered(1)

    def full(array):
        return pl.BlockSpec(array.shape, whole, pipeline_mode=once)

    return pl.pallas_call(
        hidden_back_kernel,
        grid=(length // rows,),
        in_specs=[
            pl.BlockSpec((rows, features), row),
            pl.BlockSpec((rows, hidden), row),
            pl.BlockSpec((rows, features), row),
            pl.BlockSpec((rows, 1), row),
            full(w1),
            full(wo),
            full(g1),
            pl.BlockSpec((features, rows), lambda i: (0, i)),
        ],
        out_specs=[
            pl.BlockSpec((rows, features), row),
            pl.BlockSpec((rows, features), row),
            pl.BlockSpec((features, rows), lambda i: (0, i)),
            pl.BlockSpec((HEADS, rows), lambda i: (0, i)),
            pl.BlockSpec((8, features), whole),
        ],
        out_shape=[
            jax.ShapeDtypeStruct((length, features), BF),
            jax.ShapeDtypeStruct((length, features), BF),
            jax.ShapeDtypeStruct((features, length), BF),
            jax.ShapeDtypeStruct((HEADS, length), F32),
            jax.ShapeDtypeStruct((8, features), F32),
        ],
        compiler_params=pltpu.CompilerParams(vmem_limit_bytes=60 * VMEM_MIB),
        name="hidden_back",
    )(dy, du, n1, r1, w1, wo, g1, ct)


def swap_seq(array):
    return lax.ppermute(array, "seq", [(0, 1), (1, 0)])


def swap_dp(array, bit):
    count = lax.axis_size("dp")
    return lax.ppermute(array, "dp", [(i, i ^ (1 << bit)) for i in range(count)])


def swap_crossed(array, bits):
    count = lax.axis_size("dp")
    pairs = [(2 * i + s, 2 * (i ^ (1 << bits[s])) + s) for i in range(count) for s in range(2)]
    return lax.ppermute(array, ("dp", "seq"), pairs)


def pick_half(array, axis, which):
    half = array.shape[axis] // 2
    return lax.dynamic_slice_in_dim(array, which * half, half, axis)


def join(mine, other, axis, place):
    return jnp.where(
        place == 0, jnp.concatenate([mine, other], axis), jnp.concatenate([other, mine], axis)
    )


def halving_axis(shape):
    rows, cols = shape
    if rows % 32 == 0:
        return 0
    if cols % 256 == 0:
        return 1
    return 0


def pack_kernel(sums2_ref, sums1_ref, wide_ref, *refs):
    biases, out_ref = refs[:-1], refs[-1]
    features = out_ref.shape[1]
    out_ref[...] = jnp.zeros(out_ref.shape, F32)
    out_ref[0:3, :] = sums2_ref[0:3, :]
    out_ref[3:6, :] = sums1_ref[0:3, :]
    for part, bias in enumerate(biases):
        own = bias.shape[1] // 3
        cols = slice(part * own, (part + 1) * own)
        out_ref[6:7, cols] = bias[0:1, :own]
        out_ref[7:8, cols] = bias[0:1, 2 * own :]
    for row in range(wide_ref.shape[1] // features):
        out_ref[8 + row : 9 + row, :] = wide_ref[0:1, row * features : (row + 1) * features]


def pack_sums(sums2, sums1, wide_sums, bias_sums):
    rows = -(-(8 + wide_sums.shape[1] // sums2.shape[1]) // 8) * 8
    return pl.pallas_call(
        pack_kernel,
        out_shape=jax.ShapeDtypeStruct((rows, sums2.shape[1]), F32),
        compiler_params=pltpu.CompilerParams(vmem_limit_bytes=60 * VMEM_MIB),
        name="pack_sums",
    )(sums2, sums1, wide_sums, *bias_sums)


def tokens_kernel(parts, place_ref, *refs):
    grads, fars, weights = refs[:parts], refs[parts : 2 * parts], refs[2 * parts : 2 * parts + 3]
    first_ref, out_ref = refs[2 * parts + 3 :]

    def back(source, part, which, at):
        own = grads[part].shape[1] // 3
        weight = weights[which][:, part * own : (part + 1) * own]
        return dot(source[:, at * own : (at + 1) * own], weight, ((1,), (1,)))

    total = first_ref[...].astype(F32)
    for part in range(parts):
        for which in range(3):
            total = total + back(grads[part], part, which, which)
    out_ref[...] = total
    tile = pl.program_id(0) - (1 - place_ref[0]) * 2

    @pl.when((tile >= 0) & (tile < 2))
    def _():
        total = out_ref[...]
        for part in range(parts):
            for which in (1, 2):
                total = total + back(fars[part], part, which, which - 1)
        out_ref[...] = total


def tokens_back(seq, grads, fars, weights, first):
    length, features = first.shape
    rows = fars[0].shape[0] // 2
    row = lambda i, place: (i, 0)
    whole = lambda i, place: (0, 0)
    return pl.pallas_call(
        functools.partial(tokens_kernel, len(grads)),
        grid_spec=pltpu.PrefetchScalarGridSpec(
            num_scalar_prefetch=1,
            grid=(length // rows,),
            in_specs=[pl.BlockSpec((rows, grad.shape[1]), lambda i, place: (place[0] * 2 + i, 0)) for grad in grads]
            + [
                pl.BlockSpec((rows, far.shape[1]), lambda i, place: (jnp.clip(i - (1 - place[0]) * 2, 0, 1), 0))
                for far in fars
            ]
            + [pl.BlockSpec(weight.shape, whole, pipeline_mode=pl.Buffered(1)) for weight in weights]
            + [pl.BlockSpec((rows, features), row)],
            out_specs=pl.BlockSpec((rows, features), row),
        ),
        out_shape=jax.ShapeDtypeStruct((length, features), F32),
        compiler_params=pltpu.CompilerParams(vmem_limit_bytes=60 * VMEM_MIB),
        name="tokens_back",
    )(seq.reshape(1).astype(jnp.int32), *grads, *fars, *weights, first)


WIDE = 768


def products_kernel(kinds, place_ref, *refs):
    half = len(kinds) // 2
    out_ref = refs[-1]
    block = place_ref[0] * half + pl.program_id(0)
    for left, right in sorted(set(kinds)):
        mine = functools.reduce(
            jnp.logical_or, [block == n for n in range(len(kinds)) if kinds[n] == (left, right)]
        )

        @pl.when(mine)
        def _(left=left, right=right):
            out_ref[...] = dot(refs[left][...], refs[right][...]).astype(BF)


def products(blocks, which):
    count, half = len(blocks), len(blocks) // 2
    operands, specs, kinds = [], [], []

    def place_operand(side, array, split):
        for n, held in enumerate(operands):
            if held is array:
                return n
        cuts = [pair[side][1] if pair[side][0] is array else 0 for pair in blocks]
        if split:
            shape = (WIDE, array.shape[1]) if side == 0 else (array.shape[0], WIDE)

            def index(step, place):
                block = place[0] * half + step
                cut = functools.reduce(lambda held, n: jnp.where(block == n, cuts[n], held), range(count), 0)
                return (cut, 0) if side == 0 else (0, cut)

            specs.append(pl.BlockSpec(shape, index))
        else:
            specs.append(pl.BlockSpec(array.shape, lambda step, place: (0, 0), pipeline_mode=pl.Buffered(1)))
        operands.append(array)
        return len(operands) - 1

    for (left, row), (right, col) in blocks:
        kinds.append((place_operand(0, left, row is not None), place_operand(1, right, col is not None)))
    height = blocks[0][0][0].shape[0]
    return pl.pallas_call(
        functools.partial(products_kernel, kinds),
        grid_spec=pltpu.PrefetchScalarGridSpec(
            num_scalar_prefetch=1,
            grid=(half,),
            in_specs=specs,
            out_specs=pl.BlockSpec((height, WIDE), lambda g, place: (g, 0)),
        ),
        out_shape=jax.ShapeDtypeStruct((half * height, WIDE), BF),
        compiler_params=pltpu.CompilerParams(vmem_limit_bytes=60 * VMEM_MIB),
        name="products",
    )(which.reshape(1).astype(jnp.int32), *operands)


def fold_kernel(place_ref, keep_ref, other_ref, *out_refs):
    total = (keep_ref[...].astype(F32) + other_ref[...].astype(F32)).astype(BF)
    for m, out_ref in enumerate(out_refs):

        @pl.when(pl.program_id(0) == m)
        def _(out_ref=out_ref):
            out_ref[...] = total


def fold(keep, other, place, parts, first, count):
    rows, cols = keep.shape[0] // parts, keep.shape[1]
    picked = pl.BlockSpec((rows, cols), lambda m, place: (place[0] ^ (m + first), 0))
    return pl.pallas_call(
        fold_kernel,
        grid_spec=pltpu.PrefetchScalarGridSpec(
            num_scalar_prefetch=1,
            grid=(count,),
            in_specs=[picked, picked],
            out_specs=[pl.BlockSpec((rows, cols), lambda m, place: (0, 0))] * count,
        ),
        out_shape=[jax.ShapeDtypeStruct((rows, cols), BF)] * count,
        compiler_params=pltpu.CompilerParams(vmem_limit_bytes=60 * VMEM_MIB),
        name="fold",
    )(place.reshape(1).astype(jnp.int32), keep, other)


def assemble_kernel(targets, place_ref, own_ref, other_ref, *out_refs):
    shards, rows = own_ref.shape[0], own_ref.shape[1]
    step = pl.program_id(0)
    mine = step // (len(targets) // 2) == place_ref[0]
    for ref, offset, here in ((own_ref, place_ref[1], mine), (other_ref, place_ref[2], jnp.logical_not(mine))):
        for outs in sorted(set(targets)):
            ours = functools.reduce(jnp.logical_or, [step == n for n in range(len(targets)) if targets[n] == outs])

            @pl.when(here & ours)
            def _(ref=ref, offset=offset, outs=outs):
                for shard in range(shards):
                    value = ref[shard ^ (offset & (shards - 1))].astype(F32)
                    at = 0
                    for out in outs:
                        width = out_refs[out].shape[1]
                        out_refs[out][shard * rows : (shard + 1) * rows, :] = value[:, at : at + width]
                        at += width


def assemble(own, other, places, shapes, targets):
    shards, rows, _ = own.shape
    count = len(targets)
    half = count // 2
    group = shards // half

    def shard_block(which):
        def index(step, place):
            here = (step // half == place[0]) == (which == 1)
            return (jnp.where(here, (step % half) ^ (place[which] // group), 0), 0, 0)

        return pl.BlockSpec((group, rows, WIDE), index)

    out_specs = []
    for out, shape in enumerate(shapes):
        steps = [n for n in range(count) if out in targets[n]]

        def index(step, place, steps=steps):
            return (0, sum((jnp.where(step >= n, 1, 0) for n in steps[1:]), jnp.int32(0)))

        out_specs.append(pl.BlockSpec((shape[0], shape[1] // len(steps)), index))
    return pl.pallas_call(
        functools.partial(assemble_kernel, targets),
        grid_spec=pltpu.PrefetchScalarGridSpec(
            num_scalar_prefetch=1,
            grid=(count,),
            in_specs=[shard_block(1), shard_block(2)],
            out_specs=out_specs,
        ),
        out_shape=[jax.ShapeDtypeStruct(shape, F32) for shape in shapes],
        compiler_params=pltpu.CompilerParams(vmem_limit_bytes=60 * VMEM_MIB),
        name="assemble",
    )(jnp.stack(places).astype(jnp.int32), own, other)


class GradTotal:
    steps = 8

    def __init__(self, blocks):
        self.place(0)
        self.out = [products(blocks, 1 - self.seq)]
        self.keep = products(blocks, self.seq)

    def place(self, step):
        seq, dp = lax.axis_index("seq"), lax.axis_index("dp")
        self.step, self.seq, self.far = step, seq, (dp >> 2) & 3
        self.near = ((dp >> seq) & 1, (dp >> (1 - seq)) & 1)

    @classmethod
    def resumed(cls, step, out):
        total = cls.__new__(cls)
        total.place(step)
        total.out, total.got = [out], None
        return total

    def offset(self, seq):
        dp = lax.axis_index("dp")
        return ((dp >> seq) & 1) * 8 + ((dp >> (1 - seq)) & 1) * 4 + ((dp >> 2) & 3)

    def cut(self, place, parts):
        self.out = fold(self.keep, self.got[0], place, parts, 1, parts - 1)
        (self.keep,) = fold(self.keep, self.got[0], place, parts, 0, 1)

    def prepare(self):
        step = self.step
        if step in (1, 2):
            self.cut(self.near[step - 1], 2)
        elif step == 3:
            self.cut(self.far, 4)
        elif step == 4:
            total = self.keep.astype(F32)
            for other in self.got:
                total = total + other.astype(F32)
            self.out = [total.astype(BF)]
        elif step == 5:
            self.out = [jnp.stack(self.out + self.got)]
        elif step > 5 and self.got:
            self.out, self.got = [jnp.concatenate(self.out + self.got)], None

    def exchange(self):
        step, count = self.step, lax.axis_size("dp")
        if step in (0, 7):
            self.got = [swap_seq(self.out[0])]
        elif step in (1, 6):
            self.got = [swap_crossed(self.out[0], (0, 1))]
        elif step in (2, 5):
            self.got = [swap_crossed(self.out[0], (1, 0))]
        else:
            sends = self.out if step == 3 else self.out * 3
            self.got = [
                lax.ppermute(send, "dp", [(i, i ^ (m << 2)) for i in range(count)])
                for m, send in zip((1, 2, 3), sends)
            ]
        self.step += 1

    def done(self):
        return self.step == self.steps

    def whole(self, shapes, targets):
        places = [self.seq, self.offset(self.seq), self.offset(1 - self.seq)]
        return assemble(self.out[0], self.got[0], places, shapes, targets)


def plain_total(partial):
    seq, index = lax.axis_index("seq"), lax.axis_index("dp")
    block = (pick_half(partial, 0, seq).astype(F32) + swap_seq(pick_half(partial, 0, 1 - seq)).astype(F32)).astype(BF)
    steps = []
    for bit in range(int(math.log2(lax.axis_size("dp")))):
        place, axis = (index >> bit) & 1, halving_axis(block.shape)
        steps.append((bit, place, axis))
        other = swap_dp(pick_half(block, axis, 1 - place), bit)
        block = (pick_half(block, axis, place).astype(F32) + other.astype(F32)).astype(BF)
    for bit, place, axis in reversed(steps):
        block = join(block, swap_dp(block, bit), axis, place)
    return join(block, swap_seq(block), 0, seq).astype(F32)


class Swap:
    def __init__(self, array):
        self.out, self.step = [array], 0

    def prepare(self):
        pass

    def exchange(self):
        self.got = [swap_seq(self.out[0])]
        self.step = 1

    def done(self):
        return self.step == 1


class Small:
    def __init__(self, partial):
        self.block, self.step = partial, 0
        self.steps = 1 + int(math.log2(lax.axis_size("dp")))

    def prepare(self):
        if self.step:
            self.block = self.block + self.got[0]
        self.out = [self.block]

    def exchange(self):
        block = self.out[0]
        self.block = block
        self.got = [swap_seq(block) if self.step == 0 else swap_dp(block, self.step - 1)]
        self.step += 1

    def done(self):
        return self.step == self.steps

    def whole(self):
        return self.block + self.got[0]


def fence(*values):
    return lax.optimization_barrier(values)


def beside(sums, work, *inputs):
    live = [total for total in sums if not total.done()]
    for total in live:
        total.prepare()
    inputs, sends = fence(inputs, [total.out for total in live])
    for total, send in zip(live, sends):
        total.out = send
        total.exchange()
    result, received = fence(work(*inputs), [total.got for total in live])
    for total, got in zip(live, received):
        total.got = got
    return result


def body(
    tokens, lengths, partners, query_proj, query_bias, key_proj, value_proj, value_bias, output_proj, output_bias,
    first_gain, first_shift, expand_proj, expand_bias, shrink_proj, shrink_bias, second_gain, second_shift,
):
    _, length, features = tokens.shape
    pass_count = lengths.shape[1]
    seq = lax.axis_index("seq")
    dp = lax.axis_index("dp")
    far = length // 2
    window = length + far
    x = tokens[0]

    x_far = swap_seq(lax.dynamic_slice_in_dim(x, (1 - seq) * far, far, 0))
    vectors, aux, one_t, spread, key_lo, key_hi, *pair_list = setup(
        lengths,
        seq,
        length,
        window,
        (output_bias, first_gain, first_shift, shrink_bias, second_gain, second_shift, query_bias, value_bias),
    )
    queries, queries_t, keys, keys_t, values, values_t, x_t = project(
        x, x_far, query_proj, key_proj, value_proj, vectors, seq
    )
    context_low, context_t, context_low_t, lse = attend(queries_t, one_t, keys, values_t, aux, key_lo, key_hi)
    unit1, scale1, hidden_t, unit2, scale2, pooled_part, active_t, slope = feed(
        context_low, x, one_t, pass_count, output_proj, expand_proj, shrink_proj, vectors, expand_bias
    )

    lengths_wide = lengths.reshape(pass_count, 1).astype(F32)
    pooled = (pooled_part + swap_seq(pooled_part)) / lengths_wide
    inverse = lax.rsqrt(jnp.sum(pooled * pooled, -1, keepdims=True) + 1e-06)
    every = (pooled * inverse).astype(BF)
    bits = int(math.log2(lax.axis_size("dp")))
    for low in range(0, bits, 2):
        others = [
            lax.ppermute(every, "dp", [(i, i ^ (m << low)) for i in range(1 << bits)])
            for m in range(1, 1 << min(2, bits - low))
        ]
        every = jnp.concatenate([every, *others])
    passage_loss, pooled_parts = contrast(partners, lengths, dp, every, pooled)
    passage_loss = passage_loss[:, 0]

    fast = lax.axis_size("dp") == 16
    grad_shrunk, sums2, grad_shrink, grad_expand, grad_expanded, wide_sums = feed_grads(
        spread, pooled_parts, unit2, scale2, vectors, hidden_t, shrink_proj, slope, active_t
    )
    grad_shrunk, grad_expanded, grad_shrink, grad_expand = fence(
        grad_shrunk, grad_expanded, grad_shrink, grad_expand
    )
    shrink_total, expand_total = lax.psum((grad_shrink, grad_expand), ("dp", "seq"))
    grad_attended, grad_context, grad_context_t, delta, sums1 = hidden_back(
        grad_shrunk, grad_expanded, unit1, scale1, expand_proj, output_proj, vectors, context_t
    )
    parts, swaps, grads, bias_sums = 1, [], [], []
    for part in range(parts):

        def attention_work(grad_context):
            return attend_back(
                part, parts, seq, pair_list, queries, queries_t, grad_context, grad_context_t, one_t, lse, delta, keys,
                keys_t, values, aux,
            )

        grad, far_part, bias_sum = beside(swaps[-1:], attention_work, grad_context)
        grads.append(grad)
        bias_sums.append(bias_sum)
        swaps.append(Swap(far_part))
    square = query_proj.shape
    own = features // parts

    def near_rounds(context_low_t, grad_attended, x_t, far_part, *grads):
        sums, rest = [], ()
        if fast:
            late_sum = GradTotal(
                [((context_low_t, None), (grad_attended, None))]
                + [((x_t, None), (grads[0], n)) for n in range(3)]
            )
            sums.append(late_sum)
        last = Swap(far_part)
        small_sum = Small(beside(sums + [last], lambda *bias: pack_sums(sums2, sums1, wide_sums, bias), *bias_sums))
        sums.append(small_sum)
        tokens_grad = beside(
            sums,
            lambda far_part, *grads: tokens_back(
                seq, grads, (far_part,), (query_proj, key_proj, value_proj), grad_attended
            ),
            last.got[0],
            *grads,
        )
        while not small_sum.done() or fast and late_sum.step < 7:
            beside(sums, lambda _: (), far_part)
        if fast:
            late_sum.prepare()
            rest = late_sum.out[0]
        else:
            cut = lambda which: jnp.concatenate([grad[:, which * own : (which + 1) * own] for grad in grads], 1)
            rest = [
                plain_total(dot(left, right).astype(BF))
                for left, right in ((context_low_t, grad_attended), *((x_t, cut(n)) for n in range(3)))
            ]
        return small_sum.whole(), tokens_grad, rest

    def nothing(context_low_t, grad_attended, x_t, far_part, *grads):
        small = jnp.zeros((-(-(8 + expand_bias.shape[0] // features) // 8) * 8, features), F32)
        if fast:
            shards = jnp.zeros((16, 2 * features // 16, features), BF)
            return small, jnp.zeros((length, features), F32), shards
        return small, jnp.zeros((length, features), F32), [jnp.zeros(square, F32)] * 4

    small, tokens_grad, rest = lax.cond(
        lengths[0, 0] > 0, near_rounds, nothing, context_low_t, grad_attended, x_t, swaps[0].out[0],
        *grads,
    )
    tokens_grad = tokens_grad[None]
    if fast:
        late_sum = GradTotal.resumed(7, rest)
        shrink_total, expand_total = beside(
            [late_sum], lambda *totals: [total.astype(F32) for total in totals], shrink_total, expand_total
        )
        output_total, query_total, key_total, value_total = late_sum.whole(
            [square] * 4, [(0,), (1,), (2,), (3,)]
        )
    else:
        shrink_total, expand_total = shrink_total.astype(F32), expand_total.astype(F32)
        output_total, query_total, key_total, value_total = rest
    return (
        passage_loss,
        tokens_grad,
        query_total,
        small[6],
        key_total,
        value_total,
        small[7],
        output_total,
        small[5],
        small[3],
        small[4],
        expand_total,
        small[8 : 8 + expand_bias.shape[0] // features].reshape(-1),
        shrink_total,
        small[2],
        small[0],
        small[1],
    )


def solution(mesh):
    placed = (P("dp", "seq", None), P("dp", None)) + (P(),) * 16
    return jax.shard_map(
        body,
        mesh=mesh,
        in_specs=placed,
        out_specs=(P("dp"), P("dp", "seq", None)) + (P(),) * 15,
        check_vma=False,
    )
```
